128 devices in a mesh: ty: 8 (over z, core), tx: 16 (over y, x).
Axes of the slice: x: 4, y: 4, z: 4, core: 2. Of those that a mesh axis runs over, the one named last changes fastest.
Arguments:
- atmos: float32 [3, 16, 512, 2048], P(None, None, 'ty', 'tx'), may hold values from -3 to 3
- slot_tile: int32 [3072], replicated, may hold values from -1 to 8191, as said below
- fuel_cat: int32 [3072, 3200], P(('ty', 'tx')), may hold values from 0 to 12
- front_burn: int32 [3072, 3200], P(('ty', 'tx')), may hold values 0 or 1
- front_depth: float32 [3072, 3200], P(('ty', 'tx')), may hold values from 0.2 to 2
- fuel_rate: float32 [13], replicated, may hold values from 0.1 to 0.6
- fuel_heat: float32 [13], replicated, may hold values from 0.5 to 5
Outputs:
- atmos_out: float32 [3, 16, 512, 2048], P(None, None, 'ty', 'tx')
- fire_level: float32 [3072, 3200], P(('ty', 'tx'))
The draws below stay inside these ranges and needn't reach their ends.
Inputs may be any that keep to these rules, and one draw needn't show every extreme that they name: `slot_tile`: entries are -1 for an empty slot or distinct fire tile numbers; each device's live slots come first; the cells of exactly 8 live tiles lie on every device; the live tiles whose cells lie on one device fill at most 2 slots of any one device, and some pair of devices reaches it; some device has all 24 slots live; the last tile of the window is always listed.
All inputs are finite; a program needn't handle non-finite values. No bound on the sum of `front_burn` on one device may be relied on, other than what follows from the above.
Results may differ from the reference program's by a relative error of at most 0.0001.
Values sent between devices are 32-bit elements; how exact they have to be, the bound alone decides.
No kernel may reach another device: no remote copies, remote signals or barrier semaphores. Data moves between devices by JAX's collectives and lax.ppermute only.
A program may use at most 128 MiB of HBM per device.

```python
import math
import jax
import jax.numpy as jnp
import numpy as np

LEV = 16
AY = 64
AX = 128
FTY = 8
FTX = 16
REF = 5
FC = 3200
NFUEL = 13
SLOTS = 24
STEPS = 2
NYA = 512
NXA = 2048
N_TX = 16
DEVICES = 128


LOAD_PATTERNS = np.array([[24, 4, 2, 2], [12, 10, 6, 4], [8, 8, 8, 8], [14, 10, 4, 4], [18, 8, 4, 2], [10, 10, 10, 2]], dtype=np.int32)


def draw_slot_tile(key, part):
    key = jax.random.fold_in(key, 11)
    key_blocks, key_workers, key_owners, key_tiles = jax.random.split(key, 4)
    groups = DEVICES // 4
    pattern_pick = jax.random.randint(key_blocks, (groups,), 0, LOAD_PATTERNS.shape[0]).at[0].set(0)
    load_list = jnp.asarray(LOAD_PATTERNS)[pattern_pick].reshape(-1)
    worker_perm = jax.random.permutation(key_workers, DEVICES)
    worker_load = jnp.zeros((DEVICES,), jnp.int32).at[worker_perm].set(load_list)
    load_start = jnp.cumsum(worker_load) - worker_load
    slot_order = jnp.arange(SLOTS, dtype=jnp.int32)
    global_rank = load_start[:, None] + slot_order[None, :]
    is_filled = slot_order[None, :] < worker_load[:, None]
    owner_perm = jax.random.permutation(key_owners, DEVICES).astype(jnp.int32)
    holder = owner_perm[global_rank // 2 % DEVICES]
    within = 2 * (global_rank // (2 * DEVICES)) + global_rank % 2
    per_device = AY // FTY * (AX // FTX)
    scores = jax.random.randint(key_tiles, (DEVICES, per_device), 0, 1 << 20) * per_device + jnp.arange(per_device, dtype=jnp.int32)[None, :]
    scores = scores.at[DEVICES - 1, per_device - 1].set(-1)
    shuffled = jnp.argsort(scores, axis=1).astype(jnp.int32)
    chosen = shuffled[holder, jnp.minimum(within, per_device - 1)]
    across = AX // FTX
    tile_row = holder // N_TX * (AY // FTY) + chosen // across
    tile_col = holder % N_TX * across + chosen % across
    tile_number = tile_row * (N_TX * across) + tile_col
    return jnp.where(is_filled, tile_number, -1).reshape(-1).astype(jnp.int32)


def touch_ends(values, key, low, top_value):
    longest = values.shape.index(max(values.shape))
    spots = []
    for shift in (0, 1):
        where = [jax.random.randint(jax.random.fold_in(key, axis), (), 0, length) for axis, length in enumerate(values.shape)]
        where[longest] = (where[longest] + shift) % values.shape[longest]
        spots.append(tuple(where))
    return values.at[spots[0]].set(low).at[spots[1]].set(top_value)


def steps_of(own_key, shape, pieces, smallest, top_value):
    def one(axis_at, blocks):
        heights = jax.random.uniform(jax.random.fold_in(jax.random.fold_in(own_key, 6), axis_at), (blocks,), jnp.float32, smallest / len(pieces), top_value / len(pieces))
        return jnp.repeat(jnp.exp(heights), shape[axis_at] // blocks).reshape((-1,) + (1,) * (len(shape) - axis_at - 1))

    loudness = one(*pieces[0])
    for cut in pieces[1:]:
        loudness = loudness * one(*cut)
    return loudness


def centred(own_key, dims, deviation, bound, cuts=(), kind=jnp.bfloat16):
    values = deviation * jax.random.normal(own_key, dims, jnp.float32)
    if cuts:
        values = values * steps_of(own_key, dims, cuts, -0.22, 0.18)
    return jnp.clip(values, -bound, bound).astype(kind)


def setup_inputs(seed: int = 0) -> dict:
    streams_of = jax.random.split(jax.random.key(seed), 8)
    atmos = centred(streams_of[0], (3, LEV, NYA, NXA), 1.0, 3.0, ((2, 8), (3, 16)), jnp.float32)
    slot_tile = draw_slot_tile(jax.random.fold_in(streams_of[7], 71), 0)
    fuel_cat = touch_ends(jax.random.randint(streams_of[2], (DEVICES * SLOTS, FC), 0, NFUEL), jax.random.fold_in(streams_of[2], 1), 0, NFUEL - 1).astype(jnp.int32)
    front_burn = touch_ends((jax.random.randint(streams_of[3], (DEVICES * SLOTS, FC), 0, 3) < 1).astype(jnp.int32), jax.random.fold_in(streams_of[3], 1), 0, 1)
    front_depth = jnp.clip(jnp.exp(math.log(2.0) - 2.3025851 * jax.random.uniform(streams_of[4], (DEVICES * SLOTS, FC), jnp.float32) ** steps_of(streams_of[4], (DEVICES * SLOTS, FC), ((0, 128),), -0.2, 0.2)), 0.2, 2.0)
    fuel_rate = jnp.clip(jnp.exp(jax.random.uniform(streams_of[5], (NFUEL,), jnp.float32, math.log(0.1), math.log(0.6))), 0.1, 0.6)
    fuel_heat = jnp.clip(jnp.exp(jax.random.uniform(streams_of[6], (NFUEL,), jnp.float32, math.log(0.5), math.log(5.0))), 0.5, 5.0)
    return dict(atmos=atmos, slot_tile=slot_tile, fuel_cat=fuel_cat, front_burn=front_burn, front_depth=front_depth, fuel_rate=fuel_rate, fuel_heat=fuel_heat)


TIME_STEP = 0.2
LATERAL_MIXING = 0.25
VERTICAL_MIXING = 0.5
CORIOLIS = 0.3
BUOYANCY = 0.5
HEAT_GAIN = 1.0
FIRE_STEP = 1.0
WIND_GAIN = 1.0
FRONT_WIDTH = 0.5

def tendency(padded):
    centre = padded[:, :, 1:-1, 1:-1]
    eastern = padded[:, :, 1:-1, 2:]
    western = padded[:, :, 1:-1, :-2]
    northern = padded[:, :, 2:, 1:-1]
    southern = padded[:, :, :-2, 1:-1]
    zonal_wind = centre[0:1]
    north_wind = centre[1:2]
    advect = jnp.maximum(zonal_wind, 0.0) * (centre - western) + jnp.minimum(zonal_wind, 0.0) * (eastern - centre) + jnp.maximum(north_wind, 0.0) * (centre - southern) + jnp.minimum(north_wind, 0.0) * (northern - centre)
    lateral = eastern + western + northern + southern - 4.0 * centre
    above_level = jnp.concatenate([centre[:, 1:], centre[:, -1:]], axis=1)
    below_level = jnp.concatenate([centre[:, :1], centre[:, :-1]], axis=1)
    vertical = above_level + below_level - 2.0 * centre
    change = -advect + LATERAL_MIXING * lateral + VERTICAL_MIXING * vertical
    slope_east = 0.5 * (eastern[2] - western[2])
    slope_north = 0.5 * (northern[2] - southern[2])
    zonal_change = change[0] + CORIOLIS * centre[1] - BUOYANCY * slope_east
    north_change = change[1] - CORIOLIS * centre[0] - BUOYANCY * slope_north
    return jnp.stack([zonal_change, north_change, change[2]])

def advance(air_state, extend):
    first_rate = tendency(extend(air_state))
    middle = air_state + TIME_STEP * first_rate
    second = tendency(extend(middle))
    return air_state + 0.5 * TIME_STEP * (first_rate + second)

def fire_advance(front_level, tile_wind, rate_cell, heat_cell):
    tile_count = front_level.shape[0]
    fire_rows = FTY * REF
    fire_cols = FTX * REF
    tile_cells = FTY * FTX
    level_grid = front_level.reshape(tile_count, fire_rows, fire_cols)

    def spread_out(coarse):
        coarse = coarse.reshape(tile_count, FTY, 1, FTX, 1)
        return jnp.broadcast_to(coarse, (tile_count, FTY, REF, FTX, REF)).reshape(tile_count, fire_rows, fire_cols)
    zonal_fire = spread_out(tile_wind[:, :tile_cells])
    north_fire = spread_out(tile_wind[:, tile_cells:])
    edged_grid = jnp.pad(level_grid, ((0, 0), (1, 1), (1, 1)), mode='edge')
    slope_east = 0.5 * (edged_grid[:, 1:-1, 2:] - edged_grid[:, 1:-1, :-2])
    slope_north = 0.5 * (edged_grid[:, 2:, 1:-1] - edged_grid[:, :-2, 1:-1])
    stretch = jnp.sqrt(1.0 + slope_east * slope_east + slope_north * slope_north)
    along_wind = (zonal_fire * slope_east + north_fire * slope_north) / stretch
    rate_full = rate_cell.reshape(tile_count, fire_rows, fire_cols)
    heat_full = heat_cell.reshape(tile_count, fire_rows, fire_cols)
    spread_speed = rate_full * (1.0 + WIND_GAIN * jax.nn.softplus(along_wind))
    advanced = level_grid - FIRE_STEP * spread_speed * stretch
    released = heat_full * (jax.nn.sigmoid(-advanced / FRONT_WIDTH) - jax.nn.sigmoid(-level_grid / FRONT_WIDTH))
    per_cell = released.reshape(tile_count, FTY, REF, FTX, REF).mean(axis=(2, 4))
    return (advanced.reshape(tile_count, fire_rows * fire_cols), per_cell.reshape(tile_count, tile_cells))

def tile_blocks(air_state):
    surface = air_state[0:2, 0]
    tile_rows = surface.shape[1] // FTY
    tile_cols = surface.shape[2] // FTX
    blocks = surface.reshape(2, tile_rows, FTY, tile_cols, FTX).transpose(1, 3, 0, 2, 4)
    return blocks.reshape(tile_rows * tile_cols, 2 * FTY * FTX)

def heat_field(blocks, tile_rows, tile_cols):
    return blocks.reshape(tile_rows, tile_cols, FTY, FTX).transpose(0, 2, 1, 3).reshape(tile_rows * FTY, tile_cols * FTX)

def zero_rim(air_state):
    return jnp.pad(air_state, ((0, 0), (0, 0), (1, 1), (1, 1)))

def reference(atmos, slot_tile, fuel_cat, front_burn, front_depth, fuel_rate, fuel_heat):
    air_state = atmos
    is_live = slot_tile >= 0
    tile_ids = jnp.where(is_live, slot_tile, 0).astype(jnp.int32)
    rate_cell = fuel_rate[fuel_cat]
    heat_cell = fuel_heat[fuel_cat]
    front_level = jnp.where(front_burn == 1, -front_depth, front_depth)
    tile_rows = NYA // FTY
    tile_cols = NXA // FTX
    for section_index in range(STEPS):
        blocks = tile_blocks(air_state)
        tile_wind = jnp.where(is_live[:, None], blocks[tile_ids], 0.0)
        advanced, released = fire_advance(front_level, tile_wind, rate_cell, heat_cell)
        front_level = jnp.where(is_live[:, None], advanced, front_level)
        released = jnp.where(is_live[:, None], released, 0.0)
        heat_blocks = jnp.zeros((tile_rows * tile_cols, FTY * FTX), jnp.float32).at[tile_ids].add(released)
        air_state = advance(air_state, zero_rim)
        air_state = air_state.at[2, 0].add(HEAT_GAIN * heat_field(heat_blocks, tile_rows, tile_cols))
    return (air_state, front_level)
```

```python
import jax
import jax.numpy as jnp
import numpy as np
from jax import lax
from jax.experimental import pallas as pl
from jax.experimental.pallas import tpu as pltpu
from jax.sharding import PartitionSpec as P

AXES = ("ty", "tx")
NTY, NTX, DEVICES = 8, 16, 128
LEV, AY, AX = 16, 64, 128
SLOTS, FC = 24, 3200
ROWS = 88
TOP = 12
F32, BF16 = jnp.float32, jnp.bfloat16


def roll(x, shift, axis):
    size = x.shape[axis]
    return pltpu.roll(x, shift % size, axis) if shift % size else x


def iota(shape, dim):
    return lax.broadcasted_iota(jnp.int32, shape, dim)


def parts(x):
    high = x.astype(BF16)
    rest = x - high.astype(F32)
    middle = rest.astype(BF16)
    low = (rest - middle.astype(F32)).astype(BF16)
    return high, middle, low


def dot(a, b):
    return jnp.dot(a, b, preferred_element_type=F32)


def pick(onehot, x):
    a = onehot.astype(BF16)
    high, middle, low = parts(x)
    return dot(a, high) + dot(a, middle) + dot(a, low)


def swap_blocks(x):
    x = x.reshape(x.shape[0] // 8, 8, 128)
    sub, group = iota(x.shape, 1), iota(x.shape, 2) // 16
    for step in (1, 2, 4):
        sub_bit, group_bit = (sub & step) != 0, (group & step) != 0
        below = roll(roll(x, -step, 1), 16 * step, 2)
        above = roll(roll(x, step, 1), -16 * step, 2)
        x = jnp.where(sub_bit == group_bit, x, jnp.where(group_bit, below, above))
    return x.reshape(x.shape[0] * 8, 128)


def slot_facts(tile):
    row, col = tile >> 7, tile & 127
    owner = (row >> 3) * NTX + (col >> 3)
    local = (row & 7) * 8 + (col & 7)
    live = tile >= 0
    return jnp.where(live, owner, -1), local + 1, live


def earlier(member):
    lower = (iota((32, 32), 0) > iota((32, 32), 1)).astype(F32).astype(BF16)
    return dot(lower, member.astype(BF16))


def slots_of(owner, local, home):
    member = (owner == home).astype(F32)
    before = earlier(member)
    numbers = member * local.astype(F32)
    return [
        jnp.sum(jnp.where(before == float(j), numbers, 0.0), axis=0, keepdims=True)
        for j in (0, 1)
    ]


def pack_columns(atmos, east, west):
    lane = iota((AY, 128), 1)
    group, spot = lane // 16, lane % 16
    for half in range(2):
        to_east = jnp.zeros((AY, 128), F32)
        to_west = jnp.zeros((AY, 128), F32)
        for c in range(3):
            both = jnp.zeros((AY, 128), F32)
            for k in range(8):
                moved = roll(atmos[c, half * 8 + k], 16 * k + 4, 1)
                both = jnp.where(group == k, moved, both)
            inside = (spot >= 4 * c) & (spot < 4 * c + 4)
            to_east = jnp.where(inside, roll(both, 4 * c, 1), to_east)
            to_west = jnp.where(inside, roll(both, 4 * c - 4, 1), to_west)
        east[half] = to_east
        west[half] = to_west


def pack_rows(low_rows, high_rows, from_west, from_east, east, west, up, down):
    def put(piece, high, low):
        where = pl.ds(4 * (piece % 2), 4)
        up[piece // 2, where, :] = high
        down[piece // 2, where, :] = low

    for c in range(3):
        for level in range(LEV):
            put(c * LEV + level, high_rows[c, level, 4:8, :], low_rows[c, level, 0:4, :])
    for i, source in enumerate((from_west, from_east, east, west)):
        for half in range(2):
            put(48 + 2 * i + half, source[half, 60:64, :], source[half, 0:4, :])


def rim_of(c, from_west, from_east, east, west):
    spot = iota(east.shape, 1) % 16
    out = jnp.where(spot < 3, roll(east, -(4 * c + 1), 1), 0.0)
    out = jnp.where((spot >= 3) & (spot < 7), roll(from_east, 3 - 4 * c, 1), out)
    out = jnp.where((spot >= 8) & (spot < 12), roll(from_west, 8 - 4 * c, 1), out)
    return jnp.where((spot >= 12) & (spot < 15), roll(west, 12 - 4 * c, 1), out)


def inside_window(first, rows, flags):
    y = iota((rows, 128), 0) + (first - TOP)
    return ((y >= 0) | (flags[1] > 0)) & ((y < AY) | (flags[1] < NTY - 1))


def rim_inside(first, rows, flags):
    spot = iota((rows, 128), 1) % 16
    east_out = (spot >= 3) & (spot < 7) & (flags[2] == NTX - 1)
    west_out = (spot >= 8) & (spot < 12) & (flags[2] == 0)
    return inside_window(first, rows, flags) & ~(east_out | west_out)


def fill_rim(rim, halves, flags, messages, low, high):
    from_west, from_east, east, west = messages
    for c in range(3):
        for half in range(halves):
            body = rim_of(c, *(m[half] for m in messages))
            rim[c, half, TOP : TOP + AY, :] = jnp.where(rim_inside(TOP, AY, flags), body, 0.0)
            for source, first in ((low, 8), (high, 76)):
                pieces = []
                for i in range(4):
                    piece = 48 + 2 * i + half
                    pieces.append(source[piece // 2, 4 * (piece % 2) : 4 * (piece % 2) + 4, :])
                rows = rim_of(c, *pieces)
                rim[c, half, first : first + 4, :] = jnp.where(rim_inside(first, 4, flags), rows, 0.0)


def fill_main(main, atmos, levels, flags, low, high):
    for c in range(3):
        for level in range(levels):
            piece = c * LEV + level
            where = slice(4 * (piece % 2), 4 * (piece % 2) + 4)
            main[c, level, TOP : TOP + AY, :] = atmos[c, level]
            main[c, level, 8:12, :] = jnp.where(flags[1] > 0, low[piece // 2, where, :], 0.0)
            main[c, level, 76:80, :] = jnp.where(flags[1] < NTY - 1, high[piece // 2, where, :], 0.0)


def tendency(centre, east, west, north, south, vertical):
    u, v, _ = centre
    up, vp = jnp.maximum(u, 0.0), jnp.maximum(v, 0.0)
    k_west, k_east = up + 0.25, up - u + 0.25
    k_south, k_north = vp + 0.25, vp - v + 0.25
    k_centre = k_west + k_east + k_south + k_north + 1.0
    out = []
    for c in range(3):
        out.append(
            k_west * west[c]
            + k_east * east[c]
            + k_south * south[c]
            + k_north * north[c]
            + 0.5 * vertical[c]
            - k_centre * centre[c]
        )
    out[0] = out[0] + 0.3 * v - 0.25 * (east[2] - west[2])
    out[1] = out[1] - 0.3 * u - 0.25 * (north[2] - south[2])
    return out


def edge_lanes(rim, edge, halves):
    spot = iota((72, 128), 1) % 16
    for c in range(3):
        for half in range(halves):
            x = rim[c, half, 8:80, :]
            edge[c, half, 8:80, :] = jnp.where(spot == 4, roll(x, -7, 1), x)


def main_tendency(source, edge, level, last, first, rows):
    lane = iota((rows, 128), 1)
    above, below = jnp.minimum(level + 1, last), jnp.maximum(level - 1, 0)
    shift = 124 - 16 * (level % 8)
    here = pl.ds(first, rows)
    centre, east, west, north, south, vertical = [], [], [], [], [], []
    for c in range(3):
        x = source[c, level, here, :]
        side = pltpu.roll(edge[c, level // 8, here, :], shift, 1)
        centre.append(x)
        east.append(jnp.where(lane == 127, side, roll(x, -1, 1)))
        west.append(jnp.where(lane == 0, side, roll(x, 1, 1)))
        north.append(source[c, level, pl.ds(first + 1, rows), :])
        south.append(source[c, level, pl.ds(first - 1, rows), :])
        vertical.append(source[c, above, here, :] + source[c, below, here, :])
    return centre, tendency(centre, east, west, north, south, vertical)


def rim_tendency(source, halves, half, first, rows):
    lane = iota((rows, 128), 1)
    here = pl.ds(first, rows)
    centre, east, west, north, south, vertical = [], [], [], [], [], []
    for c in range(3):
        x = source[c, half, here, :]
        next_up = source[c, 1, here, :] if half == 0 and halves == 2 else x
        next_down = source[c, 0, here, :] if half == 1 else x
        above = jnp.where(lane < 112, roll(x, -16, 1), x if next_up is x else roll(next_up, -16, 1))
        below = jnp.where(lane >= 16, roll(x, 16, 1), x if next_down is x else roll(next_down, 16, 1))
        centre.append(x)
        east.append(roll(x, -1, 1))
        west.append(roll(x, 1, 1))
        north.append(source[c, half, pl.ds(first + 1, rows), :])
        south.append(source[c, half, pl.ds(first - 1, rows), :])
        vertical.append(above + below)
    return centre, tendency(centre, east, west, north, south, vertical)


CHUNKS = ((8, 24), (32, 24), (56, 24))


def first_stage(source, target, edge, low, high, last, flags):
    def body(level, carry):
        for first, rows in CHUNKS:
            centre, change = main_tendency(source, edge, level, last, first, rows)
            for c in range(3):
                value = centre[c] + 0.2 * change[c]
                if first != 32:
                    value = jnp.where(inside_window(first, rows, flags), value, 0.0)
                target[c, level, pl.ds(first, rows), :] = value
        return carry

    lax.fori_loop(low, high, body, 0)


def second_stage(source, state, edge, low, high, last, chunks, write):
    def body(level, carry):
        for first, rows in chunks:
            centre, change = main_tendency(source, edge, level, last, first, rows)
            for c in range(3):
                old = state[c, level, pl.ds(first, rows), :]
                write(c, level, first, rows, 0.5 * (old + centre[c]) + 0.1 * change[c])
        return carry

    lax.fori_loop(low, high, body, 0)


def first_rim_stage(source, target, halves, flags):
    for half in range(halves):
        for first, rows in CHUNKS:
            centre, change = rim_tendency(source, halves, half, first, rows)
            for c in range(3):
                value = centre[c] + 0.2 * change[c]
                target[c, half, pl.ds(first, rows), :] = jnp.where(rim_inside(first, rows, flags), value, 0.0)


def second_rim_stage(source, state, halves, flags):
    for half in range(halves):
        for first, rows in CHUNKS:
            centre, change = rim_tendency(source, halves, half, first, rows)
            for c in range(3):
                here = pl.ds(first, rows)
                value = 0.5 * (state[c, half, here, :] + centre[c]) + 0.1 * change[c]
                state[c, half, here, :] = jnp.where(rim_inside(first, rows, flags), value, 0.0)


def clear_ends(*buffers):
    for ref in buffers:
        for a in range(ref.shape[0]):
            for b in range(ref.shape[1]):
                ref[a, b, 0:8, :] = jnp.zeros((8, 128), F32)
                ref[a, b, 80:88, :] = jnp.zeros((8, 128), F32)


def wind_kernel(
    flags, atmos, from_west, from_east, east, west, low, high, tiles, out, main, middle, rim, rim_middle, edge
):
    clear_ends(main, middle, rim, rim_middle)
    fill_rim(rim, 1, flags, (from_west, from_east, east, west), low, high)
    fill_main(main, atmos, 3, flags, low, high)
    edge_lanes(rim, edge, 1)
    first_stage(main, middle, edge, 0, 2, 2, flags)
    first_rim_stage(rim, rim_middle, 1, flags)
    edge_lanes(rim_middle, edge, 1)
    later = [[], []]
    for first, rows in ((12, 32), (44, 32)):
        centre, change = main_tendency(middle, edge, 0, 2, first, rows)
        for c in range(2):
            later[c].append(0.5 * (main[c, 0, pl.ds(first, rows), :] + centre[c]) + 0.1 * change[c])
    fields = [atmos[0, 0], atmos[1, 0]] + [jnp.concatenate(x, axis=0) for x in later]
    blocks = jnp.concatenate([swap_blocks(f) for f in fields], axis=1)
    owner, local, _ = slot_facts(tiles[...])
    numbers = slots_of(owner, local, flags[0])
    wanted = iota((64, 128), 0).astype(F32) + 1.0
    chosen = jnp.concatenate([(n == wanted).astype(F32) for n in numbers], axis=0)
    chosen = chosen.T
    half = iota((128, 128), 1) // 64
    onehot = jnp.concatenate([jnp.where(half == j, chosen, 0.0) for j in (0, 1)], axis=0)
    picked = pick(onehot, jnp.concatenate([blocks, blocks], axis=0))
    for j in range(2):
        for q in range(4):
            out[pl.ds(j * 4 + q, 128, stride=8), :] = picked[j * 128 : (j + 1) * 128, q * 128 : (q + 1) * 128]


def step_kernel(
    flags, atmos, from_west, from_east, east, west, low, high, main, rim, middle, rim_middle, edge
):
    clear_ends(main, middle, rim, rim_middle)
    fill_rim(rim, 2, flags, (from_west, from_east, east, west), low, high)
    fill_main(main, atmos, LEV, flags, low, high)
    edge_lanes(rim, edge, 2)
    first_stage(main, middle, edge, 0, LEV, LEV - 1, flags)
    first_rim_stage(rim, rim_middle, 2, flags)
    edge_lanes(rim_middle, edge, 2)

    def write(c, level, first, rows, value):
        if first != 32:
            value = jnp.where(inside_window(first, rows, flags), value, 0.0)
        main[c, level, pl.ds(first, rows), :] = value

    second_stage(middle, main, edge, 0, LEV, LEV - 1, CHUNKS, write)
    second_rim_stage(rim_middle, rim, 2, flags)


def fuel_kernel(rates, heats, category, burn, depth, rate, heat, level):
    kind = category[...]
    rate_cell = jnp.zeros(kind.shape, F32)
    heat_cell = jnp.zeros(kind.shape, F32)
    for k in range(13):
        match = kind == k
        rate_cell = jnp.where(match, rates[k], rate_cell)
        heat_cell = jnp.where(match, heats[k], heat_cell)
    rate[...] = rate_cell
    heat[...] = heat_cell
    level[...] = jnp.where(burn[...] == 1, -depth[...], depth[...])


def fire_kernel(
    flags, received, tiles, rate, heat, level, column, spread, gather, out, new_level, wind, released
):
    mine = jnp.sum(
        jnp.where(iota((32, 128), 1) == flags[0], tiles[...].astype(F32), 0.0), axis=1, keepdims=True
    ).astype(jnp.int32)
    owner, _, live = slot_facts(mine)
    member = (owner == iota((32, 128), 1)).astype(F32)
    before = earlier(member)
    places = [jnp.where(before == float(j), member, 0.0) for j in (0, 1)]

    rows = [[received[pl.ds(j * 4 + q, 128, stride=8), :] for q in range(4)] for j in range(2)]
    table = jnp.concatenate([jnp.concatenate(r, axis=1) for r in rows], axis=0)
    winds = pick(jnp.concatenate(places, axis=1), table)
    winds = jnp.concatenate([winds[:, q * 128 : (q + 1) * 128] for q in range(4)], axis=0)
    high, middle, low = parts(winds)
    wind[...] = dot(high, spread[...]) + dot(middle, spread[...]) + dot(low, spread[...])

    col = column[...]
    cell = iota((8, FC), 1)
    first_col, last_col = col == 0, col == 79
    first_row, last_row = cell < 80, cell >= FC - 80
    for g in range(3):
        here = slice(8 * g, 8 * g + 8)
        alive = live[here]
        p = level[here, :]
        tanh_p = jnp.tanh(p)
        for t in range(2):
            u = wind[t * 64 + 8 * g : t * 64 + 8 * g + 8, :]
            v = wind[t * 64 + 32 + 8 * g : t * 64 + 40 + 8 * g, :]
            east = jnp.where(last_col, p, roll(p, -1, 1))
            west = jnp.where(first_col, p, roll(p, 1, 1))
            north = jnp.where(last_row, p, roll(p, -80, 1))
            south = jnp.where(first_row, p, roll(p, 80, 1))
            gx, gy = 0.5 * (east - west), 0.5 * (north - south)
            square = 1.0 + gx * gx + gy * gy
            inverse = lax.rsqrt(square)
            along = (u * gx + v * gy) * inverse
            softplus = jnp.maximum(along, 0.0) + jnp.log(1.0 + jnp.exp(-jnp.abs(along)))
            moved = p - rate[here, :] * (1.0 + softplus) * (square * inverse)
            p = jnp.where(alive, moved, p)
            tanh_new = jnp.tanh(p)
            released[t * 32 + 8 * g : t * 32 + 8 * g + 8, :] = heat[here, :] * (tanh_p - tanh_new)
            tanh_p = tanh_new
        new_level[here, :] = p
    for t in range(2):
        released[t * 32 + 24 : t * 32 + 32, :] = jnp.zeros((8, FC), F32)
    high, middle, low = parts(released[...])
    sums = 0.02 * (dot(high, gather[...]) + dot(middle, gather[...]) + dot(low, gather[...]))

    heats = jnp.concatenate([sums[0:32], sums[32:64]], axis=1)
    zeros = jnp.zeros((64, 256), F32)
    stacked = jnp.concatenate([heats, heats, zeros], axis=0)
    chosen = jnp.concatenate(places + [jnp.zeros((64, 128), F32)], axis=0).T
    part = iota((128, 128), 1) // 32
    onehot = jnp.concatenate([jnp.where(part == j, chosen, 0.0) for j in (0, 1)], axis=0)
    blocks = pick(onehot, stacked)
    lane = iota((128, 128), 1)
    group, spot = lane // 16, lane % 16
    for j in range(2):
        first = blocks[j * 128 : (j + 1) * 128, 0:128]
        out[pl.ds(j, 128, stride=8), :] = first
        out[pl.ds(2 + j, 128, stride=8), :] = blocks[j * 128 : (j + 1) * 128, 128:256]
        north, south = roll(first, -16, 0), roll(first, 16, 0)
        west, east = roll(first, 1, 0), roll(first, -1, 0)
        strip = jnp.where(group < 2, north, jnp.where(group >= 6, south, 0.0))
        middle_rows = (group >= 2) & (group < 6)
        west_moved = jnp.where(group < 4, roll(west, 30, 1), roll(west, -34, 1))
        east_moved = jnp.where(group < 4, roll(east, 34, 1), roll(east, -30, 1))
        strip = jnp.where(middle_rows & (spot >= 14), west, strip)
        strip = jnp.where(middle_rows & ((spot == 12) | (spot == 13)), west_moved, strip)
        strip = jnp.where(middle_rows & (spot < 2), east, strip)
        strip = jnp.where(middle_rows & ((spot == 2) | (spot == 3)), east_moved, strip)
        strip = jnp.where(lane == 40, roll(roll(first, 17, 0), 41, 1), strip)
        strip = jnp.where(lane == 41, roll(roll(first, 15, 0), 57, 1), strip)
        strip = jnp.where(lane == 56, roll(roll(first, -15, 0), 41, 1), strip)
        strip = jnp.where(lane == 57, roll(roll(first, -17, 0), 57, 1), strip)
        out[pl.ds(4 + j, 128, stride=8), :] = strip
        out[pl.ds(6 + j, 128, stride=8), :] = jnp.zeros((128, 128), F32)


def heat_fields(flags, received, tiles):
    me, ty, tx = flags[0], flags[1], flags[2]
    owner, local, _ = slot_facts(tiles[...])

    def numbers(dy, dx):
        ok = (ty + dy >= 0) & (ty + dy < NTY) & (tx + dx >= 0) & (tx + dx < NTX)
        return slots_of(owner, local, jnp.where(ok, me + dy * NTX + dx, -7))

    here = numbers(0, 0)
    north, south, west, east = numbers(1, 0), numbers(-1, 0), numbers(0, -1), numbers(0, 1)
    south_west, south_east = numbers(-1, -1), numbers(-1, 1)
    north_west, north_east = numbers(1, -1), numbers(1, 1)
    tile = iota((64, 128), 0).astype(F32) + 1.0
    edge_tile = iota((8, 128), 0).astype(F32) + 1.0
    row = iota((80, 128), 0)
    first_tile = ((row // 8 - 1) * 8 + 1).astype(F32)
    body = (row >= 8) & (row < 72)
    home, strips = [], []
    for j in range(2):
        home.append((here[j] == tile).astype(F32))
        from_south = (south[j] == edge_tile + 56.0).astype(F32)
        from_north = (north[j] == edge_tile).astype(F32)
        from_west = body & (west[j] == first_tile + 7.0)
        from_west = from_west | ((row == 7) & (south_west[j] == 64.0)) | ((row == 72) & (north_west[j] == 8.0))
        from_east = body & (east[j] == first_tile)
        from_east = from_east | ((row == 7) & (south_east[j] == 57.0)) | ((row == 72) & (north_east[j] == 1.0))
        strips.append(
            jnp.concatenate([from_south, from_north, from_west.astype(F32), from_east.astype(F32)], axis=0)
        )
    rows = [received[pl.ds(q, 128, stride=8), :] for q in range(6)]
    table = jnp.concatenate(
        [jnp.concatenate([rows[0], rows[2]], axis=1), jnp.concatenate([rows[1], rows[3]], axis=1)], axis=0
    )
    home = pick(jnp.concatenate(home, axis=1), table)
    strips = pick(jnp.concatenate(strips, axis=1), jnp.concatenate(rows[4:6], axis=0))
    lane8 = iota((8, 128), 1)
    blocks = jnp.concatenate(
        [
            jnp.where(lane8 >= 96, strips[0:8], 0.0),
            home[:, 0:128],
            jnp.where(lane8 < 32, strips[8:16], 0.0),
        ],
        axis=0,
    )
    first, second = swap_blocks(blocks), swap_blocks(home[:, 128:256])

    lane = iota((80, 128), 1)
    group, spot, y = lane // 16, lane % 16, row % 8
    straight = (y >= 2) & (y < 6)
    corner = (row == 7) | (row == 72)
    wanted_group = jnp.where(y < 2, y + 2, jnp.where(y > 5, y - 2, y))
    wanted_group = jnp.where(row == 7, 2, jnp.where(row == 72, 3, wanted_group))
    fits = group == wanted_group
    west_spot = spot - jnp.where(corner, 8, jnp.where(straight, 14, 12))
    east_spot = spot - jnp.where(corner, 9, jnp.where(straight, 0, 2))
    width = jnp.where(corner, 1, 2)
    west_fits = fits & (west_spot >= 0) & (west_spot < width)
    east_fits = fits & (east_spot >= 0) & (east_spot < width)
    value = jnp.where(west_fits, strips[16:96], 0.0) + jnp.where(east_fits, strips[96:176], 0.0)
    for shift in (64, 32, 16):
        value = value + roll(value, shift, 1)
    to_west = jnp.where(corner, roll(value, 3, 1), jnp.where(straight, roll(value, -4, 1), roll(value, -2, 1)))
    to_east = jnp.where(corner, roll(value, -6, 1), jnp.where(straight, roll(value, 3, 1), roll(value, 1, 1)))
    rim = jnp.where((lane == 11) | ((lane == 10) & ~corner), to_west, 0.0)
    rim = jnp.where((lane == 3) | ((lane == 4) & ~corner), to_east, rim)
    rim = jnp.where((lane == 12) | (lane == 13), roll(first, 12, 1), rim)
    rim = jnp.where((lane == 1) | (lane == 2), roll(first, 3, 1), rim)
    return first, second, rim


def last_kernel(flags, received, tiles, main_in, rim_in, out, main, middle, rim, rim_middle, edge, sems):
    copies = [
        pltpu.make_async_copy(main_in, main, sems.at[0]),
        pltpu.make_async_copy(rim_in, rim, sems.at[1]),
    ]
    for copy in copies:
        copy.start()
    clear_ends(middle, rim_middle)
    first, second, rim_heat = heat_fields(flags, received, tiles)
    for copy in copies:
        copy.wait()
    main[2, 0, 4:84, :] = main[2, 0, 4:84, :] + first
    rim[2, 0, 4:84, :] = rim[2, 0, 4:84, :] + rim_heat
    edge_lanes(rim, edge, 2)
    first_stage(main, middle, edge, 0, LEV, LEV - 1, flags)
    first_rim_stage(rim, rim_middle, 2, flags)
    edge_lanes(rim_middle, edge, 2)

    def write(c, level, first_row, rows, value):
        out[c, level, pl.ds(first_row - TOP, rows), :] = value

    second_stage(middle, main, edge, 0, LEV, LEV - 1, ((12, 32), (44, 32)), write)
    out[2, 0] = out[2, 0] + second


SMEM = pl.BlockSpec(memory_space=pltpu.SMEM)
VMEM = pl.BlockSpec(memory_space=pltpu.VMEM)
ANY = pl.BlockSpec(memory_space=pl.ANY)


def shape(*dims):
    return jax.ShapeDtypeStruct(dims, F32)


def call(kernel, out_shape, in_specs, scratch=(), flops=0, moved=0, name=None):
    return pl.pallas_call(
        kernel,
        out_shape=out_shape,
        in_specs=in_specs,
        out_specs=jax.tree.map(lambda _: VMEM, out_shape),
        scratch_shapes=list(scratch),
        compiler_params=pltpu.CompilerParams(vmem_limit_bytes=48 << 20),
        cost_estimate=pl.CostEstimate(flops=flops, bytes_accessed=moved, transcendentals=0),
        name=name,
    )


def fire_tables():
    cell = np.arange(FC)
    coarse = (cell // 80 // 5) * 16 + cell % 80 // 5
    spread = (coarse[None, :] == np.arange(128)[:, None]).astype(np.float32)
    column = np.broadcast_to((cell % 80).astype(np.int32)[None, :], (8, FC))
    return jnp.asarray(spread, BF16), jnp.asarray(spread.T, BF16), jnp.asarray(column)


def both_ways(to_next, to_previous, axis):
    size = lax.axis_size(axis)
    ahead = [(i, (i + 1) % size) for i in range(size)]
    return (
        lax.ppermute(to_next, axis, ahead),
        lax.ppermute(to_previous, axis, [(j, i) for i, j in ahead]),
    )


def exchange(x):
    return lax.all_to_all(x.reshape(DEVICES, 8, 128), AXES, 0, 0, tiled=True).reshape(DEVICES * 8, 128)


def on_device(atmos, slot_tile, fuel_cat, front_burn, front_depth, fuel_rate, fuel_heat):
    ty, tx = lax.axis_index("ty"), lax.axis_index("tx")
    flags = jnp.stack([ty * NTX + tx, ty, tx]).astype(jnp.int32)
    tiles = jnp.pad(slot_tile.reshape(DEVICES, SLOTS).T, ((0, 8), (0, 0)), constant_values=-1)
    spread, gather, column = fire_tables()

    message = shape(2, AY, 128)
    east, west = call(pack_columns, (message, message), [VMEM], flops=4_000_000, moved=1_800_000)(atmos)
    from_west, from_east = both_ways(east, west, "tx")
    rate, heat, level = call(
        fuel_kernel, (shape(SLOTS, FC),) * 3, [SMEM, SMEM, VMEM, VMEM, VMEM], flops=4_000_000, moved=1_800_000
    )(fuel_rate, fuel_heat, fuel_cat, front_burn, front_depth)

    rows = shape(28, 8, 128)
    up, down = pl.pallas_call(
        pack_rows,
        grid=(1,),
        out_shape=(rows, rows),
        in_specs=[
            pl.BlockSpec((3, LEV, 8, 128), lambda i: (0, 0, 0, 0)),
            pl.BlockSpec((3, LEV, 8, 128), lambda i: (0, 0, 7, 0)),
        ]
        + [pl.BlockSpec((2, AY, 128), lambda i: (0, 0, 0))] * 4,
        out_specs=(pl.BlockSpec((28, 8, 128), lambda i: (0, 0, 0)),) * 2,
        compiler_params=pltpu.CompilerParams(vmem_limit_bytes=48 << 20),
        name="pack_rows",
    )(atmos, atmos, from_west, from_east, east, west)
    low, high = both_ways(up, down, "ty")

    halo = (from_west, from_east, east, west, low, high)

    def main_buffer(levels):
        return pltpu.VMEM((3, levels, ROWS, 128), F32)

    def rim_buffer(halves):
        return pltpu.VMEM((3, halves, ROWS, 128), F32)

    surface = pl.BlockSpec((3, 4, AY, 128), lambda i: (0, 0, 0, 0))
    whole2 = [pl.BlockSpec((2, AY, 128), lambda i: (0, 0, 0))] * 4
    whole3 = [pl.BlockSpec((28, 8, 128), lambda i: (0, 0, 0))] * 2
    winds = pl.pallas_call(
        wind_kernel,
        grid=(1,),
        out_shape=shape(DEVICES * 8, 128),
        in_specs=[SMEM, surface] + whole2 + whole3 + [pl.BlockSpec((32, 128), lambda i: (0, 0))],
        out_specs=pl.BlockSpec((DEVICES * 8, 128), lambda i: (0, 0)),
        scratch_shapes=[main_buffer(3), main_buffer(3), rim_buffer(1), rim_buffer(1), rim_buffer(1)],
        compiler_params=pltpu.CompilerParams(vmem_limit_bytes=48 << 20),
        name="wind",
    )(flags, atmos, *halo, tiles)
    got_winds = exchange(winds)

    main, rim = call(
        step_kernel,
        (shape(3, LEV, ROWS, 128), shape(3, 2, ROWS, 128)),
        [SMEM] + [VMEM] * 7,
        [main_buffer(LEV), rim_buffer(2), rim_buffer(2)],
        flops=40_000_000,
        moved=8_000_000,
    )(flags, atmos, *halo)

    heats, fire_level = call(
        fire_kernel,
        (shape(DEVICES * 8, 128), shape(SLOTS, FC)),
        [SMEM] + [VMEM] * 8,
        [pltpu.VMEM((128, FC), F32), pltpu.VMEM((64, FC), F32)],
        flops=40_000_000,
        moved=4_000_000,
    )(flags, got_winds, tiles, rate, heat, level, column, spread, gather)
    got_heats = exchange(heats)

    atmos_out = call(
        last_kernel,
        shape(3, LEV, AY, 128),
        [SMEM, VMEM, VMEM, ANY, ANY],
        [
            main_buffer(LEV),
            main_buffer(LEV),
            rim_buffer(2),
            rim_buffer(2),
            rim_buffer(2),
            pltpu.SemaphoreType.DMA((2,)),
        ],
        flops=40_000_000,
        moved=8_000_000,
    )(flags, got_heats, tiles, main, rim)
    return atmos_out, fire_level


def solution(mesh):
    in_specs = (
        P(None, None, "ty", "tx"),
        P(),
        P(("ty", "tx"), None),
        P(("ty", "tx"), None),
        P(("ty", "tx"), None),
        P(),
        P(),
    )
    out_specs = (P(None, None, "ty", "tx"), P(("ty", "tx"), None))
    return jax.shard_map(
        on_device, mesh=mesh, in_specs=in_specs, out_specs=out_specs, check_vma=False
    )
```

```python
import jax
import jax.numpy as jnp
from jax import lax
from jax.experimental import pallas as pl
from jax.experimental.pallas import tpu as pltpu
from jax.sharding import PartitionSpec as P

AXES = ("ty", "tx")
NTY, NTX, DEVICES = 8, 16, 128
LEV, AY, AX = 16, 64, 128
SLOTS, FC = 24, 3200
ROWS = 88
TOP = 12
F32, BF16 = jnp.float32, jnp.bfloat16


def roll(x, shift, axis):
    size = x.shape[axis]
    return pltpu.roll(x, shift % size, axis) if shift % size else x


def iota(shape, dim):
    return lax.broadcasted_iota(jnp.int32, shape, dim)


def parts(x):
    high = x.astype(BF16)
    rest = x - high.astype(F32)
    middle = rest.astype(BF16)
    low = (rest - middle.astype(F32)).astype(BF16)
    return high, middle, low


def dot(a, b):
    return jnp.dot(a, b, preferred_element_type=F32)


def dot_rows(a, b):
    return lax.dot_general(a, b, (((1,), (1,)), ((), ())), preferred_element_type=F32)


def pick(onehot, x):
    high, middle, _ = parts(x)
    return dot(onehot, high) + dot(onehot, middle)


def swap_blocks(x):
    x = x.reshape(x.shape[0] // 8, 8, 128)
    sub, group = iota(x.shape, 1), iota(x.shape, 2) // 16
    for step in (1, 2, 4):
        sub_bit, group_bit = (sub & step) != 0, (group & step) != 0
        below = roll(roll(x, -step, 1), 16 * step, 2)
        above = roll(roll(x, step, 1), -16 * step, 2)
        x = jnp.where(sub_bit == group_bit, x, jnp.where(group_bit, below, above))
    return x.reshape(x.shape[0] * 8, 128)


def pick_right(x, onehot, product):
    high, middle, _ = parts(x)
    return product(high, onehot) + product(middle, onehot)


def slot_facts(tile):
    row, col = tile >> 7, tile & 127
    owner = (row >> 3) * NTX + (col >> 3)
    local = (row & 7) * 8 + (col & 7)
    live = tile >= 0
    return jnp.where(live, owner, -1), local + 1, live


def earlier(member):
    lower = (iota((32, 32), 0) > iota((32, 32), 1)).astype(F32).astype(BF16)
    return dot(lower, member.astype(BF16))


def slots_of(owner, local, home):
    member = (owner == home).astype(F32)
    before = earlier(member)
    numbers = member * local.astype(F32)
    return [
        jnp.sum(jnp.where(before == float(j), numbers, 0.0), axis=0, keepdims=True)
        for j in (0, 1)
    ]


def pack_rows(atmos, up, down, low_rows, high_rows, sems):
    copies = [
        pltpu.make_async_copy(atmos.at[:, :, pl.ds(0, 8), :], low_rows, sems.at[0]),
        pltpu.make_async_copy(atmos.at[:, :, pl.ds(AY - 8, 8), :], high_rows, sems.at[1]),
    ]
    for copy in copies:
        copy.start()
    for copy in copies:
        copy.wait()
    for c in range(3):
        for level in range(LEV):
            plane = c * LEV + level
            where = pl.ds(4 * (plane % 2), 4)
            up[plane // 2, where, :] = high_rows[c, level, 4:8, :]
            down[plane // 2, where, :] = low_rows[c, level, 0:4, :]


def packed_columns(plane, half, rows):
    lane = iota((rows, 128), 1)
    group, spot = lane // 16, lane % 16
    to_east = jnp.zeros((rows, 128), F32)
    to_west = jnp.zeros((rows, 128), F32)
    for c in range(3):
        both = jnp.zeros((rows, 128), F32)
        for k in range(8):
            moved = roll(plane(c, half * 8 + k), 16 * k + 4, 1)
            both = jnp.where(group == k, moved, both)
        inside = (spot >= 4 * c) & (spot < 4 * c + 4)
        to_east = jnp.where(inside, roll(both, 4 * c, 1), to_east)
        to_west = jnp.where(inside, roll(both, 4 * c - 4, 1), to_west)
    return to_east, to_west


def pack_columns(atmos, east, west, surface, blocks, planes, sems):
    copies = [
        pltpu.make_async_copy(atmos.at[:, pl.ds(8 * half, 8)], planes.at[:, pl.ds(8 * half, 8)], sems.at[half])
        for half in range(2)
    ]
    for copy in copies:
        copy.start()
    for half in range(2):
        copies[half].wait()
        if half == 0:
            surface[...] = planes[:, 0:3]
            blocks[...] = jnp.concatenate([swap_blocks(planes[c, 0]) for c in range(2)], axis=1)
        east[half], west[half] = packed_columns(lambda c, level: planes[c, level], half, AY)


def join_columns(east_rows, west_rows, low, high, east, west):
    def plane(c, level):
        piece = c * LEV + level
        where = slice(4 * (piece % 2), 4 * (piece % 2) + 4)
        return jnp.concatenate([low[piece // 2, where, :], high[piece // 2, where, :]], axis=0)

    for half in range(2):
        east[half, 0:AY, :] = east_rows[half]
        west[half, 0:AY, :] = west_rows[half]
        east[half, AY : AY + 8, :], west[half, AY : AY + 8, :] = packed_columns(plane, half, 8)


def rim_of(c, from_west, from_east, east, west):
    spot = iota(east.shape, 1) % 16
    out = jnp.where(spot < 3, roll(east, -(4 * c + 1), 1), 0.0)
    out = jnp.where((spot >= 3) & (spot < 7), roll(from_east, 3 - 4 * c, 1), out)
    out = jnp.where((spot >= 8) & (spot < 12), roll(from_west, 8 - 4 * c, 1), out)
    return jnp.where((spot >= 12) & (spot < 15), roll(west, 12 - 4 * c, 1), out)


def inside_window(first, rows, flags):
    y = iota((rows, 128), 0) + (first - TOP)
    return ((y >= 0) | (flags[1] > 0)) & ((y < AY) | (flags[1] < NTY - 1))


def rim_inside(first, rows, flags):
    spot = iota((rows, 128), 1) % 16
    east_out = (spot >= 3) & (spot < 7) & (flags[2] == NTX - 1)
    west_out = (spot >= 8) & (spot < 12) & (flags[2] == 0)
    return inside_window(first, rows, flags) & ~(east_out | west_out)


def fill_rim(rim, halves, flags, messages):
    for c in range(3):
        for half in range(halves):
            for source, first, rows in ((0, TOP, AY), (AY, 8, 4), (AY + 4, 76, 4)):
                value = rim_of(c, *(m[half, source : source + rows, :] for m in messages))
                rim[c, half, first : first + rows, :] = jnp.where(rim_inside(first, rows, flags), value, 0.0)


def fill_main(main, atmos, levels, flags, low, high):
    for c in range(3):
        for level in levels:
            piece = c * LEV + level
            where = slice(4 * (piece % 2), 4 * (piece % 2) + 4)
            main[c, level, TOP : TOP + AY, :] = atmos[c, level]
            main[c, level, 8:12, :] = jnp.where(flags[1] > 0, low[piece // 2, where, :], 0.0)
            main[c, level, 76:80, :] = jnp.where(flags[1] < NTY - 1, high[piece // 2, where, :], 0.0)


def tendency(centre, east, west, north, south, vertical):
    u, v, _ = centre
    up, vp = jnp.maximum(u, 0.0), jnp.maximum(v, 0.0)
    k_west, k_east = up + 0.25, up - u + 0.25
    k_south, k_north = vp + 0.25, vp - v + 0.25
    k_centre = k_west + k_east + k_south + k_north + 1.0
    out = []
    for c in range(3):
        out.append(
            k_west * west[c]
            + k_east * east[c]
            + k_south * south[c]
            + k_north * north[c]
            + 0.5 * vertical[c]
            - k_centre * centre[c]
        )
    out[0] = out[0] + 0.3 * v - 0.25 * (east[2] - west[2])
    out[1] = out[1] - 0.3 * u - 0.25 * (north[2] - south[2])
    return out


def edge_lanes(rim, edge, halves):
    spot = iota((72, 128), 1) % 16
    for c in range(3):
        for half in range(halves):
            x = rim[c, half, 8:80, :]
            edge[c, half, 8:80, :] = jnp.where(spot == 4, roll(x, -7, 1), x)


def main_tendency(source, edge, level, last, first, rows):
    lane = iota((rows, 128), 1)
    above, below = min(level + 1, last), max(level - 1, 0)
    here = pl.ds(first, rows)
    centre, east, west, north, south, vertical = [], [], [], [], [], []
    for c in range(3):
        x = source[c, level, here, :]
        side = roll(edge[c, level // 8, here, :], 124 - 16 * (level % 8), 1)
        centre.append(x)
        east.append(jnp.where(lane == 127, side, roll(x, -1, 1)))
        west.append(jnp.where(lane == 0, side, roll(x, 1, 1)))
        north.append(source[c, level, pl.ds(first + 1, rows), :])
        south.append(source[c, level, pl.ds(first - 1, rows), :])
        vertical.append(source[c, above, here, :] + source[c, below, here, :])
    return centre, tendency(centre, east, west, north, south, vertical)


def rim_tendency(source, halves, half, first, rows):
    lane = iota((rows, 128), 1)
    here = pl.ds(first, rows)
    centre, east, west, north, south, vertical = [], [], [], [], [], []
    for c in range(3):
        x = source[c, half, here, :]
        next_up = source[c, 1, here, :] if half == 0 and halves == 2 else x
        next_down = source[c, 0, here, :] if half == 1 else x
        above = jnp.where(lane < 112, roll(x, -16, 1), x if next_up is x else roll(next_up, -16, 1))
        below = jnp.where(lane >= 16, roll(x, 16, 1), x if next_down is x else roll(next_down, 16, 1))
        centre.append(x)
        east.append(roll(x, -1, 1))
        west.append(roll(x, 1, 1))
        north.append(source[c, half, pl.ds(first + 1, rows), :])
        south.append(source[c, half, pl.ds(first - 1, rows), :])
        vertical.append(above + below)
    return centre, tendency(centre, east, west, north, south, vertical)


CHUNKS = ((8, 24), (32, 24), (56, 24))
ALL_ROWS = tuple(range(8, 80, 8))
BODY = tuple(range(TOP, TOP + AY, 8))


def window_masks(flags):
    return {first: inside_window(first, 8, flags) for first in (8, 72)}


def first_stage(source, target, edge, levels, last, masks):
    for level in levels:
        for first in ALL_ROWS:
            centre, change = main_tendency(source, edge, level, last, first, 8)
            for c in range(3):
                value = centre[c] + 0.2 * change[c]
                if first in masks:
                    value = jnp.where(masks[first], value, 0.0)
                target[c, level, first : first + 8, :] = value


def second_stage(source, state, edge, levels, last, rows, write):
    for level in levels:
        for first in rows:
            centre, change = main_tendency(source, edge, level, last, first, 8)
            for c in range(3):
                old = state[c, level, first : first + 8, :]
                write(c, level, first, 0.5 * (old + centre[c]) + 0.1 * change[c])


def first_rim_stage(source, target, halves, flags):
    for half in range(halves):
        for first, rows in CHUNKS:
            centre, change = rim_tendency(source, halves, half, first, rows)
            for c in range(3):
                value = centre[c] + 0.2 * change[c]
                target[c, half, pl.ds(first, rows), :] = jnp.where(rim_inside(first, rows, flags), value, 0.0)


def second_rim_stage(source, state, halves, flags):
    for half in range(halves):
        for first, rows in CHUNKS:
            centre, change = rim_tendency(source, halves, half, first, rows)
            for c in range(3):
                here = pl.ds(first, rows)
                value = 0.5 * (state[c, half, here, :] + centre[c]) + 0.1 * change[c]
                state[c, half, here, :] = jnp.where(rim_inside(first, rows, flags), value, 0.0)


def plan_kernel(flags, tiles, wind_plan, fire_plan, fire_sends, alive, home_plan, strip_plan):
    me, ty, tx = flags[0], flags[1], flags[2]
    listed = tiles[...]
    owner, local, _ = slot_facts(listed)

    def numbers(dy, dx):
        ok = (ty + dy >= 0) & (ty + dy < NTY) & (tx + dx >= 0) & (tx + dx < NTX)
        return slots_of(owner, local, jnp.where(ok, me + dy * NTX + dx, -7))

    here = numbers(0, 0)
    north, south, west, east = numbers(1, 0), numbers(-1, 0), numbers(0, -1), numbers(0, 1)
    south_west, south_east = numbers(-1, -1), numbers(-1, 1)
    north_west, north_east = numbers(1, -1), numbers(1, 1)
    tile = iota((64, 128), 0).astype(F32) + 1.0
    edge_tile = iota((8, 128), 0).astype(F32) + 1.0
    row = iota((80, 128), 0)
    first_tile = ((row // 8 - 1) * 8 + 1).astype(F32)
    body = (row >= 8) & (row < 72)

    for j in range(2):
        chosen = (here[j] == tile).astype(F32)
        chosen = jnp.concatenate([chosen, chosen], axis=0).T.astype(BF16)
        wind_plan[j * 128 : (j + 1) * 128, 0:128] = chosen
        wind_plan[j * 128 : (j + 1) * 128, 128:256] = chosen
    mine = jnp.sum(
        jnp.where(iota((32, 128), 1) == me, listed.astype(F32), 0.0), axis=1, keepdims=True
    ).astype(jnp.int32)
    holder, _, live = slot_facts(mine)
    member = (holder == iota((32, 128), 1)).astype(F32)
    before = earlier(member)
    places = [jnp.where(before == float(j), member, 0.0) for j in (0, 1)]
    fire_plan[...] = jnp.concatenate(places, axis=1).astype(BF16)
    alive[...] = jnp.where(live, jnp.ones((32, 128), F32), 0.0)

    chosen = jnp.concatenate(places + [jnp.zeros((64, 128), F32)], axis=0).T
    part = iota((128, 128), 1) // 32
    for j in range(2):
        fire_sends[j * 128 : (j + 1) * 128, :] = jnp.where(part == j, chosen, 0.0).astype(BF16)
        from_south = (south[j] == edge_tile + 56.0).astype(F32)
        from_north = (north[j] == edge_tile).astype(F32)
        from_west = body & (west[j] == first_tile + 7.0)
        from_west = from_west | ((row == 7) & (south_west[j] == 64.0)) | ((row == 72) & (north_west[j] == 8.0))
        from_east = body & (east[j] == first_tile)
        from_east = from_east | ((row == 7) & (south_east[j] == 57.0)) | ((row == 72) & (north_east[j] == 1.0))
        lanes = slice(j * 128, (j + 1) * 128)
        home_plan[:, lanes] = (here[j] == tile).astype(F32).astype(BF16)
        strips = [from_south, from_north, from_west.astype(F32), from_east.astype(F32)]
        strip_plan[:, lanes] = jnp.concatenate(strips, axis=0).astype(BF16)


def wind_kernel(
    flags, planes, blocks, from_west, from_east, east, west, low, high, plan, fuel, out, main, middle, rim, rim_middle,
    edge,
):
    fill_rim(rim, 1, flags, (from_west, from_east, east, west))
    fill_main(main, planes, range(3), flags, low, high)
    edge_lanes(rim, edge, 1)
    first_stage(main, middle, edge, range(2), 2, window_masks(flags))
    first_rim_stage(rim, rim_middle, 1, flags)
    edge_lanes(rim_middle, edge, 1)
    later = [[], []]
    for first in BODY:
        centre, change = main_tendency(middle, edge, 0, 2, first, 8)
        for c in range(2):
            later[c].append(0.5 * (main[c, 0, first : first + 8, :] + centre[c]) + 0.1 * change[c])
    fields = [blocks[...]] + [swap_blocks(jnp.concatenate(x, axis=0)) for x in later]
    pieces = parts(jnp.concatenate(fields, axis=1))
    pieces = jnp.concatenate(pieces + (jnp.zeros((64, 512), BF16),), axis=0)
    picked = dot(plan[...], pieces)
    for j in range(2):
        for q in range(4):
            out[pl.ds(j * 4 + q, 128, stride=8), :] = picked[j * 128 : (j + 1) * 128, q * 128 : (q + 1) * 128]


def step_kernel(
    flags, atmos, from_west, from_east, east, west, low, high, out, rim, main, middle, rim_middle, edge, planes, sems
):
    groups = [pl.ds(4 * g, 4) for g in range(4)]
    loads = [pltpu.make_async_copy(atmos.at[:, x], planes.at[:, x], sems.at[g]) for g, x in enumerate(groups)]
    stores = [pltpu.make_async_copy(main.at[:, x], out.at[:, x], sems.at[4 + g]) for g, x in enumerate(groups)]
    for load in loads:
        load.start()
    fill_rim(rim, 2, flags, (from_west, from_east, east, west))
    edge_lanes(rim, edge, 2)
    masks = window_masks(flags)
    for g in range(4):
        loads[g].wait()
        fill_main(main, planes, range(4 * g, 4 * g + 4), flags, low, high)
        first_stage(main, middle, edge, range(max(4 * g - 1, 0), 4 * g + 3 if g < 3 else LEV), LEV - 1, masks)
    first_rim_stage(rim, rim_middle, 2, flags)
    edge_lanes(rim_middle, edge, 2)

    def write(c, level, first, value):
        if first in masks:
            value = jnp.where(masks[first], value, 0.0)
        main[c, level, first : first + 8, :] = value

    for g in range(4):
        second_stage(middle, main, edge, range(4 * g, 4 * g + 4), LEV - 1, ALL_ROWS, write)
        stores[g].start()
    second_rim_stage(rim_middle, rim, 2, flags)
    for store in stores:
        store.wait()


def slopes(p):
    cell = iota((8, FC), 1)
    col = cell - 80 * ((cell * 52429) >> 22)
    east = jnp.where(col == 79, p, roll(p, -1, 1))
    west = jnp.where(col == 0, p, roll(p, 1, 1))
    north = jnp.where(cell >= FC - 80, p, roll(p, -80, 1))
    south = jnp.where(cell < 80, p, roll(p, 80, 1))
    gx, gy = 0.5 * (east - west), 0.5 * (north - south)
    square = 1.0 + gx * gx + gy * gy
    inverse = lax.rsqrt(square)
    return gx * inverse, gy * inverse, square * inverse


def fuel_kernel(
    rates, heats, category, burn, depth, east, rate, heat, level, slope_x, slope_y, reach, kinds, burns, depths, sems
):
    copies = [
        pltpu.make_async_copy(source, target, sems.at[i])
        for i, (source, target) in enumerate(((category, kinds), (burn, burns), (depth, depths)))
    ]
    for copy in copies:
        copy.start()
    for copy in copies:
        copy.wait()
    for g in range(3):
        here = slice(8 * g, 8 * g + 8)
        kind = kinds[here, :]
        rate_cell = jnp.zeros(kind.shape, F32)
        heat_cell = jnp.zeros(kind.shape, F32)
        for k in range(13):
            match = kind == k
            rate_cell = jnp.where(match, rates[k], rate_cell)
            heat_cell = jnp.where(match, heats[k], heat_cell)
        p = jnp.where(burns[here, :] == 1, -depths[here, :], depths[here, :])
        along_x, along_y, stretch = slopes(p)
        rate[here, :] = rate_cell
        heat[here, :] = heat_cell
        level[here, :] = p
        slope_x[here, :] = along_x
        slope_y[here, :] = along_y
        reach[here, :] = rate_cell * stretch


def fire_kernel(
    received, plan, sends, live, rate, heat, level, slope_x, slope_y, reach, rim,
    out, out_level, wind, released, spread, sent, new_level, sems,
):
    cell = iota((1, FC), 1)
    fire_row = (cell * 52429) >> 22
    fire_col = cell - 80 * fire_row
    coarse = ((fire_row * 13108) >> 16) * 16 + ((fire_col * 13108) >> 16)
    spread[...] = (iota((128, FC), 0) == coarse).astype(F32).astype(BF16)
    rows = [[received[pl.ds(j * 4 + q, 128, stride=8), :] for q in range(4)] for j in range(2)]
    table = jnp.concatenate([jnp.concatenate(r, axis=1) for r in rows], axis=0)
    winds = pick(plan[...], table)
    winds = [winds[0:SLOTS, q * 128 : (q + 1) * 128] for q in range(4)]
    wind[...] = pick_right(jnp.concatenate(winds, axis=0), spread[...], dot)

    for g in range(3):
        here = slice(8 * g, 8 * g + 8)
        alive = live[here, 0:1] > 0.0
        p = level[here, :]
        tanh_p = jnp.tanh(p)
        along_x, along_y, far = slope_x[here, :], slope_y[here, :], reach[here, :]
        for t in range(2):
            if t:
                along_x, along_y, stretch = slopes(p)
                far = rate[here, :] * stretch
            u = wind[t * 48 + 8 * g : t * 48 + 8 * g + 8, :]
            v = wind[t * 48 + 24 + 8 * g : t * 48 + 32 + 8 * g, :]
            along = u * along_x + v * along_y
            softplus = jnp.maximum(along, 0.0) + jnp.log(1.0 + jnp.exp(-jnp.abs(along)))
            p = jnp.where(alive, p - far * (1.0 + softplus), p)
            tanh_new = jnp.tanh(p)
            released[t * 24 + 8 * g : t * 24 + 8 * g + 8, :] = heat[here, :] * (tanh_p - tanh_new)
            tanh_p = tanh_new
        new_level[here, :] = p
    level_copy = pltpu.make_async_copy(new_level, out_level, sems.at[0])
    level_copy.start()
    sums = 0.02 * pick_right(released[...], spread[...], dot_rows)

    heats = jnp.concatenate([sums[0:SLOTS], sums[SLOTS:]], axis=1)
    gap = jnp.zeros((8, 256), F32)
    heats = jnp.concatenate([heats, gap, heats, gap, jnp.zeros((64, 256), F32)], axis=0)
    blocks = pick(sends[...], heats)
    lane = iota((128, 128), 1)
    group, spot = lane // 16, lane % 16
    for j in range(2):
        first = blocks[j * 128 : (j + 1) * 128, 0:128]
        sent[pl.ds(j, 128, stride=6), :] = first
        sent[pl.ds(2 + j, 128, stride=6), :] = blocks[j * 128 : (j + 1) * 128, 128:256]
        north, south = roll(first, -16, 0), roll(first, 16, 0)
        west, east = roll(first, 1, 0), roll(first, -1, 0)
        west_corner, east_corner = roll(west, 41, 1), roll(east, 57, 1)
        strip = jnp.where(group < 2, north, jnp.where(group >= 6, south, 0.0))
        middle_rows = (group >= 2) & (group < 6)
        strip = jnp.where(middle_rows & (spot >= 14), west, strip)
        strip = jnp.where(middle_rows & ((spot == 12) | (spot == 13)), roll(west, 62, 1), strip)
        strip = jnp.where(middle_rows & (spot < 2), east, strip)
        strip = jnp.where(middle_rows & ((spot == 2) | (spot == 3)), roll(east, 66, 1), strip)
        strip = jnp.where(lane == 40, roll(west_corner, 16, 0), strip)
        strip = jnp.where(lane == 41, roll(east_corner, 16, 0), strip)
        strip = jnp.where(lane == 56, roll(west_corner, -16, 0), strip)
        strip = jnp.where(lane == 57, roll(east_corner, -16, 0), strip)
        sent[pl.ds(4 + j, 128, stride=6), :] = strip
    copy = pltpu.make_async_copy(sent, out, sems.at[1])
    copy.start()
    copy.wait()
    level_copy.wait()


def heat_fields(received, home_plan, strip_plan):
    rows = [received[pl.ds(q, 128, stride=6), :] for q in range(6)]
    table = jnp.concatenate(
        [jnp.concatenate([rows[0], rows[2]], axis=1), jnp.concatenate([rows[1], rows[3]], axis=1)], axis=0
    )
    home = pick(home_plan[...], table)
    strips = pick(strip_plan[...], jnp.concatenate(rows[4:6], axis=0))
    lane8 = iota((8, 128), 1)
    blocks = jnp.concatenate(
        [
            jnp.where(lane8 >= 96, strips[0:8], 0.0),
            home[:, 0:128],
            jnp.where(lane8 < 32, strips[8:16], 0.0),
        ],
        axis=0,
    )
    first, second = swap_blocks(blocks), swap_blocks(home[:, 128:256])

    lane, row = iota((80, 128), 1), iota((80, 128), 0)
    group, spot, y = lane // 16, lane % 16, row % 8
    straight = (y >= 2) & (y < 6)
    corner = (row == 7) | (row == 72)
    wanted_group = jnp.where(y < 2, y + 4, jnp.where(y > 5, y - 4, y))
    wanted_group = jnp.where(row == 7, 2, jnp.where(row == 72, 3, wanted_group))
    fits = group == wanted_group
    west_spot = spot - jnp.where(corner, 8, jnp.where(straight, 14, 12))
    east_spot = spot - jnp.where(corner, 9, jnp.where(straight, 0, 2))
    width = jnp.where(corner, 1, 2)
    west_fits = fits & (west_spot >= 0) & (west_spot < width)
    east_fits = fits & (east_spot >= 0) & (east_spot < width)
    value = jnp.where(west_fits, strips[16:96], 0.0) + jnp.where(east_fits, strips[96:176], 0.0)
    for shift in (64, 32, 16):
        value = value + roll(value, shift, 1)
    to_west = jnp.where(corner, roll(value, 3, 1), jnp.where(straight, roll(value, -4, 1), roll(value, -2, 1)))
    to_east = jnp.where(corner, roll(value, -6, 1), jnp.where(straight, roll(value, 3, 1), roll(value, 1, 1)))
    rim = jnp.where((lane == 11) | ((lane == 10) & ~corner), to_west, 0.0)
    rim = jnp.where((lane == 3) | ((lane == 4) & ~corner), to_east, rim)
    rim = jnp.where((lane == 12) | (lane == 13), roll(first, 12, 1), rim)
    rim = jnp.where((lane == 1) | (lane == 2), roll(first, 3, 1), rim)
    return first, second, rim


def upper_kernel(flags, main_in, rim, fire_level, out, kept, main, middle, rim_middle, edge, result, sems):
    groups = [(1, 4), (5, 4), (9, 4), (13, 3)]
    loads = [
        pltpu.make_async_copy(main_in.at[:, pl.ds(*x)], main.at[:, pl.ds(*x)], sems.at[g])
        for g, x in enumerate(groups)
    ]
    for load in loads:
        load.start()
    edge_lanes(rim, edge, 2)
    masks = window_masks(flags)
    for g, (first, count) in enumerate(groups):
        loads[g].wait()
        end = first + count - 1 if g < 3 else LEV
        first_stage(main, middle, edge, range(max(first - 1, 2), end), LEV - 1, masks)
    first_rim_stage(rim, rim_middle, 2, flags)
    edge_lanes(rim_middle, edge, 2)
    kept[...] = middle[:, 2:4]

    def write(c, level, first, value):
        result[c, level - 3, first - TOP : first - TOP + 8, :] = value

    stores = []
    for g, (first, count) in enumerate(((3, 4), (7, 4), (11, 5))):
        second_stage(middle, main, edge, range(first, first + count), LEV - 1, BODY, write)
        part = result.at[:, pl.ds(first - 3, count)]
        stores.append(pltpu.make_async_copy(part, out.at[:, pl.ds(first, count)], sems.at[4 + g]))
        stores[g].start()
    for store in stores:
        store.wait()


def lower_kernel(
    flags, received, home_plan, strip_plan, main_in, rim_in, kept, upper, out, main, middle, rim, rim_middle, edge,
    result, sems,
):
    copy = pltpu.make_async_copy(main_in.at[:, pl.ds(0, 3)], main, sems.at[0])
    copy.start()
    rim[:, 0] = rim_in[:, 0]
    middle[:, 2:4] = kept[...]
    first, second, rim_heat = heat_fields(received, home_plan, strip_plan)
    copy.wait()
    main[2, 0, 4:84, :] = main[2, 0, 4:84, :] + first
    rim[2, 0, 4:84, :] = rim[2, 0, 4:84, :] + rim_heat
    edge_lanes(rim, edge, 1)
    first_stage(main, middle, edge, range(2), 2, window_masks(flags))
    first_rim_stage(rim, rim_middle, 1, flags)
    edge_lanes(rim_middle, edge, 1)

    def write(c, level, row, value):
        if c == 2 and level == 0:
            value = value + second[row - TOP : row - TOP + 8]
        result[c, level, row - TOP : row - TOP + 8, :] = value

    stores = []
    for level in (2, 1, 0):
        second_stage(middle, main, edge, (level,), 3, BODY, write)
        stores.append(pltpu.make_async_copy(result.at[:, level], out.at[:, level], sems.at[1 + level]))
        stores[-1].start()
    for store in stores:
        store.wait()


SMEM = pl.BlockSpec(memory_space=pltpu.SMEM)
VMEM = pl.BlockSpec(memory_space=pltpu.VMEM)
HBM = pl.BlockSpec(memory_space=pltpu.HBM)
ANY = pl.BlockSpec(memory_space=pl.ANY)


def shape(*dims, dtype=F32):
    return jax.ShapeDtypeStruct(dims, dtype)


def hbm(*dims):
    return pltpu.HBM(dims, F32)


def in_hbm(x):
    return pltpu.with_memory_space_constraint(x, pltpu.HBM)


def call(kernel, name, out_shape, in_specs, scratch=(), out_specs=None, flops=0, moved=0, mib=16, aliases=None):
    return pl.pallas_call(
        kernel,
        out_shape=out_shape,
        in_specs=in_specs,
        out_specs=jax.tree.map(lambda _: VMEM, out_shape) if out_specs is None else out_specs,
        scratch_shapes=list(scratch),
        input_output_aliases=aliases or {},
        compiler_params=pltpu.CompilerParams(vmem_limit_bytes=mib << 20),
        cost_estimate=pl.CostEstimate(flops=flops, bytes_accessed=moved, transcendentals=0),
        name=name,
    )


def both_ways(to_next, to_previous, axis):
    size = lax.axis_size(axis)
    ahead = [(i, (i + 1) % size) for i in range(size)]
    return (
        lax.ppermute(to_next, axis, ahead),
        lax.ppermute(to_previous, axis, [(j, i) for i, j in ahead]),
    )


def exchange(x):
    return lax.all_to_all(x.reshape(-1), AXES, 0, 0, tiled=True).reshape(x.shape)


def main_buffer(levels):
    return pltpu.VMEM((3, levels, ROWS, 128), F32)


def rim_buffer(halves):
    return pltpu.VMEM((3, halves, ROWS, 128), F32)


def copy_sems(n):
    return pltpu.SemaphoreType.DMA((n,))


def on_device(atmos, slot_tile, fuel_cat, front_burn, front_depth, fuel_rate, fuel_heat):
    ty, tx = lax.axis_index("ty"), lax.axis_index("tx")
    flags = jnp.stack([ty * NTX + tx, ty, tx]).astype(jnp.int32)
    tiles = jnp.pad(slot_tile.reshape(DEVICES, SLOTS).T, ((0, 8), (0, 0)), constant_values=-1)
    atmos = in_hbm(atmos)

    rows = shape(24, 8, 128)
    eight = pltpu.VMEM((3, LEV, 8, 128), F32)
    up, down = call(pack_rows, "pack_rows", (rows, rows), [HBM], [eight, eight, copy_sems(2)], mib=8)(atmos)
    low, high = both_ways(up, down, "ty")
    body = shape(2, AY, 128)
    east_rows, west_rows, surface, blocks = call(
        pack_columns, "pack_columns", (body, body, shape(3, 3, AY, 128), shape(64, 256)), [HBM], [pltpu.VMEM((3, LEV, AY, 128), F32), copy_sems(2)],
        flops=4_000_000, moved=1_800_000, mib=8,
    )(atmos)
    columns = shape(2, AY + 8, 128)
    east, west = call(join_columns, "join_columns", (columns, columns), [VMEM] * 4, mib=8)(
        east_rows, west_rows, low, high
    )
    from_west, from_east = both_ways(east, west, "tx")
    halo = (from_west, from_east, east, west, low, high)

    cells = shape(SLOTS, FC)
    fuel = call(
        fuel_kernel,
        "fuel",
        (cells,) * 6,
        [SMEM, SMEM, HBM, HBM, HBM, ANY],
        [pltpu.VMEM((SLOTS, FC), jnp.int32)] * 2 + [pltpu.VMEM((SLOTS, FC), F32), copy_sems(3)],
        flops=8_000_000,
        moved=2_800_000,
    )(fuel_rate, fuel_heat, in_hbm(fuel_cat), in_hbm(front_burn), in_hbm(front_depth), east)
    wind_plan, fire_plan, fire_sends, alive, home_plan, strip_plan = call(
        plan_kernel,
        "plan",
        (
            shape(256, 256, dtype=BF16),
            shape(32, 256, dtype=BF16),
            shape(256, 128, dtype=BF16),
            shape(32, 128),
            shape(64, 256, dtype=BF16),
            shape(176, 256, dtype=BF16),
        ),
        [SMEM, VMEM],
        flops=4_000_000,
        moved=400_000,
        mib=8,
    )(flags, tiles)
    winds = call(
        wind_kernel,
        "wind",
        shape(DEVICES * 8, 128),
        [SMEM] + [VMEM] * 9 + [ANY],
        [main_buffer(3), main_buffer(3), rim_buffer(1), rim_buffer(1), rim_buffer(1)],
        flops=10_000_000,
        moved=2_000_000,
        mib=8,
    )(flags, surface, blocks, *halo, wind_plan, fuel[0])
    got_winds = exchange(winds)

    main, rim = call(
        step_kernel,
        "step",
        (hbm(3, LEV, ROWS, 128), shape(3, 2, ROWS, 128)),
        [SMEM, HBM] + [VMEM] * 6,
        [main_buffer(LEV), main_buffer(LEV), rim_buffer(2), rim_buffer(2)]
        + [pltpu.VMEM((3, LEV, AY, 128), F32), copy_sems(8)],
        (HBM, VMEM),
        flops=40_000_000,
        moved=8_000_000,
        mib=12,
    )(flags, atmos, *halo)

    heats, fire_level = call(
        fire_kernel,
        "fire",
        (hbm(DEVICES * 6, 128), hbm(SLOTS, FC)),
        [VMEM] * 10 + [ANY],
        [
            pltpu.VMEM((4 * SLOTS, FC), F32),
            pltpu.VMEM((2 * SLOTS, FC), F32),
            pltpu.VMEM((128, FC), BF16),
            pltpu.VMEM((DEVICES * 6, 128), F32),
            pltpu.VMEM((SLOTS, FC), F32),
            copy_sems(2),
        ],
        (HBM, HBM),
        flops=40_000_000,
        moved=4_000_000,
    )(got_winds, fire_plan, fire_sends, alive, *fuel, rim)
    got_heats = exchange(heats)

    upper, kept = call(
        upper_kernel,
        "upper",
        (hbm(3, LEV, AY, 128), shape(3, 2, ROWS, 128)),
        [SMEM, HBM, VMEM, HBM],
        [main_buffer(LEV), main_buffer(LEV), rim_buffer(2), rim_buffer(2)]
        + [pltpu.VMEM((3, LEV - 3, AY, 128), F32), copy_sems(7)],
        (HBM, VMEM),
        flops=40_000_000,
        moved=8_000_000,
        mib=12,
    )(flags, in_hbm(main), rim, in_hbm(fire_level))
    atmos_out = call(
        lower_kernel,
        "lower",
        hbm(3, LEV, AY, 128),
        [SMEM] + [VMEM] * 3 + [HBM] + [VMEM] * 2 + [HBM],
        [
            main_buffer(3),
            main_buffer(4),
            rim_buffer(1),
            rim_buffer(1),
            rim_buffer(1),
            pltpu.VMEM((3, 3, AY, 128), F32),
            copy_sems(4),
        ],
        HBM,
        flops=10_000_000,
        moved=2_000_000,
        mib=12,
        aliases={7: 0},
    )(flags, got_heats, home_plan, strip_plan, in_hbm(main), rim, kept, in_hbm(upper))
    return atmos_out, fire_level


def solution(mesh):
    in_specs = (
        P(None, None, "ty", "tx"),
        P(),
        P(("ty", "tx"), None),
        P(("ty", "tx"), None),
        P(("ty", "tx"), None),
        P(),
        P(),
    )
    out_specs = (P(None, None, "ty", "tx"), P(("ty", "tx"), None))
    return jax.shard_map(
        on_device, mesh=mesh, in_specs=in_specs, out_specs=out_specs, check_vma=False
    )
```

```python
import jax
import jax.numpy as jnp
from jax import lax
from jax.experimental import pallas as pl
from jax.experimental.pallas import tpu as pltpu
from jax.sharding import PartitionSpec as P

AXES = ("ty", "tx")
NTY, NTX, DEVICES = 8, 16, 128
LEV, AY, AX = 16, 64, 128
SLOTS, FC = 24, 3200
ROWS = 88
TOP = 12
F32, BF16 = jnp.float32, jnp.bfloat16


def roll(x, shift, axis):
    size = x.shape[axis]
    return pltpu.roll(x, shift % size, axis) if shift % size else x


def place():
    ty, tx = lax.axis_index("ty"), lax.axis_index("tx")
    return ty * NTX + tx, ty, tx


def iota(shape, dim):
    return lax.broadcasted_iota(jnp.int32, shape, dim)


def parts(x):
    high = x.astype(BF16)
    rest = x - high.astype(F32)
    middle = rest.astype(BF16)
    low = (rest - middle.astype(F32)).astype(BF16)
    return high, middle, low


def dot(a, b):
    return jnp.dot(a, b, preferred_element_type=F32)


def dot_rows(a, b):
    return lax.dot_general(a, b, (((1,), (1,)), ((), ())), preferred_element_type=F32)


def pick(onehot, x):
    high, middle, _ = parts(x)
    return dot(onehot, high) + dot(onehot, middle)


def swap_blocks(x):
    x = x.reshape(x.shape[0] // 8, 8, 128)
    sub, group = iota(x.shape, 1), iota(x.shape, 2) // 16
    for step in (1, 2, 4):
        sub_bit, group_bit = (sub & step) != 0, (group & step) != 0
        below = roll(roll(x, -step, 1), 16 * step, 2)
        above = roll(roll(x, step, 1), -16 * step, 2)
        x = jnp.where(sub_bit == group_bit, x, jnp.where(group_bit, below, above))
    return x.reshape(x.shape[0] * 8, 128)


def pick_right(x, onehot, product):
    high, middle, _ = parts(x)
    both = product(jnp.concatenate([high, middle], axis=0), onehot)
    return both[0 : x.shape[0]] + both[x.shape[0] :]


def slot_facts(tile):
    row, col = tile >> 7, tile & 127
    owner = (row >> 3) * NTX + (col >> 3)
    local = (row & 7) * 8 + (col & 7)
    live = tile >= 0
    return jnp.where(live, owner, -1), local + 1, live


def earlier(member):
    lower = (iota((32, 32), 0) > iota((32, 32), 1)).astype(F32).astype(BF16)
    return dot(lower, member.astype(BF16))


def slots_of(owner, local, home):
    member = (owner == home).astype(F32)
    before = earlier(member)
    numbers = member * local.astype(F32)
    return [
        jnp.sum(jnp.where(before == float(j), numbers, 0.0), axis=0, keepdims=True)
        for j in (0, 1)
    ]


def pack_rows(atmos, up, down, low_rows, high_rows, sems):
    copies = [
        pltpu.make_async_copy(atmos.at[:, :, pl.ds(0, 8), :], low_rows, sems.at[0]),
        pltpu.make_async_copy(atmos.at[:, :, pl.ds(AY - 8, 8), :], high_rows, sems.at[1]),
    ]
    for copy in copies:
        copy.start()
    for copy in copies:
        copy.wait()
    for c in range(3):
        for level in range(LEV):
            plane = c * LEV + level
            where = pl.ds(4 * (plane % 2), 4)
            up[plane // 2, where, :] = high_rows[c, level, 4:8, :]
            down[plane // 2, where, :] = low_rows[c, level, 0:4, :]


def packed_columns(plane, half, rows, quarters=None):
    lane = iota((rows, 128), 1)
    group, spot = lane // 16, lane % 16
    both = [jnp.zeros((rows, 128), F32)] * 3
    for k in range(8):
        if quarters is not None and k % 4 == 0:
            quarters[2 * half + k // 4].wait()
        for c in range(3):
            both[c] = jnp.where(group == k, roll(plane(c, half * 8 + k), 16 * k + 4, 1), both[c])
    to_east = jnp.zeros((rows, 128), F32)
    to_west = jnp.zeros((rows, 128), F32)
    for c in range(3):
        inside = (spot >= 4 * c) & (spot < 4 * c + 4)
        to_east = jnp.where(inside, roll(both[c], 4 * c, 1), to_east)
        to_west = jnp.where(inside, roll(both[c], 4 * c - 4, 1), to_west)
    return to_east, to_west


def pack_columns(atmos, east, west, surface, blocks, planes, sems):
    quarters = [
        pltpu.make_async_copy(atmos.at[:, pl.ds(4 * i, 4)], planes.at[:, pl.ds(4 * i, 4)], sems.at[i])
        for i in range(4)
    ]
    for copy in quarters:
        copy.start()
    for half in range(2):
        east[half], west[half] = packed_columns(lambda c, level: planes[c, level], half, AY, quarters)
        if half == 0:
            surface[...] = planes[:, 0:3]
            blocks[...] = jnp.concatenate([swap_blocks(planes[c, 0]) for c in range(2)], axis=1)


def join_columns(east_rows, west_rows, low, high, east, west):
    def plane(c, level):
        piece = c * LEV + level
        where = slice(4 * (piece % 2), 4 * (piece % 2) + 4)
        return jnp.concatenate([low[piece // 2, where, :], high[piece // 2, where, :]], axis=0)

    for half in range(2):
        east[half, 0:AY, :] = east_rows[half]
        west[half, 0:AY, :] = west_rows[half]
        east[half, AY : AY + 8, :], west[half, AY : AY + 8, :] = packed_columns(plane, half, 8)


def rim_of(c, from_west, from_east, east, west):
    spot = iota(east.shape, 1) % 16
    out = jnp.where(spot < 3, roll(east, -(4 * c + 1), 1), 0.0)
    out = jnp.where((spot >= 3) & (spot < 7), roll(from_east, 3 - 4 * c, 1), out)
    out = jnp.where((spot >= 8) & (spot < 12), roll(from_west, 8 - 4 * c, 1), out)
    return jnp.where((spot >= 12) & (spot < 15), roll(west, 12 - 4 * c, 1), out)


def inside_window(first, rows, flags):
    y = iota((rows, 128), 0) + (first - TOP)
    return ((y >= 0) | (flags[1] > 0)) & ((y < AY) | (flags[1] < NTY - 1))


def rim_inside(first, rows, flags):
    spot = iota((rows, 128), 1) % 16
    east_out = (spot >= 3) & (spot < 7) & (flags[2] == NTX - 1)
    west_out = (spot >= 8) & (spot < 12) & (flags[2] == 0)
    return inside_window(first, rows, flags) & ~(east_out | west_out)


def fill_rim(rim, halves, flags, messages):
    for c in range(3):
        for half in range(halves):
            for source, first, rows in ((0, TOP, AY), (AY, 8, 4), (AY + 4, 76, 4)):
                value = rim_of(c, *(m[half, source : source + rows, :] for m in messages))
                rim[c, half, first : first + rows, :] = jnp.where(rim_inside(first, rows, flags), value, 0.0)


def fill_main(main, atmos, levels, flags, low, high):
    for c in range(3):
        for level in levels:
            piece = c * LEV + level
            where = slice(4 * (piece % 2), 4 * (piece % 2) + 4)
            main[c, level, TOP : TOP + AY, :] = atmos[c, level]
            main[c, level, 8:12, :] = jnp.where(flags[1] > 0, low[piece // 2, where, :], 0.0)
            main[c, level, 76:80, :] = jnp.where(flags[1] < NTY - 1, high[piece // 2, where, :], 0.0)


def tendency(centre, east, west, north, south, vertical):
    u, v, _ = centre
    up, vp = jnp.maximum(u, 0.0), jnp.maximum(v, 0.0)
    k_west, k_east = up + 0.25, up - u + 0.25
    k_south, k_north = vp + 0.25, vp - v + 0.25
    k_centre = k_west + k_east + k_south + k_north + 1.0
    out = []
    for c in range(3):
        out.append(
            k_west * west[c]
            + k_east * east[c]
            + k_south * south[c]
            + k_north * north[c]
            + 0.5 * vertical[c]
            - k_centre * centre[c]
        )
    out[0] = out[0] + 0.3 * v - 0.25 * (east[2] - west[2])
    out[1] = out[1] - 0.3 * u - 0.25 * (north[2] - south[2])
    return out


def edge_lanes(rim, edge, halves):
    spot = iota((72, 128), 1) % 16
    for c in range(3):
        for half in range(halves):
            x = rim[c, half, 8:80, :]
            edge[c, half, 8:80, :] = jnp.where(spot == 4, roll(x, -7, 1), x)


def main_tendency(source, edge, level, last, first, rows):
    lane = iota((rows, 128), 1)
    above, below = min(level + 1, last), max(level - 1, 0)
    here = pl.ds(first, rows)
    centre, east, west, north, south, vertical = [], [], [], [], [], []
    for c in range(3):
        x = source[c, level, here, :]
        side = roll(edge[c, level // 8, here, :], 124 - 16 * (level % 8), 1)
        centre.append(x)
        east.append(jnp.where(lane == 127, side, roll(x, -1, 1)))
        west.append(jnp.where(lane == 0, side, roll(x, 1, 1)))
        north.append(source[c, level, pl.ds(first + 1, rows), :])
        south.append(source[c, level, pl.ds(first - 1, rows), :])
        vertical.append(source[c, above, here, :] + source[c, below, here, :])
    return centre, tendency(centre, east, west, north, south, vertical)


def rim_tendency(source, halves, half, first, rows):
    lane = iota((rows, 128), 1)
    here = pl.ds(first, rows)
    centre, east, west, north, south, vertical = [], [], [], [], [], []
    for c in range(3):
        x = source[c, half, here, :]
        next_up = source[c, 1, here, :] if half == 0 and halves == 2 else x
        next_down = source[c, 0, here, :] if half == 1 else x
        above = jnp.where(lane < 112, roll(x, -16, 1), x if next_up is x else roll(next_up, -16, 1))
        below = jnp.where(lane >= 16, roll(x, 16, 1), x if next_down is x else roll(next_down, 16, 1))
        centre.append(x)
        east.append(roll(x, -1, 1))
        west.append(roll(x, 1, 1))
        north.append(source[c, half, pl.ds(first + 1, rows), :])
        south.append(source[c, half, pl.ds(first - 1, rows), :])
        vertical.append(above + below)
    return centre, tendency(centre, east, west, north, south, vertical)


CHUNKS = ((8, 24), (32, 24), (56, 24))
ALL_ROWS = tuple(range(8, 80, 8))
BODY = tuple(range(TOP, TOP + AY, 8))


def window_masks(flags):
    return {first: inside_window(first, 8, flags) for first in (8, 72)}


def first_stage(source, target, edge, levels, last, masks):
    for level in levels:
        for first in ALL_ROWS:
            centre, change = main_tendency(source, edge, level, last, first, 8)
            for c in range(3):
                value = centre[c] + 0.2 * change[c]
                if first in masks:
                    value = jnp.where(masks[first], value, 0.0)
                target[c, level, first : first + 8, :] = value


def second_stage(source, state, edge, levels, last, rows, write):
    for level in levels:
        for first in rows:
            centre, change = main_tendency(source, edge, level, last, first, 8)
            for c in range(3):
                old = state[c, level, first : first + 8, :]
                write(c, level, first, 0.5 * (old + centre[c]) + 0.1 * change[c])


def first_rim_stage(source, target, halves, flags):
    for half in range(halves):
        for first, rows in CHUNKS:
            centre, change = rim_tendency(source, halves, half, first, rows)
            for c in range(3):
                value = centre[c] + 0.2 * change[c]
                target[c, half, pl.ds(first, rows), :] = jnp.where(rim_inside(first, rows, flags), value, 0.0)


def second_rim_stage(source, state, halves, flags):
    for half in range(halves):
        for first, rows in CHUNKS:
            centre, change = rim_tendency(source, halves, half, first, rows)
            for c in range(3):
                here = pl.ds(first, rows)
                value = 0.5 * (state[c, half, here, :] + centre[c]) + 0.1 * change[c]
                state[c, half, here, :] = jnp.where(rim_inside(first, rows, flags), value, 0.0)


def plan_kernel(tiles, wind_plan, fire_plan, fire_sends, alive, home_plan, strip_plan):
    flags = place()
    me, ty, tx = flags[0], flags[1], flags[2]
    listed = tiles[...]
    owner, local, _ = slot_facts(listed)

    def numbers(dy, dx):
        ok = (ty + dy >= 0) & (ty + dy < NTY) & (tx + dx >= 0) & (tx + dx < NTX)
        return slots_of(owner, local, jnp.where(ok, me + dy * NTX + dx, -7))

    here = numbers(0, 0)
    north, south, west, east = numbers(1, 0), numbers(-1, 0), numbers(0, -1), numbers(0, 1)
    south_west, south_east = numbers(-1, -1), numbers(-1, 1)
    north_west, north_east = numbers(1, -1), numbers(1, 1)
    tile = iota((64, 128), 0).astype(F32) + 1.0
    edge_tile = iota((8, 128), 0).astype(F32) + 1.0
    row = iota((80, 128), 0)
    first_tile = ((row // 8 - 1) * 8 + 1).astype(F32)
    body = (row >= 8) & (row < 72)

    for j in range(2):
        chosen = (here[j] == tile).astype(F32)
        chosen = jnp.concatenate([chosen, chosen], axis=0).T.astype(BF16)
        wind_plan[j * 128 : (j + 1) * 128, 0:128] = chosen
        wind_plan[j * 128 : (j + 1) * 128, 128:256] = chosen
    mine = jnp.sum(
        jnp.where(iota((32, 128), 1) == me, listed.astype(F32), 0.0), axis=1, keepdims=True
    ).astype(jnp.int32)
    holder, _, live = slot_facts(mine)
    member = (holder == iota((32, 128), 1)).astype(F32)
    before = earlier(member)
    places = [jnp.where(before == float(j), member, 0.0) for j in (0, 1)]
    fire_plan[...] = jnp.concatenate(places, axis=1).astype(BF16)
    alive[...] = jnp.where(live, jnp.ones((32, 128), F32), 0.0)

    chosen = jnp.concatenate(places + [jnp.zeros((64, 128), F32)], axis=0).T
    part = iota((128, 128), 1) // 32
    for j in range(2):
        fire_sends[j * 128 : (j + 1) * 128, :] = jnp.where(part == j, chosen, 0.0).astype(BF16)
        from_south = (south[j] == edge_tile + 56.0).astype(F32)
        from_north = (north[j] == edge_tile).astype(F32)
        from_west = body & (west[j] == first_tile + 7.0)
        from_west = from_west | ((row == 7) & (south_west[j] == 64.0)) | ((row == 72) & (north_west[j] == 8.0))
        from_east = body & (east[j] == first_tile)
        from_east = from_east | ((row == 7) & (south_east[j] == 57.0)) | ((row == 72) & (north_east[j] == 1.0))
        lanes = slice(j * 128, (j + 1) * 128)
        home_plan[:, lanes] = (here[j] == tile).astype(F32).astype(BF16)
        strips = [from_south, from_north, from_west.astype(F32), from_east.astype(F32)]
        strip_plan[:, lanes] = jnp.concatenate(strips, axis=0).astype(BF16)


def wind_kernel(
    planes, blocks, from_west, from_east, east, west, low, high, plan, fuel, out, main, middle, rim, rim_middle,
    edge,
):
    flags = place()
    fill_rim(rim, 1, flags, (from_west, from_east, east, west))
    fill_main(main, planes, range(3), flags, low, high)
    edge_lanes(rim, edge, 1)
    first_stage(main, middle, edge, range(2), 2, window_masks(flags))
    first_rim_stage(rim, rim_middle, 1, flags)
    edge_lanes(rim_middle, edge, 1)
    later = [[], []]
    for first in BODY:
        centre, change = main_tendency(middle, edge, 0, 2, first, 8)
        for c in range(2):
            later[c].append(0.5 * (main[c, 0, first : first + 8, :] + centre[c]) + 0.1 * change[c])
    fields = [blocks[...]] + [swap_blocks(jnp.concatenate(x, axis=0)) for x in later]
    pieces = parts(jnp.concatenate(fields, axis=1))
    pieces = jnp.concatenate(pieces + (jnp.zeros((64, 512), BF16),), axis=0)
    picked = dot(plan[...], pieces)
    for j in range(2):
        for q in range(4):
            out[pl.ds(j * 4 + q, 128, stride=8), :] = picked[j * 128 : (j + 1) * 128, q * 128 : (q + 1) * 128]


def step_kernel(
    atmos, from_west, from_east, east, west, low, high, out, rim, main, middle, rim_middle, edge, planes, sems
):
    flags = place()
    groups = [pl.ds(4 * g, 4) for g in range(4)]
    loads = [pltpu.make_async_copy(atmos.at[:, x], planes.at[:, x], sems.at[g]) for g, x in enumerate(groups)]
    stores = [pltpu.make_async_copy(main.at[:, x], out.at[:, x], sems.at[4 + g]) for g, x in enumerate(groups)]
    for load in loads:
        load.start()
    fill_rim(rim, 2, flags, (from_west, from_east, east, west))
    edge_lanes(rim, edge, 2)
    masks = window_masks(flags)
    for g in range(4):
        loads[g].wait()
        fill_main(main, planes, range(4 * g, 4 * g + 4), flags, low, high)
        first_stage(main, middle, edge, range(max(4 * g - 1, 0), 4 * g + 3 if g < 3 else LEV), LEV - 1, masks)
    first_rim_stage(rim, rim_middle, 2, flags)
    edge_lanes(rim_middle, edge, 2)

    def write(c, level, first, value):
        if first in masks:
            value = jnp.where(masks[first], value, 0.0)
        main[c, level, first : first + 8, :] = value

    for g in range(4):
        second_stage(middle, main, edge, range(4 * g, 4 * g + 4), LEV - 1, ALL_ROWS, write)
        stores[g].start()
    second_rim_stage(rim_middle, rim, 2, flags)
    for store in stores:
        store.wait()


def slopes(p):
    cell = iota((8, FC), 1)
    col = cell - 80 * ((cell * 52429) >> 22)
    east = jnp.where(col == 79, p, roll(p, -1, 1))
    west = jnp.where(col == 0, p, roll(p, 1, 1))
    north = jnp.where(cell >= FC - 80, p, roll(p, -80, 1))
    south = jnp.where(cell < 80, p, roll(p, 80, 1))
    gx, gy = 0.5 * (east - west), 0.5 * (north - south)
    square = 1.0 + gx * gx + gy * gy
    inverse = lax.rsqrt(square)
    return gx * inverse, gy * inverse, square * inverse


def fuel_kernel(
    rates, heats, category, burn, depth, east, rate, heat, level, slope_x, slope_y, reach, kinds, burns, depths, sems
):
    copies = [
        pltpu.make_async_copy(source, target, sems.at[i])
        for i, (source, target) in enumerate(((category, kinds), (burn, burns), (depth, depths)))
    ]
    for copy in copies:
        copy.start()
    for copy in copies:
        copy.wait()
    for g in range(3):
        here = slice(8 * g, 8 * g + 8)
        kind = kinds[here, :]
        rate_cell = jnp.zeros(kind.shape, F32)
        heat_cell = jnp.zeros(kind.shape, F32)
        for k in range(13):
            match = kind == k
            rate_cell = jnp.where(match, rates[k], rate_cell)
            heat_cell = jnp.where(match, heats[k], heat_cell)
        p = jnp.where(burns[here, :] == 1, -depths[here, :], depths[here, :])
        along_x, along_y, stretch = slopes(p)
        rate[here, :] = rate_cell
        heat[here, :] = heat_cell
        level[here, :] = p
        slope_x[here, :] = along_x
        slope_y[here, :] = along_y
        reach[here, :] = rate_cell * stretch


def fire_kernel(
    received, plan, sends, live, rate, heat, level, slope_x, slope_y, reach, rim,
    out, out_level, wind, released, spread, sent, new_level, sems,
):
    cell = iota((1, FC), 1)
    fire_row = (cell * 52429) >> 22
    fire_col = cell - 80 * fire_row
    coarse = ((fire_row * 13108) >> 16) * 16 + ((fire_col * 13108) >> 16)
    spread[...] = (iota((128, FC), 0) == coarse).astype(F32).astype(BF16)
    rows = [[received[pl.ds(j * 4 + q, 128, stride=8), :] for q in range(4)] for j in range(2)]
    table = jnp.concatenate([jnp.concatenate(r, axis=1) for r in rows], axis=0)
    winds = pick(plan[...], table)
    winds = [winds[0:SLOTS, q * 128 : (q + 1) * 128] for q in range(4)]
    wind[...] = pick_right(jnp.concatenate(winds, axis=0), spread[...], dot)

    for g in range(3):
        here = slice(8 * g, 8 * g + 8)
        alive = live[here, 0:1] > 0.0
        p = level[here, :]
        tanh_p = jnp.tanh(p)
        along_x, along_y, far = slope_x[here, :], slope_y[here, :], reach[here, :]
        for t in range(2):
            if t:
                along_x, along_y, stretch = slopes(p)
                far = rate[here, :] * stretch
            u = wind[t * 48 + 8 * g : t * 48 + 8 * g + 8, :]
            v = wind[t * 48 + 24 + 8 * g : t * 48 + 32 + 8 * g, :]
            along = u * along_x + v * along_y
            softplus = jnp.maximum(along, 0.0) + jnp.log(1.0 + jnp.exp(-jnp.abs(along)))
            p = jnp.where(alive, p - far * (1.0 + softplus), p)
            tanh_new = jnp.tanh(p)
            released[t * 24 + 8 * g : t * 24 + 8 * g + 8, :] = heat[here, :] * (tanh_p - tanh_new)
            tanh_p = tanh_new
        new_level[here, :] = p
    level_copy = pltpu.make_async_copy(new_level, out_level, sems.at[0])
    level_copy.start()
    sums = 0.02 * pick_right(released[...], spread[...], dot_rows)

    heats = jnp.concatenate([sums[0:SLOTS], sums[SLOTS:]], axis=1)
    gap = jnp.zeros((8, 256), F32)
    heats = jnp.concatenate([heats, gap, heats, gap, jnp.zeros((64, 256), F32)], axis=0)
    blocks = pick(sends[...], heats)
    lane = iota((128, 128), 1)
    group, spot = lane // 16, lane % 16
    for j in range(2):
        first = blocks[j * 128 : (j + 1) * 128, 0:128]
        sent[pl.ds(j, 128, stride=6), :] = first
        sent[pl.ds(2 + j, 128, stride=6), :] = blocks[j * 128 : (j + 1) * 128, 128:256]
        north, south = roll(first, -16, 0), roll(first, 16, 0)
        west, east = roll(first, 1, 0), roll(first, -1, 0)
        west_corner, east_corner = roll(west, 41, 1), roll(east, 57, 1)
        strip = jnp.where(group < 2, north, jnp.where(group >= 6, south, 0.0))
        middle_rows = (group >= 2) & (group < 6)
        strip = jnp.where(middle_rows & (spot >= 14), west, strip)
        strip = jnp.where(middle_rows & ((spot == 12) | (spot == 13)), roll(west, 62, 1), strip)
        strip = jnp.where(middle_rows & (spot < 2), east, strip)
        strip = jnp.where(middle_rows & ((spot == 2) | (spot == 3)), roll(east, 66, 1), strip)
        strip = jnp.where(lane == 40, roll(west_corner, 16, 0), strip)
        strip = jnp.where(lane == 41, roll(east_corner, 16, 0), strip)
        strip = jnp.where(lane == 56, roll(west_corner, -16, 0), strip)
        strip = jnp.where(lane == 57, roll(east_corner, -16, 0), strip)
        sent[pl.ds(4 + j, 128, stride=6), :] = strip
    copy = pltpu.make_async_copy(sent, out, sems.at[1])
    copy.start()
    copy.wait()
    level_copy.wait()


def heat_fields(received, home_plan, strip_plan):
    rows = [received[pl.ds(q, 128, stride=6), :] for q in range(6)]
    table = jnp.concatenate(
        [jnp.concatenate([rows[0], rows[2]], axis=1), jnp.concatenate([rows[1], rows[3]], axis=1)], axis=0
    )
    home = pick(home_plan[...], table)
    strips = pick(strip_plan[...], jnp.concatenate(rows[4:6], axis=0))
    lane8 = iota((8, 128), 1)
    blocks = jnp.concatenate(
        [
            jnp.where(lane8 >= 96, strips[0:8], 0.0),
            home[:, 0:128],
            jnp.where(lane8 < 32, strips[8:16], 0.0),
        ],
        axis=0,
    )
    first, second = swap_blocks(blocks), swap_blocks(home[:, 128:256])

    lane, row = iota((80, 128), 1), iota((80, 128), 0)
    group, spot, y = lane // 16, lane % 16, row % 8
    straight = (y >= 2) & (y < 6)
    corner = (row == 7) | (row == 72)
    wanted_group = jnp.where(y < 2, y + 4, jnp.where(y > 5, y - 4, y))
    wanted_group = jnp.where(row == 7, 2, jnp.where(row == 72, 3, wanted_group))
    fits = group == wanted_group
    west_spot = spot - jnp.where(corner, 8, jnp.where(straight, 14, 12))
    east_spot = spot - jnp.where(corner, 9, jnp.where(straight, 0, 2))
    width = jnp.where(corner, 1, 2)
    west_fits = fits & (west_spot >= 0) & (west_spot < width)
    east_fits = fits & (east_spot >= 0) & (east_spot < width)
    value = jnp.where(west_fits, strips[16:96], 0.0) + jnp.where(east_fits, strips[96:176], 0.0)
    for shift in (64, 32, 16):
        value = value + roll(value, shift, 1)
    to_west = jnp.where(corner, roll(value, 3, 1), jnp.where(straight, roll(value, -4, 1), roll(value, -2, 1)))
    to_east = jnp.where(corner, roll(value, -6, 1), jnp.where(straight, roll(value, 3, 1), roll(value, 1, 1)))
    rim = jnp.where((lane == 11) | ((lane == 10) & ~corner), to_west, 0.0)
    rim = jnp.where((lane == 3) | ((lane == 4) & ~corner), to_east, rim)
    rim = jnp.where((lane == 12) | (lane == 13), roll(first, 12, 1), rim)
    rim = jnp.where((lane == 1) | (lane == 2), roll(first, 3, 1), rim)
    return first, second, rim


def upper_kernel(main_in, rim, fire_level, out, kept, bottom, main, middle, rim_middle, edge, result, sems):
    flags = place()
    groups = [(0, 5), (5, 4), (9, 4), (13, 3)]
    loads = [
        pltpu.make_async_copy(main_in.at[:, pl.ds(*x)], main.at[:, pl.ds(*x)], sems.at[g])
        for g, x in enumerate(groups)
    ]
    for load in loads:
        load.start()
    edge_lanes(rim, edge, 2)
    masks = window_masks(flags)
    for g, (first, count) in enumerate(groups):
        loads[g].wait()
        end = first + count - 1 if g < 3 else LEV
        first_stage(main, middle, edge, range(max(first - 1, 2), end), LEV - 1, masks)
    first_rim_stage(rim, rim_middle, 2, flags)
    edge_lanes(rim_middle, edge, 2)
    bottom[...] = main[:, 0:3]
    kept[...] = middle[:, 2:4]

    def write(c, level, first, value):
        result[c, level - 3, first - TOP : first - TOP + 8, :] = value

    stores = []
    for g, (first, count) in enumerate(((3, 4), (7, 4), (11, 5))):
        second_stage(middle, main, edge, range(first, first + count), LEV - 1, BODY, write)
        part = result.at[:, pl.ds(first - 3, count)]
        stores.append(pltpu.make_async_copy(part, out.at[:, pl.ds(first, count)], sems.at[4 + g]))
        stores[g].start()
    for store in stores:
        store.wait()


def lower_kernel(
    received, home_plan, strip_plan, main_in, rim_in, kept, upper, out, main, middle, rim, rim_middle, edge,
    result, sems,
):
    flags = place()
    main[...] = main_in[...]
    rim[:, 0] = rim_in[:, 0]
    middle[:, 2:4] = kept[...]
    first, second, rim_heat = heat_fields(received, home_plan, strip_plan)
    main[2, 0, 4:84, :] = main[2, 0, 4:84, :] + first
    rim[2, 0, 4:84, :] = rim[2, 0, 4:84, :] + rim_heat
    edge_lanes(rim, edge, 1)
    first_stage(main, middle, edge, range(2), 2, window_masks(flags))
    first_rim_stage(rim, rim_middle, 1, flags)
    edge_lanes(rim_middle, edge, 1)

    def write(c, level, row, value):
        if c == 2 and level == 0:
            value = value + second[row - TOP : row - TOP + 8]
        result[c, level, row - TOP : row - TOP + 8, :] = value

    stores = []
    for level in (2, 1, 0):
        second_stage(middle, main, edge, (level,), 3, BODY, write)
        stores.append(pltpu.make_async_copy(result.at[:, level], out.at[:, level], sems.at[level]))
        stores[-1].start()
    for store in stores:
        store.wait()


SMEM = pl.BlockSpec(memory_space=pltpu.SMEM)
VMEM = pl.BlockSpec(memory_space=pltpu.VMEM)
HBM = pl.BlockSpec(memory_space=pltpu.HBM)
ANY = pl.BlockSpec(memory_space=pl.ANY)


def shape(*dims, dtype=F32):
    return jax.ShapeDtypeStruct(dims, dtype)


def hbm(*dims):
    return pltpu.HBM(dims, F32)


def in_hbm(x):
    return pltpu.with_memory_space_constraint(x, pltpu.HBM)


def call(kernel, name, out_shape, in_specs, scratch=(), out_specs=None, flops=0, moved=0, mib=16, aliases=None):
    return pl.pallas_call(
        kernel,
        out_shape=out_shape,
        in_specs=in_specs,
        out_specs=jax.tree.map(lambda _: VMEM, out_shape) if out_specs is None else out_specs,
        scratch_shapes=list(scratch),
        input_output_aliases=aliases or {},
        compiler_params=pltpu.CompilerParams(vmem_limit_bytes=mib << 20),
        cost_estimate=pl.CostEstimate(flops=flops, bytes_accessed=moved, transcendentals=0),
        name=name,
    )


def both_ways(to_next, to_previous, axis):
    size = lax.axis_size(axis)
    ahead = [(i, (i + 1) % size) for i in range(size)]
    return (
        lax.ppermute(to_next, axis, ahead),
        lax.ppermute(to_previous, axis, [(j, i) for i, j in ahead]),
    )


def exchange(x):
    return lax.all_to_all(x.reshape(-1), AXES, 0, 0, tiled=True).reshape(x.shape)


def main_buffer(levels):
    return pltpu.VMEM((3, levels, ROWS, 128), F32)


def rim_buffer(halves):
    return pltpu.VMEM((3, halves, ROWS, 128), F32)


def copy_sems(n):
    return pltpu.SemaphoreType.DMA((n,))


def on_device(atmos, slot_tile, fuel_cat, front_burn, front_depth, fuel_rate, fuel_heat):
    tiles = jnp.pad(slot_tile.reshape(DEVICES, SLOTS).T, ((0, 8), (0, 0)), constant_values=-1)
    atmos = in_hbm(atmos)

    rows = shape(24, 8, 128)
    eight = pltpu.VMEM((3, LEV, 8, 128), F32)
    up, down = call(pack_rows, "pack_rows", (rows, rows), [HBM], [eight, eight, copy_sems(2)], mib=8)(atmos)
    low, high = both_ways(up, down, "ty")
    body = shape(2, AY, 128)
    east_rows, west_rows, surface, blocks = call(
        pack_columns, "pack_columns", (body, body, shape(3, 3, AY, 128), shape(64, 256)), [HBM], [pltpu.VMEM((3, LEV, AY, 128), F32), copy_sems(4)],
        flops=4_000_000, moved=1_800_000, mib=8,
    )(atmos)
    columns = shape(2, AY + 8, 128)
    east, west = call(join_columns, "join_columns", (columns, columns), [VMEM] * 4, mib=8)(
        east_rows, west_rows, low, high
    )
    from_west, from_east = both_ways(east, west, "tx")
    halo = (from_west, from_east, east, west, low, high)

    cells = shape(SLOTS, FC)
    fuel = call(
        fuel_kernel,
        "fuel",
        (cells,) * 6,
        [SMEM, SMEM, HBM, HBM, HBM, ANY],
        [pltpu.VMEM((SLOTS, FC), jnp.int32)] * 2 + [pltpu.VMEM((SLOTS, FC), F32), copy_sems(3)],
        flops=8_000_000,
        moved=2_800_000,
    )(fuel_rate, fuel_heat, in_hbm(fuel_cat), in_hbm(front_burn), in_hbm(front_depth), east)
    wind_plan, fire_plan, fire_sends, alive, home_plan, strip_plan = call(
        plan_kernel,
        "plan",
        (
            shape(256, 256, dtype=BF16),
            shape(32, 256, dtype=BF16),
            shape(256, 128, dtype=BF16),
            shape(32, 128),
            shape(64, 256, dtype=BF16),
            shape(176, 256, dtype=BF16),
        ),
        [VMEM],
        flops=4_000_000,
        moved=400_000,
        mib=8,
    )(tiles)
    winds = call(
        wind_kernel,
        "wind",
        shape(DEVICES * 8, 128),
        [VMEM] * 9 + [ANY],
        [main_buffer(3), main_buffer(3), rim_buffer(1), rim_buffer(1), rim_buffer(1)],
        flops=10_000_000,
        moved=2_000_000,
        mib=8,
    )(surface, blocks, *halo, wind_plan, fuel[0])
    got_winds = exchange(winds)

    main, rim = call(
        step_kernel,
        "step",
        (hbm(3, LEV, ROWS, 128), shape(3, 2, ROWS, 128)),
        [HBM] + [VMEM] * 6,
        [main_buffer(LEV), main_buffer(LEV), rim_buffer(2), rim_buffer(2)]
        + [pltpu.VMEM((3, LEV, AY, 128), F32), copy_sems(8)],
        (HBM, VMEM),
        flops=40_000_000,
        moved=8_000_000,
        mib=12,
    )(atmos, *halo)

    heats, fire_level = call(
        fire_kernel,
        "fire",
        (hbm(DEVICES * 6, 128), hbm(SLOTS, FC)),
        [VMEM] * 10 + [ANY],
        [
            pltpu.VMEM((4 * SLOTS, FC), F32),
            pltpu.VMEM((2 * SLOTS, FC), F32),
            pltpu.VMEM((128, FC), BF16),
            pltpu.VMEM((DEVICES * 6, 128), F32),
            pltpu.VMEM((SLOTS, FC), F32),
            copy_sems(2),
        ],
        (HBM, HBM),
        flops=40_000_000,
        moved=4_000_000,
    )(got_winds, fire_plan, fire_sends, alive, *fuel, rim)
    got_heats = exchange(heats)

    upper, kept, bottom = call(
        upper_kernel,
        "upper",
        (hbm(3, LEV, AY, 128), shape(3, 2, ROWS, 128), shape(3, 3, ROWS, 128)),
        [HBM, VMEM, HBM],
        [main_buffer(LEV), main_buffer(LEV), rim_buffer(2), rim_buffer(2)]
        + [pltpu.VMEM((3, LEV - 3, AY, 128), F32), copy_sems(7)],
        (HBM, VMEM, VMEM),
        flops=40_000_000,
        moved=8_000_000,
        mib=12,
    )(in_hbm(main), rim, in_hbm(fire_level))
    atmos_out = call(
        lower_kernel,
        "lower",
        hbm(3, LEV, AY, 128),
        [VMEM] * 6 + [HBM],
        [
            main_buffer(3),
            main_buffer(4),
            rim_buffer(1),
            rim_buffer(1),
            rim_buffer(1),
            pltpu.VMEM((3, 3, AY, 128), F32),
            copy_sems(3),
        ],
        HBM,
        flops=10_000_000,
        moved=2_000_000,
        mib=12,
        aliases={6: 0},
    )(got_heats, home_plan, strip_plan, bottom, rim, kept, in_hbm(upper))
    return atmos_out, fire_level


def solution(mesh):
    in_specs = (
        P(None, None, "ty", "tx"),
        P(),
        P(("ty", "tx"), None),
        P(("ty", "tx"), None),
        P(("ty", "tx"), None),
        P(),
        P(),
    )
    out_specs = (P(None, None, "ty", "tx"), P(("ty", "tx"), None))
    return jax.shard_map(
        on_device, mesh=mesh, in_specs=in_specs, out_specs=out_specs, check_vma=False
    )
```

```python
import jax
import jax.numpy as jnp
import numpy as np
from jax import lax
from jax.experimental import pallas as pl
from jax.experimental.pallas import tpu as pltpu
from jax.sharding import PartitionSpec as P

AXES = ("ty", "tx")
NTY, NTX, DEVICES = 8, 16, 128
LEV, AY, AX = 16, 64, 128
SLOTS, FC = 24, 3200
ROWS = 88
TOP = 12
F32, BF16 = jnp.float32, jnp.bfloat16


def roll(x, shift, axis):
    size = x.shape[axis]
    return pltpu.roll(x, shift % size, axis) if shift % size else x


def place():
    ty, tx = lax.axis_index("ty"), lax.axis_index("tx")
    return ty * NTX + tx, ty, tx


def iota(shape, dim):
    return lax.broadcasted_iota(jnp.int32, shape, dim)


def parts(x):
    high = x.astype(BF16)
    rest = x - high.astype(F32)
    middle = rest.astype(BF16)
    low = (rest - middle.astype(F32)).astype(BF16)
    return high, middle, low


def dot(a, b):
    return jnp.dot(a, b, preferred_element_type=F32)


def pick(onehot, x):
    high, middle, _ = parts(x)
    return dot(onehot, high) + dot(onehot, middle)


def swap_blocks(x):
    x = x.reshape(x.shape[0] // 8, 8, 128)
    sub, group = iota(x.shape, 1), iota(x.shape, 2) // 16
    for step in (1, 2, 4):
        sub_bit, group_bit = (sub & step) != 0, (group & step) != 0
        below = roll(roll(x, -step, 1), 16 * step, 2)
        above = roll(roll(x, step, 1), -16 * step, 2)
        x = jnp.where(sub_bit == group_bit, x, jnp.where(group_bit, below, above))
    return x.reshape(x.shape[0] * 8, 128)


def pick_right(x, onehot, product):
    high, middle, _ = parts(x)
    both = product(jnp.concatenate([high, middle], axis=0), onehot)
    return both[0 : x.shape[0]] + both[x.shape[0] :]


def slot_facts(tile):
    row, col = tile >> 7, tile & 127
    owner = (row >> 3) * NTX + (col >> 3)
    local = (row & 7) * 8 + (col & 7)
    live = tile >= 0
    return jnp.where(live, owner, -1), local + 1, live


def earlier(member):
    lower = (iota((32, 32), 0) > iota((32, 32), 1)).astype(F32).astype(BF16)
    return dot(lower, member.astype(BF16))


def slots_of(owner, local, home):
    member = (owner == home).astype(F32)
    before = earlier(member)
    numbers = member * local.astype(F32)
    return [
        jnp.sum(jnp.where(before == float(j), numbers, 0.0), axis=0, keepdims=True)
        for j in (0, 1)
    ]


def pack_rows(atmos, up, down, low_rows, high_rows, sems):
    copies = [
        pltpu.make_async_copy(atmos.at[:, :, pl.ds(0, 8), :], low_rows, sems.at[0]),
        pltpu.make_async_copy(atmos.at[:, :, pl.ds(AY - 8, 8), :], high_rows, sems.at[1]),
    ]
    for copy in copies:
        copy.start()
    for copy in copies:
        copy.wait()
    for c in range(3):
        for level in range(LEV):
            plane = c * LEV + level
            where = pl.ds(4 * (plane % 2), 4)
            up[plane // 2, where, :] = high_rows[c, level, 4:8, :]
            down[plane // 2, where, :] = low_rows[c, level, 0:4, :]


def packed_columns(plane, half, rows, quarters=None):
    lane = iota((rows, 128), 1)
    group, spot = lane // 16, lane % 16
    both = [jnp.zeros((rows, 128), F32)] * 3
    for k in range(8):
        if quarters is not None and k % 4 == 0:
            quarters[2 * half + k // 4].wait()
        for c in range(3):
            both[c] = jnp.where(group == k, roll(plane(c, half * 8 + k), 16 * k + 4, 1), both[c])
    to_east = jnp.zeros((rows, 128), F32)
    to_west = jnp.zeros((rows, 128), F32)
    for c in range(3):
        inside = (spot >= 4 * c) & (spot < 4 * c + 4)
        to_east = jnp.where(inside, roll(both[c], 4 * c, 1), to_east)
        to_west = jnp.where(inside, roll(both[c], 4 * c - 4, 1), to_west)
    return to_east, to_west


def pack_columns(atmos, east, west, surface, blocks, planes, sems):
    quarters = [
        pltpu.make_async_copy(atmos.at[:, pl.ds(4 * i, 4)], planes.at[:, pl.ds(4 * i, 4)], sems.at[i])
        for i in range(4)
    ]
    for copy in quarters:
        copy.start()
    for half in range(2):
        east[half], west[half] = packed_columns(lambda c, level: planes[c, level], half, AY, quarters)
        if half == 0:
            surface[...] = planes[:, 0:3]
            blocks[...] = jnp.concatenate([swap_blocks(planes[c, 0]) for c in range(2)], axis=1)


def join_columns(east_rows, west_rows, low, high, east, west):
    def plane(c, level):
        piece = c * LEV + level
        where = slice(4 * (piece % 2), 4 * (piece % 2) + 4)
        return jnp.concatenate([low[piece // 2, where, :], high[piece // 2, where, :]], axis=0)

    for half in range(2):
        east[half, 0:AY, :] = east_rows[half]
        west[half, 0:AY, :] = west_rows[half]
        east[half, AY : AY + 8, :], west[half, AY : AY + 8, :] = packed_columns(plane, half, 8)


def rim_of(c, from_west, from_east, east, west):
    spot = iota(east.shape, 1) % 16
    out = jnp.where(spot < 4, roll(east, -4 * c, 1), roll(from_east, 4 - 4 * c, 1))
    out = jnp.where(spot < 8, out, roll(from_west, 8 - 4 * c, 1))
    return jnp.where(spot < 12, out, roll(west, 12 - 4 * c, 1))


def inside_window(first, rows, flags):
    y = iota((rows, 128), 0) + (first - TOP)
    return ((y >= 0) | (flags[1] > 0)) & ((y < AY) | (flags[1] < NTY - 1))


def rim_inside(first, rows, flags):
    spot = iota((rows, 128), 1) % 16
    east_out = (spot >= 4) & (spot < 8) & (flags[2] == NTX - 1)
    west_out = (spot >= 8) & (spot < 12) & (flags[2] == 0)
    return inside_window(first, rows, flags) & ~(east_out | west_out)


def fill_rim(rim, halves, flags, messages):
    for c in range(3):
        for half in range(halves):
            for source, first, rows in ((0, TOP, AY), (AY, 8, 4), (AY + 4, 76, 4)):
                value = rim_of(c, *(m[half, source : source + rows, :] for m in messages))
                rim[c, half, first : first + rows, :] = jnp.where(rim_inside(first, rows, flags), value, 0.0)


def fill_main(main, atmos, levels, flags, low, high):
    for c in range(3):
        for level in levels:
            piece = c * LEV + level
            where = slice(4 * (piece % 2), 4 * (piece % 2) + 4)
            main[c, level, TOP : TOP + AY, :] = atmos[c, level]
            main[c, level, 8:12, :] = jnp.where(flags[1] > 0, low[piece // 2, where, :], 0.0)
            main[c, level, 76:80, :] = jnp.where(flags[1] < NTY - 1, high[piece // 2, where, :], 0.0)


def tendency(centre, east, west, north, south, vertical):
    u, v, _ = centre
    up, vp = jnp.maximum(u, 0.0), jnp.maximum(v, 0.0)
    k_west, k_east = up + 0.25, up - u + 0.25
    k_south, k_north = vp + 0.25, vp - v + 0.25
    k_centre = k_west + k_east + k_south + k_north + 1.0
    out = []
    for c in range(3):
        out.append(
            k_west * west[c]
            + k_east * east[c]
            + k_south * south[c]
            + k_north * north[c]
            + 0.5 * vertical[c]
            - k_centre * centre[c]
        )
    out[0] = out[0] + 0.3 * v - 0.25 * (east[2] - west[2])
    out[1] = out[1] - 0.3 * u - 0.25 * (north[2] - south[2])
    return out


def edge_lanes(rim, edge, halves):
    spot = iota((72, 128), 1) % 16
    for c in range(3):
        for half in range(halves):
            x = rim[c, half, 8:80, :]
            edge[c, half, 8:80, :] = jnp.where(spot == 5, roll(x, -6, 1), x)


def main_tendency(source, edge, level, last, first, rows):
    lane = iota((rows, 128), 1)
    above, below = min(level + 1, last), max(level - 1, 0)
    here = pl.ds(first, rows)
    centre, east, west, north, south, vertical = [], [], [], [], [], []
    for c in range(3):
        x = source[c, level, here, :]
        centre.append(x)
        east.append(roll(x, -1, 1))
        west.append(roll(x, 1, 1))
        if edge is not None:
            side = roll(edge[c, level // 8, here, :], 123 - 16 * (level % 8), 1)
            east[c] = jnp.where(lane == 127, side, east[c])
            west[c] = jnp.where(lane == 0, side, west[c])
        north.append(source[c, level, pl.ds(first + 1, rows), :])
        south.append(source[c, level, pl.ds(first - 1, rows), :])
        vertical.append(source[c, above, here, :] + source[c, below, here, :])
    return centre, tendency(centre, east, west, north, south, vertical)


def rim_tendency(source, halves, half, first, rows):
    lane = iota((rows, 128), 1)
    here = pl.ds(first, rows)
    centre, east, west, north, south, vertical = [], [], [], [], [], []
    for c in range(3):
        x = source[c, half, here, :]
        next_up = source[c, 1, here, :] if half == 0 and halves == 2 else x
        next_down = source[c, 0, here, :] if half == 1 else x
        above = jnp.where(lane < 112, roll(x, -16, 1), x if next_up is x else roll(next_up, -16, 1))
        below = jnp.where(lane >= 16, roll(x, 16, 1), x if next_down is x else roll(next_down, 16, 1))
        centre.append(x)
        east.append(roll(x, -1, 1))
        west.append(roll(x, 1, 1))
        north.append(source[c, half, pl.ds(first + 1, rows), :])
        south.append(source[c, half, pl.ds(first - 1, rows), :])
        vertical.append(above + below)
    return centre, tendency(centre, east, west, north, south, vertical)


CHUNKS = ((8, 24), (32, 24), (56, 24))
ALL_ROWS = tuple(range(8, 80, 8))
BODY = tuple(range(TOP, TOP + AY, 8))


def window_masks(flags):
    return {first: inside_window(first, 8, flags) for first in (8, 72)}


def first_stage(source, target, edge, levels, last, masks):
    for level in levels:
        for first in ALL_ROWS:
            centre, change = main_tendency(source, edge, level, last, first, 8)
            for c in range(3):
                value = centre[c] + 0.2 * change[c]
                if first in masks:
                    value = jnp.where(masks[first], value, 0.0)
                target[c, level, first : first + 8, :] = value


def second_stage(source, state, edge, levels, last, rows, write):
    for level in levels:
        for first in rows:
            centre, change = main_tendency(source, edge, level, last, first, 8)
            for c in range(3):
                old = state[c, level, first : first + 8, :]
                write(c, level, first, 0.5 * (old + centre[c]) + 0.1 * change[c])


def first_rim_stage(source, target, halves, flags):
    for half in range(halves):
        for first, rows in CHUNKS:
            centre, change = rim_tendency(source, halves, half, first, rows)
            for c in range(3):
                value = centre[c] + 0.2 * change[c]
                target[c, half, pl.ds(first, rows), :] = jnp.where(rim_inside(first, rows, flags), value, 0.0)


def second_rim_stage(source, state, halves, flags):
    for half in range(halves):
        for first, rows in CHUNKS:
            centre, change = rim_tendency(source, halves, half, first, rows)
            for c in range(3):
                here = pl.ds(first, rows)
                value = 0.5 * (state[c, half, here, :] + centre[c]) + 0.1 * change[c]
                state[c, half, here, :] = jnp.where(rim_inside(first, rows, flags), value, 0.0)


def plan_kernel(tiles, wind_plan, fire_plan, fire_sends, alive, home_plan, strip_plan):
    flags = place()
    me, ty, tx = flags[0], flags[1], flags[2]
    listed = tiles[...]
    owner, local, _ = slot_facts(listed)

    def numbers(dy, dx):
        ok = (ty + dy >= 0) & (ty + dy < NTY) & (tx + dx >= 0) & (tx + dx < NTX)
        return slots_of(owner, local, jnp.where(ok, me + dy * NTX + dx, -7))

    here = numbers(0, 0)
    north, south, west, east = numbers(1, 0), numbers(-1, 0), numbers(0, -1), numbers(0, 1)
    south_west, south_east = numbers(-1, -1), numbers(-1, 1)
    north_west, north_east = numbers(1, -1), numbers(1, 1)
    tile = iota((64, 128), 0).astype(F32) + 1.0
    edge_tile = iota((8, 128), 0).astype(F32) + 1.0
    row = iota((80, 128), 0)
    first_tile = ((row // 8 - 1) * 8 + 1).astype(F32)
    body = (row >= 8) & (row < 72)

    for j in range(2):
        chosen = (here[j] == tile).astype(F32)
        chosen = jnp.concatenate([chosen, chosen], axis=0).T.astype(BF16)
        wind_plan[j * 128 : (j + 1) * 128, 0:128] = chosen
        wind_plan[j * 128 : (j + 1) * 128, 128:256] = chosen
    mine = jnp.sum(
        jnp.where(iota((32, 128), 1) == me, listed.astype(F32), 0.0), axis=1, keepdims=True
    ).astype(jnp.int32)
    holder, _, live = slot_facts(mine)
    member = (holder == iota((32, 128), 1)).astype(F32)
    before = earlier(member)
    places = [jnp.where(before == float(j), member, 0.0) for j in (0, 1)]
    fire_plan[...] = jnp.concatenate(places, axis=1).astype(BF16)
    alive[...] = jnp.where(live, jnp.ones((32, 128), F32), 0.0)

    chosen = jnp.concatenate(places + [jnp.zeros((64, 128), F32)], axis=0).T
    part = iota((128, 128), 1) // 32
    for j in range(2):
        fire_sends[j * 128 : (j + 1) * 128, :] = jnp.where(part == j, chosen, 0.0).astype(BF16)
        from_south = (south[j] == edge_tile + 56.0).astype(F32)
        from_north = (north[j] == edge_tile).astype(F32)
        from_west = body & (west[j] == first_tile + 7.0)
        from_west = from_west | ((row == 7) & (south_west[j] == 64.0)) | ((row == 72) & (north_west[j] == 8.0))
        from_east = body & (east[j] == first_tile)
        from_east = from_east | ((row == 7) & (south_east[j] == 57.0)) | ((row == 72) & (north_east[j] == 1.0))
        lanes = slice(j * 128, (j + 1) * 128)
        home_plan[:, lanes] = (here[j] == tile).astype(F32).astype(BF16)
        strips = [from_south, from_north, from_west.astype(F32), from_east.astype(F32)]
        strip_plan[:, lanes] = jnp.concatenate(strips, axis=0).astype(BF16)


def surface_kernel(planes, low, high, after, out, main, middle):
    flags = place()
    fill_main(main, planes, range(3), flags, low, high)
    first_stage(main, middle, None, range(2), 2, window_masks(flags))
    for first in BODY:
        centre, change = main_tendency(middle, None, 0, 2, first, 8)
        for c in range(2):
            value = 0.5 * (main[c, 0, first : first + 8, :] + centre[c]) + 0.1 * change[c]
            out[first - TOP : first - TOP + 8, 128 * c : 128 * c + 128] = value


def wind_kernel(inner, blocks, from_west, from_east, east, west, plan, out, rim, rim_middle):
    flags = place()
    fill_rim(rim, 1, flags, (from_west, from_east, east, west))
    first_rim_stage(rim, rim_middle, 1, flags)
    centre, change = rim_tendency(rim_middle, 1, 0, TOP, AY)
    lane = iota((AY, 128), 1)
    later = []
    for c in range(2):
        sides = 0.5 * (rim[c, 0, TOP : TOP + AY, :] + centre[c]) + 0.1 * change[c]
        field = jnp.where(lane < 2, roll(sides, -12, 1), inner[:, 128 * c : 128 * c + 128])
        later.append(jnp.where(lane >= 126, roll(sides, 124, 1), field))
    pieces = parts(jnp.concatenate([blocks[...]] + [swap_blocks(x) for x in later], axis=1))
    pieces = jnp.concatenate(pieces + (jnp.zeros((64, 512), BF16),), axis=0)
    picked = dot(plan[...], pieces)
    for j in range(2):
        for q in range(4):
            out[pl.ds(j * 4 + q, 128, stride=8), :] = picked[j * 128 : (j + 1) * 128, q * 128 : (q + 1) * 128]


def slopes(p):
    cell = iota((8, FC), 1)
    col = cell - 80 * ((cell * 52429) >> 22)
    east = jnp.where(col == 79, p, roll(p, -1, 1))
    west = jnp.where(col == 0, p, roll(p, 1, 1))
    north = jnp.where(cell >= FC - 80, p, roll(p, -80, 1))
    south = jnp.where(cell < 80, p, roll(p, 80, 1))
    gx, gy = 0.5 * (east - west), 0.5 * (north - south)
    square = 1.0 + gx * gx + gy * gy
    inverse = lax.rsqrt(square)
    return gx * inverse, gy * inverse, square * inverse


def fuel_fields(rates, heats, kinds, burns, depths, rate, heat, level, slope_x, slope_y, reach):
    for g in range(3):
        here = slice(8 * g, 8 * g + 8)
        kind = kinds[here, :]
        rate_cell = jnp.zeros(kind.shape, F32)
        heat_cell = jnp.zeros(kind.shape, F32)
        for k in range(13):
            match = kind == k
            rate_cell = jnp.where(match, rates[0:1, k : k + 1], rate_cell)
            heat_cell = jnp.where(match, heats[0:1, k : k + 1], heat_cell)
        p = jnp.where(burns[here, :] == 1, -depths[here, :], depths[here, :])
        along_x, along_y, stretch = slopes(p)
        rate[here, :] = rate_cell
        heat[here, :] = heat_cell
        level[here, :] = p
        slope_x[here, :] = along_x
        slope_y[here, :] = along_y
        reach[here, :] = rate_cell * stretch


def step_kernel(
    atmos, from_west, from_east, east, west, low, high, rates, heats, category, burn, depth,
    out, rim, rate, heat, level, slope_x, slope_y, reach,
    main, middle, rim_middle, edge, planes, kinds, burns, depths, sems,
):
    flags = place()
    groups = [pl.ds(4 * g, 4) for g in range(4)]
    loads = [pltpu.make_async_copy(atmos.at[:, x], planes.at[:, x], sems.at[g]) for g, x in enumerate(groups)]
    stores = [pltpu.make_async_copy(main.at[:, x], out.at[:, x], sems.at[4 + g]) for g, x in enumerate(groups)]
    fuel = [
        pltpu.make_async_copy(source, target, sems.at[8 + i])
        for i, (source, target) in enumerate(((category, kinds), (burn, burns), (depth, depths)))
    ]
    for load in loads + fuel:
        load.start()
    fill_rim(rim, 2, flags, (from_west, from_east, east, west))
    edge_lanes(rim, edge, 2)
    masks = window_masks(flags)
    for g in range(4):
        loads[g].wait()
        fill_main(main, planes, range(4 * g, 4 * g + 4), flags, low, high)
        first_stage(main, middle, edge, range(max(4 * g - 1, 0), 4 * g + 3 if g < 3 else LEV), LEV - 1, masks)
    first_rim_stage(rim, rim_middle, 2, flags)
    edge_lanes(rim_middle, edge, 2)

    def write(c, level, first, value):
        if first in masks:
            value = jnp.where(masks[first], value, 0.0)
        main[c, level, first : first + 8, :] = value

    for g in range(4):
        second_stage(middle, main, edge, range(4 * g, 4 * g + 4), LEV - 1, ALL_ROWS, write)
        stores[g].start()
    second_rim_stage(rim_middle, rim, 2, flags)
    for load in fuel:
        load.wait()
    fuel_fields(rates, heats, kinds, burns, depths, rate, heat, level, slope_x, slope_y, reach)
    for store in stores:
        store.wait()


def fire_kernel(
    received, plan, sends, live, rate, heat, level, slope_x, slope_y, reach, table_in, rim,
    out, out_level, wind, released, spread, gather, sent, new_level, sems,
):
    gather_copy = pltpu.make_async_copy(table_in, gather, sems.at[2])
    gather_copy.start()
    cell = iota((1, FC), 1)
    fire_row = (cell * 52429) >> 22
    fire_col = cell - 80 * fire_row
    coarse = ((fire_row * 13108) >> 16) * 16 + ((fire_col * 13108) >> 16)
    spread[...] = (iota((128, FC), 0) == coarse).astype(F32).astype(BF16)
    rows = [[received[pl.ds(j * 4 + q, 128, stride=8), :] for q in range(4)] for j in range(2)]
    table = jnp.concatenate([jnp.concatenate(r, axis=1) for r in rows], axis=0)
    winds = pick(plan[...], table)
    winds = [winds[0:SLOTS, q * 128 : (q + 1) * 128] for q in range(4)]
    wind[...] = pick_right(jnp.concatenate(winds, axis=0), spread[...], dot)

    for g in range(3):
        here = slice(8 * g, 8 * g + 8)
        alive = live[here, 0:1] > 0.0
        p = level[here, :]
        tanh_p = jnp.tanh(p)
        along_x, along_y, far = slope_x[here, :], slope_y[here, :], reach[here, :]
        for t in range(2):
            if t:
                along_x, along_y, stretch = slopes(p)
                far = rate[here, :] * stretch
            u = wind[t * 48 + 8 * g : t * 48 + 8 * g + 8, :]
            v = wind[t * 48 + 24 + 8 * g : t * 48 + 32 + 8 * g, :]
            along = u * along_x + v * along_y
            softplus = jnp.maximum(along, 0.0) + jnp.log(1.0 + jnp.exp(-jnp.abs(along)))
            p = jnp.where(alive, p - far * (1.0 + softplus), p)
            tanh_new = jnp.tanh(p)
            released[t * 24 + 8 * g : t * 24 + 8 * g + 8, :] = heat[here, :] * (tanh_p - tanh_new)
            tanh_p = tanh_new
        new_level[here, :] = p
    level_copy = pltpu.make_async_copy(new_level, out_level, sems.at[0])
    level_copy.start()
    gather_copy.wait()
    sums = 0.02 * pick_right(released[...], gather[...], dot)

    heats = jnp.concatenate([sums[0:SLOTS], sums[SLOTS:]], axis=1)
    gap = jnp.zeros((8, 256), F32)
    heats = jnp.concatenate([heats, gap, heats, gap, jnp.zeros((64, 256), F32)], axis=0)
    blocks = pick(sends[...], heats)
    lane = iota((128, 128), 1)
    group, spot = lane // 16, lane % 16
    for j in range(2):
        first = blocks[j * 128 : (j + 1) * 128, 0:128]
        sent[pl.ds(j, 128, stride=6), :] = first
        sent[pl.ds(2 + j, 128, stride=6), :] = blocks[j * 128 : (j + 1) * 128, 128:256]
        north, south = roll(first, -16, 0), roll(first, 16, 0)
        west, east = roll(first, 1, 0), roll(first, -1, 0)
        west_corner, east_corner = roll(west, 41, 1), roll(east, 57, 1)
        strip = jnp.where(group < 2, north, jnp.where(group >= 6, south, 0.0))
        middle_rows = (group >= 2) & (group < 6)
        strip = jnp.where(middle_rows & (spot >= 14), west, strip)
        strip = jnp.where(middle_rows & ((spot == 12) | (spot == 13)), roll(west, 62, 1), strip)
        strip = jnp.where(middle_rows & (spot < 2), east, strip)
        strip = jnp.where(middle_rows & ((spot == 2) | (spot == 3)), roll(east, 66, 1), strip)
        strip = jnp.where(lane == 40, roll(west_corner, 16, 0), strip)
        strip = jnp.where(lane == 41, roll(east_corner, 16, 0), strip)
        strip = jnp.where(lane == 56, roll(west_corner, -16, 0), strip)
        strip = jnp.where(lane == 57, roll(east_corner, -16, 0), strip)
        sent[pl.ds(4 + j, 128, stride=6), :] = strip
    copy = pltpu.make_async_copy(sent, out, sems.at[1])
    copy.start()
    copy.wait()
    level_copy.wait()


def heat_fields(received, home_plan, strip_plan):
    rows = [received[pl.ds(q, 128, stride=6), :] for q in range(6)]
    table = jnp.concatenate(
        [jnp.concatenate([rows[0], rows[2]], axis=1), jnp.concatenate([rows[1], rows[3]], axis=1)], axis=0
    )
    home = pick(home_plan[...], table)
    strips = pick(strip_plan[...], jnp.concatenate(rows[4:6], axis=0))
    lane8 = iota((8, 128), 1)
    blocks = jnp.concatenate(
        [
            jnp.where(lane8 >= 96, strips[0:8], 0.0),
            home[:, 0:128],
            jnp.where(lane8 < 32, strips[8:16], 0.0),
        ],
        axis=0,
    )
    first, second = swap_blocks(blocks), swap_blocks(home[:, 128:256])

    lane, row = iota((80, 128), 1), iota((80, 128), 0)
    group, spot, y = lane // 16, lane % 16, row % 8
    straight = (y >= 2) & (y < 6)
    corner = (row == 7) | (row == 72)
    wanted_group = jnp.where(y < 2, y + 4, jnp.where(y > 5, y - 4, y))
    wanted_group = jnp.where(row == 7, 2, jnp.where(row == 72, 3, wanted_group))
    fits = group == wanted_group
    west_spot = spot - jnp.where(corner, 8, jnp.where(straight, 14, 12))
    east_spot = spot - jnp.where(corner, 9, jnp.where(straight, 0, 2))
    width = jnp.where(corner, 1, 2)
    west_fits = fits & (west_spot >= 0) & (west_spot < width)
    east_fits = fits & (east_spot >= 0) & (east_spot < width)
    value = jnp.where(west_fits, strips[16:96], 0.0) + jnp.where(east_fits, strips[96:176], 0.0)
    for shift in (64, 32, 16):
        value = value + roll(value, shift, 1)
    to_west = jnp.where(corner, roll(value, 3, 1), jnp.where(straight, roll(value, -4, 1), roll(value, -2, 1)))
    to_east = jnp.where(corner, roll(value, -5, 1), jnp.where(straight, roll(value, 4, 1), roll(value, 2, 1)))
    rim = jnp.where((lane == 11) | ((lane == 10) & ~corner), to_west, 0.0)
    rim = jnp.where((lane == 4) | ((lane == 5) & ~corner), to_east, rim)
    rim = jnp.where((lane == 12) | (lane == 13), roll(first, 12, 1), rim)
    rim = jnp.where((lane == 2) | (lane == 3), roll(first, 4, 1), rim)
    return first, second, rim


def upper_kernel(main_in, rim, fire_level, out, kept, bottom, main, middle, rim_middle, edge, result, sems):
    flags = place()
    groups = [(0, 5), (5, 4), (9, 4), (13, 3)]
    loads = [
        pltpu.make_async_copy(main_in.at[:, pl.ds(*x)], main.at[:, pl.ds(*x)], sems.at[g])
        for g, x in enumerate(groups)
    ]
    for load in loads:
        load.start()
    edge_lanes(rim, edge, 2)
    masks = window_masks(flags)
    for g, (first, count) in enumerate(groups):
        loads[g].wait()
        end = first + count - 1 if g < 3 else LEV
        first_stage(main, middle, edge, range(max(first - 1, 2), end), LEV - 1, masks)
    first_rim_stage(rim, rim_middle, 2, flags)
    edge_lanes(rim_middle, edge, 2)
    bottom[...] = main[:, 0:3]
    kept[...] = middle[:, 2:4]

    def write(c, level, first, value):
        result[c, level - 3, first - TOP : first - TOP + 8, :] = value

    stores = []
    for g, (first, count) in enumerate(((3, 4), (7, 4), (11, 5))):
        second_stage(middle, main, edge, range(first, first + count), LEV - 1, BODY, write)
        part = result.at[:, pl.ds(first - 3, count)]
        stores.append(pltpu.make_async_copy(part, out.at[:, pl.ds(first, count)], sems.at[4 + g]))
        stores[g].start()
    for store in stores:
        store.wait()


def lower_kernel(
    received, home_plan, strip_plan, main_in, rim_in, kept, upper, out, main, middle, rim, rim_middle, edge,
    result, sems,
):
    flags = place()
    main[...] = main_in[...]
    rim[:, 0] = rim_in[:, 0]
    middle[:, 2:4] = kept[...]
    first, second, rim_heat = heat_fields(received, home_plan, strip_plan)
    main[2, 0, 4:84, :] = main[2, 0, 4:84, :] + first
    rim[2, 0, 4:84, :] = rim[2, 0, 4:84, :] + rim_heat
    edge_lanes(rim, edge, 1)
    first_stage(main, middle, edge, range(2), 2, window_masks(flags))
    first_rim_stage(rim, rim_middle, 1, flags)
    edge_lanes(rim_middle, edge, 1)

    def write(c, level, row, value):
        if c == 2 and level == 0:
            value = value + second[row - TOP : row - TOP + 8]
        result[c, level, row - TOP : row - TOP + 8, :] = value

    stores = []
    for level in (2, 1, 0):
        second_stage(middle, main, edge, (level,), 3, BODY, write)
        stores.append(pltpu.make_async_copy(result.at[:, level], out.at[:, level], sems.at[level]))
        stores[-1].start()
    for store in stores:
        store.wait()


SMEM = pl.BlockSpec(memory_space=pltpu.SMEM)
VMEM = pl.BlockSpec(memory_space=pltpu.VMEM)
HBM = pl.BlockSpec(memory_space=pltpu.HBM)
ANY = pl.BlockSpec(memory_space=pl.ANY)


def shape(*dims, dtype=F32):
    return jax.ShapeDtypeStruct(dims, dtype)


def hbm(*dims):
    return pltpu.HBM(dims, F32)


def in_hbm(x):
    return pltpu.with_memory_space_constraint(x, pltpu.HBM)


def call(kernel, name, out_shape, in_specs, scratch=(), out_specs=None, flops=0, moved=0, mib=16, aliases=None):
    return pl.pallas_call(
        kernel,
        out_shape=out_shape,
        in_specs=in_specs,
        out_specs=jax.tree.map(lambda _: VMEM, out_shape) if out_specs is None else out_specs,
        scratch_shapes=list(scratch),
        input_output_aliases=aliases or {},
        compiler_params=pltpu.CompilerParams(vmem_limit_bytes=mib << 20),
        cost_estimate=pl.CostEstimate(flops=flops, bytes_accessed=moved, transcendentals=0),
        name=name,
    )


def gather_table():
    cell = np.arange(FC)
    coarse = cell // 80 // 5 * 16 + cell % 80 // 5
    return jnp.asarray((coarse[:, None] == np.arange(128)[None, :]).astype(np.float32), BF16)


def both_ways(to_next, to_previous, axis):
    size = lax.axis_size(axis)
    ahead = [(i, (i + 1) % size) for i in range(size)]
    return (
        lax.ppermute(to_next, axis, ahead),
        lax.ppermute(to_previous, axis, [(j, i) for i, j in ahead]),
    )


def exchange(x):
    return lax.all_to_all(x.reshape(-1), AXES, 0, 0, tiled=True).reshape(x.shape)


def main_buffer(levels):
    return pltpu.VMEM((3, levels, ROWS, 128), F32)


def rim_buffer(halves):
    return pltpu.VMEM((3, halves, ROWS, 128), F32)


def copy_sems(n):
    return pltpu.SemaphoreType.DMA((n,))


def on_device(atmos, slot_tile, fuel_cat, front_burn, front_depth, fuel_rate, fuel_heat):
    tiles = jnp.pad(slot_tile.reshape(DEVICES, SLOTS).T, ((0, 8), (0, 0)), constant_values=-1)
    atmos = in_hbm(atmos)

    rows = shape(24, 8, 128)
    eight = pltpu.VMEM((3, LEV, 8, 128), F32)
    up, down = call(pack_rows, "pack_rows", (rows, rows), [HBM], [eight, eight, copy_sems(2)], mib=8)(atmos)
    low, high = both_ways(up, down, "ty")
    body = shape(2, AY, 128)
    east_rows, west_rows, surface, blocks = call(
        pack_columns, "pack_columns", (body, body, shape(3, 3, AY, 128), shape(64, 256)), [HBM], [pltpu.VMEM((3, LEV, AY, 128), F32), copy_sems(4)],
        flops=4_000_000, moved=1_800_000, mib=8,
    )(atmos)
    columns = shape(2, AY + 8, 128)
    east, west = call(join_columns, "join_columns", (columns, columns), [VMEM] * 4, mib=8)(
        east_rows, west_rows, low, high
    )
    from_west, from_east = both_ways(east, west, "tx")
    halo = (from_west, from_east, east, west, low, high)

    cells = shape(SLOTS, FC)
    wind_plan, fire_plan, fire_sends, alive, home_plan, strip_plan = call(
        plan_kernel,
        "plan",
        (
            shape(256, 256, dtype=BF16),
            shape(32, 256, dtype=BF16),
            shape(256, 128, dtype=BF16),
            shape(32, 128),
            shape(64, 256, dtype=BF16),
            shape(176, 256, dtype=BF16),
        ),
        [VMEM],
        flops=4_000_000,
        moved=400_000,
        mib=8,
    )(tiles)
    inner = call(
        surface_kernel,
        "surface",
        shape(AY, 256),
        [VMEM] * 3 + [ANY],
        [main_buffer(3), main_buffer(3)],
        flops=10_000_000,
        moved=2_000_000,
        mib=8,
    )(surface, low, high, east)
    winds = call(
        wind_kernel,
        "wind",
        shape(DEVICES * 8, 128),
        [VMEM] * 7,
        [rim_buffer(1), rim_buffer(1)],
        flops=10_000_000,
        moved=2_000_000,
        mib=8,
    )(inner, blocks, from_west, from_east, east, west, wind_plan)
    got_winds = exchange(winds)

    main, rim, *fuel = call(
        step_kernel,
        "step",
        (hbm(3, LEV, ROWS, 128), shape(3, 2, ROWS, 128)) + (cells,) * 6,
        [HBM] + [VMEM] * 8 + [HBM] * 3,
        [main_buffer(LEV), main_buffer(LEV), rim_buffer(2), rim_buffer(2)]
        + [pltpu.VMEM((3, LEV, AY, 128), F32)]
        + [pltpu.VMEM((SLOTS, FC), jnp.int32)] * 2
        + [pltpu.VMEM((SLOTS, FC), F32), copy_sems(11)],
        (HBM,) + (VMEM,) * 7,
        flops=40_000_000,
        moved=8_000_000,
        mib=12,
    )(
        atmos,
        *halo,
        fuel_rate.reshape(1, -1),
        fuel_heat.reshape(1, -1),
        in_hbm(fuel_cat),
        in_hbm(front_burn),
        in_hbm(front_depth),
    )

    heats, fire_level = call(
        fire_kernel,
        "fire",
        (hbm(DEVICES * 6, 128), hbm(SLOTS, FC)),
        [VMEM] * 10 + [HBM, ANY],
        [
            pltpu.VMEM((4 * SLOTS, FC), F32),
            pltpu.VMEM((2 * SLOTS, FC), F32),
            pltpu.VMEM((128, FC), BF16),
            pltpu.VMEM((FC, 128), BF16),
            pltpu.VMEM((DEVICES * 6, 128), F32),
            pltpu.VMEM((SLOTS, FC), F32),
            copy_sems(3),
        ],
        (HBM, HBM),
        flops=40_000_000,
        moved=4_000_000,
    )(got_winds, fire_plan, fire_sends, alive, *fuel, in_hbm(gather_table()), rim)
    got_heats = exchange(heats)

    upper, kept, bottom = call(
        upper_kernel,
        "upper",
        (hbm(3, LEV, AY, 128), shape(3, 2, ROWS, 128), shape(3, 3, ROWS, 128)),
        [HBM, VMEM, HBM],
        [main_buffer(LEV), main_buffer(LEV), rim_buffer(2), rim_buffer(2)]
        + [pltpu.VMEM((3, LEV - 3, AY, 128), F32), copy_sems(7)],
        (HBM, VMEM, VMEM),
        flops=40_000_000,
        moved=8_000_000,
        mib=12,
    )(in_hbm(main), rim, in_hbm(fire_level))
    atmos_out = call(
        lower_kernel,
        "lower",
        hbm(3, LEV, AY, 128),
        [VMEM] * 6 + [HBM],
        [
            main_buffer(3),
            main_buffer(4),
            rim_buffer(1),
            rim_buffer(1),
            rim_buffer(1),
            pltpu.VMEM((3, 3, AY, 128), F32),
            copy_sems(3),
        ],
        HBM,
        flops=10_000_000,
        moved=2_000_000,
        mib=12,
        aliases={6: 0},
    )(got_heats, home_plan, strip_plan, bottom, rim, kept, in_hbm(upper))
    return atmos_out, fire_level


def solution(mesh):
    in_specs = (
        P(None, None, "ty", "tx"),
        P(),
        P(("ty", "tx"), None),
        P(("ty", "tx"), None),
        P(("ty", "tx"), None),
        P(),
        P(),
    )
    out_specs = (P(None, None, "ty", "tx"), P(("ty", "tx"), None))
    return jax.shard_map(
        on_device, mesh=mesh, in_specs=in_specs, out_specs=out_specs, check_vma=False
    )
```

```python
import jax
import jax.numpy as jnp
import numpy as np
from jax import lax
from jax.experimental import pallas as pl
from jax.experimental.pallas import tpu as pltpu
from jax.sharding import PartitionSpec as P

AXES = ("tx", "ty")
NTY, NTX, DEVICES = 8, 16, 128
LEV, AY, AX = 16, 64, 128
SLOTS, FC = 24, 3200
ROWS = 88
TOP = 12
F32, BF16 = jnp.float32, jnp.bfloat16


def roll(x, shift, axis):
    size = x.shape[axis]
    return pltpu.roll(x, shift % size, axis) if shift % size else x


def place():
    ty, tx = lax.axis_index("ty"), lax.axis_index("tx")
    return tx * NTY + ty, ty, tx


def iota(shape, dim):
    return lax.broadcasted_iota(jnp.int32, shape, dim)


def parts(x):
    high = x.astype(BF16)
    rest = x - high.astype(F32)
    middle = rest.astype(BF16)
    low = (rest - middle.astype(F32)).astype(BF16)
    return high, middle, low


def dot(a, b):
    return jnp.dot(a, b, preferred_element_type=F32)


def pick(onehot, x):
    high, middle, _ = parts(x)
    return dot(onehot, high) + dot(onehot, middle)


def swap_blocks(x):
    x = x.reshape(x.shape[0] // 8, 8, 128)
    sub, group = iota(x.shape, 1), iota(x.shape, 2) // 16
    for step in (1, 2, 4):
        sub_bit, group_bit = (sub & step) != 0, (group & step) != 0
        below = roll(roll(x, -step, 1), 16 * step, 2)
        above = roll(roll(x, step, 1), -16 * step, 2)
        x = jnp.where(sub_bit == group_bit, x, jnp.where(group_bit, below, above))
    return x.reshape(x.shape[0] * 8, 128)


def pick_right(x, onehot, product):
    high, middle, _ = parts(x)
    both = product(jnp.concatenate([high, middle], axis=0), onehot)
    return both[0 : x.shape[0]] + both[x.shape[0] :]


def slot_facts(tile):
    row, col = tile >> 7, tile & 127
    owner = (col >> 3) * NTY + (row >> 3)
    local = (row & 7) * 8 + (col & 7)
    live = tile >= 0
    return jnp.where(live, owner, -1), local + 1, live


def earlier(member):
    lower = (iota((32, 32), 0) > iota((32, 32), 1)).astype(F32).astype(BF16)
    return dot(lower, member.astype(BF16))


def slots_of(owner, local, home):
    member = (owner == home).astype(F32)
    before = earlier(member)
    numbers = member * local.astype(F32)
    return [
        jnp.sum(jnp.where(before == float(j), numbers, 0.0), axis=0, keepdims=True)
        for j in (0, 1)
    ]


def pack_rows(atmos, up, down, low_rows, high_rows, sems):
    copies = [
        pltpu.make_async_copy(atmos.at[:, :, pl.ds(0, 8), :], low_rows, sems.at[0]),
        pltpu.make_async_copy(atmos.at[:, :, pl.ds(AY - 8, 8), :], high_rows, sems.at[1]),
    ]
    for copy in copies:
        copy.start()
    for copy in copies:
        copy.wait()
    for c in range(3):
        for level in range(LEV):
            plane = c * LEV + level
            where = pl.ds(4 * (plane % 2), 4)
            up[plane // 2, where, :] = high_rows[c, level, 4:8, :]
            down[plane // 2, where, :] = low_rows[c, level, 0:4, :]


def packed_columns(plane, half, rows, quarters=None):
    lane = iota((rows, 128), 1)
    group, spot = lane // 16, lane % 16
    both = [jnp.zeros((rows, 128), F32)] * 3
    for k in range(8):
        if quarters is not None and k % 4 == 0:
            quarters[2 * half + k // 4].wait()
        for c in range(3):
            both[c] = jnp.where(group == k, roll(plane(c, half * 8 + k), 16 * k + 4, 1), both[c])
    to_east = jnp.zeros((rows, 128), F32)
    to_west = jnp.zeros((rows, 128), F32)
    for c in range(3):
        inside = (spot >= 4 * c) & (spot < 4 * c + 4)
        to_east = jnp.where(inside, roll(both[c], 4 * c, 1), to_east)
        to_west = jnp.where(inside, roll(both[c], 4 * c - 4, 1), to_west)
    return to_east, to_west


def pack_columns(atmos, east, west, surface, blocks, planes, sems):
    quarters = [
        pltpu.make_async_copy(atmos.at[:, pl.ds(4 * i, 4)], planes.at[:, pl.ds(4 * i, 4)], sems.at[i])
        for i in range(4)
    ]
    for copy in quarters:
        copy.start()
    for half in range(2):
        east[half], west[half] = packed_columns(lambda c, level: planes[c, level], half, AY, quarters)
        if half == 0:
            surface[...] = planes[:, 0:3]
            blocks[...] = jnp.concatenate([swap_blocks(planes[c, 0]) for c in range(2)], axis=1)


def join_columns(east_rows, west_rows, low, high, east, west):
    def plane(c, level):
        piece = c * LEV + level
        where = slice(4 * (piece % 2), 4 * (piece % 2) + 4)
        return jnp.concatenate([low[piece // 2, where, :], high[piece // 2, where, :]], axis=0)

    for half in range(2):
        east[half, 0:AY, :] = east_rows[half]
        west[half, 0:AY, :] = west_rows[half]
        east[half, AY : AY + 8, :], west[half, AY : AY + 8, :] = packed_columns(plane, half, 8)


def rim_of(c, from_west, from_east, east, west):
    spot = iota(east.shape, 1) % 16
    out = jnp.where(spot < 4, roll(east, -4 * c, 1), roll(from_east, 4 - 4 * c, 1))
    out = jnp.where(spot < 8, out, roll(from_west, 8 - 4 * c, 1))
    return jnp.where(spot < 12, out, roll(west, 12 - 4 * c, 1))


def inside_window(first, rows, flags):
    y = iota((rows, 128), 0) + (first - TOP)
    return ((y >= 0) | (flags[1] > 0)) & ((y < AY) | (flags[1] < NTY - 1))


def rim_inside(first, rows, flags):
    spot = iota((rows, 128), 1) % 16
    east_out = (spot >= 4) & (spot < 8) & (flags[2] == NTX - 1)
    west_out = (spot >= 8) & (spot < 12) & (flags[2] == 0)
    return inside_window(first, rows, flags) & ~(east_out | west_out)


def fill_rim(rim, halves, flags, messages):
    for c in range(3):
        for half in range(halves):
            for source, first, rows in ((0, TOP, AY), (AY, 8, 4), (AY + 4, 76, 4)):
                value = rim_of(c, *(m[half, source : source + rows, :] for m in messages))
                rim[c, half, first : first + rows, :] = jnp.where(rim_inside(first, rows, flags), value, 0.0)


def fill_main(main, atmos, levels, flags, low, high):
    for c in range(3):
        for level in levels:
            piece = c * LEV + level
            where = slice(4 * (piece % 2), 4 * (piece % 2) + 4)
            main[c, level, TOP : TOP + AY, :] = atmos[c, level]
            main[c, level, 8:12, :] = jnp.where(flags[1] > 0, low[piece // 2, where, :], 0.0)
            main[c, level, 76:80, :] = jnp.where(flags[1] < NTY - 1, high[piece // 2, where, :], 0.0)


def tendency(centre, east, west, north, south, vertical):
    u, v, _ = centre
    up, vp = jnp.maximum(u, 0.0), jnp.maximum(v, 0.0)
    k_west, k_east = up + 0.25, up - u + 0.25
    k_south, k_north = vp + 0.25, vp - v + 0.25
    k_centre = k_west + k_east + k_south + k_north + 1.0
    out = []
    for c in range(3):
        out.append(
            k_west * west[c]
            + k_east * east[c]
            + k_south * south[c]
            + k_north * north[c]
            + 0.5 * vertical[c]
            - k_centre * centre[c]
        )
    out[0] = out[0] + 0.3 * v - 0.25 * (east[2] - west[2])
    out[1] = out[1] - 0.3 * u - 0.25 * (north[2] - south[2])
    return out


def edge_lanes(rim, edge, halves):
    spot = iota((72, 128), 1) % 16
    for c in range(3):
        for half in range(halves):
            x = rim[c, half, 8:80, :]
            edge[c, half, 8:80, :] = jnp.where(spot == 5, roll(x, -6, 1), x)


def main_tendency(source, edge, level, last, first, rows):
    lane = iota((rows, 128), 1)
    above, below = min(level + 1, last), max(level - 1, 0)
    here = pl.ds(first, rows)
    centre, east, west, north, south, vertical = [], [], [], [], [], []
    for c in range(3):
        x = source[c, level, here, :]
        centre.append(x)
        east.append(roll(x, -1, 1))
        west.append(roll(x, 1, 1))
        if edge is not None:
            side = roll(edge[c, level // 8, here, :], 123 - 16 * (level % 8), 1)
            east[c] = jnp.where(lane == 127, side, east[c])
            west[c] = jnp.where(lane == 0, side, west[c])
        north.append(source[c, level, pl.ds(first + 1, rows), :])
        south.append(source[c, level, pl.ds(first - 1, rows), :])
        vertical.append(source[c, above, here, :] + source[c, below, here, :])
    return centre, tendency(centre, east, west, north, south, vertical)


def rim_tendency(source, halves, half, first, rows):
    lane = iota((rows, 128), 1)
    here = pl.ds(first, rows)
    centre, east, west, north, south, vertical = [], [], [], [], [], []
    for c in range(3):
        x = source[c, half, here, :]
        next_up = source[c, 1, here, :] if half == 0 and halves == 2 else x
        next_down = source[c, 0, here, :] if half == 1 else x
        above = jnp.where(lane < 112, roll(x, -16, 1), x if next_up is x else roll(next_up, -16, 1))
        below = jnp.where(lane >= 16, roll(x, 16, 1), x if next_down is x else roll(next_down, 16, 1))
        centre.append(x)
        east.append(roll(x, -1, 1))
        west.append(roll(x, 1, 1))
        north.append(source[c, half, pl.ds(first + 1, rows), :])
        south.append(source[c, half, pl.ds(first - 1, rows), :])
        vertical.append(above + below)
    return centre, tendency(centre, east, west, north, south, vertical)


CHUNKS = ((8, 24), (32, 24), (56, 24))
ALL_ROWS = tuple(range(8, 80, 8))
BODY = tuple(range(TOP, TOP + AY, 8))


def window_masks(flags):
    return {first: inside_window(first, 8, flags) for first in (8, 72)}


def first_stage(source, target, edge, levels, last, masks):
    for level in levels:
        for first in ALL_ROWS:
            centre, change = main_tendency(source, edge, level, last, first, 8)
            for c in range(3):
                value = centre[c] + 0.2 * change[c]
                if first in masks:
                    value = jnp.where(masks[first], value, 0.0)
                target[c, level, first : first + 8, :] = value


def second_stage(source, state, edge, levels, last, rows, write):
    for level in levels:
        for first in rows:
            centre, change = main_tendency(source, edge, level, last, first, 8)
            for c in range(3):
                old = state[c, level, first : first + 8, :]
                write(c, level, first, 0.5 * (old + centre[c]) + 0.1 * change[c])


def first_rim_stage(source, target, halves, flags):
    for half in range(halves):
        for first, rows in CHUNKS:
            centre, change = rim_tendency(source, halves, half, first, rows)
            for c in range(3):
                value = centre[c] + 0.2 * change[c]
                target[c, half, pl.ds(first, rows), :] = jnp.where(rim_inside(first, rows, flags), value, 0.0)


def second_rim_stage(source, state, halves, flags):
    for half in range(halves):
        for first, rows in CHUNKS:
            centre, change = rim_tendency(source, halves, half, first, rows)
            for c in range(3):
                here = pl.ds(first, rows)
                value = 0.5 * (state[c, half, here, :] + centre[c]) + 0.1 * change[c]
                state[c, half, here, :] = jnp.where(rim_inside(first, rows, flags), value, 0.0)


def plan_kernel(tiles, wind_plan, fire_plan, fire_sends, alive, home_plan, strip_plan):
    flags = place()
    me, ty, tx = flags[0], flags[1], flags[2]
    listed = tiles[...]
    owner, local, _ = slot_facts(listed)

    def numbers(dy, dx):
        ok = (ty + dy >= 0) & (ty + dy < NTY) & (tx + dx >= 0) & (tx + dx < NTX)
        return slots_of(owner, local, jnp.where(ok, me + dx * NTY + dy, -7))

    here = numbers(0, 0)
    north, south, west, east = numbers(1, 0), numbers(-1, 0), numbers(0, -1), numbers(0, 1)
    south_west, south_east = numbers(-1, -1), numbers(-1, 1)
    north_west, north_east = numbers(1, -1), numbers(1, 1)
    tile = iota((64, 128), 0).astype(F32) + 1.0
    edge_tile = iota((8, 128), 0).astype(F32) + 1.0
    row = iota((80, 128), 0)
    first_tile = ((row // 8 - 1) * 8 + 1).astype(F32)
    body = (row >= 8) & (row < 72)

    for j in range(2):
        chosen = (here[j] == tile).astype(F32)
        chosen = jnp.concatenate([chosen, chosen], axis=0).T.astype(BF16)
        wind_plan[j * 128 : (j + 1) * 128, 0:128] = chosen
        wind_plan[j * 128 : (j + 1) * 128, 128:256] = chosen
    mine = jnp.sum(
        jnp.where(iota((32, 128), 1) == me, listed.astype(F32), 0.0), axis=1, keepdims=True
    ).astype(jnp.int32)
    holder, _, live = slot_facts(mine)
    member = (holder == iota((32, 128), 1)).astype(F32)
    before = earlier(member)
    places = [jnp.where(before == float(j), member, 0.0) for j in (0, 1)]
    fire_plan[...] = jnp.concatenate(places, axis=1).astype(BF16)
    alive[...] = jnp.where(live, jnp.ones((32, 128), F32), 0.0)

    chosen = jnp.concatenate(places + [jnp.zeros((64, 128), F32)], axis=0).T
    part = iota((128, 128), 1) // 32
    for j in range(2):
        fire_sends[j * 128 : (j + 1) * 128, :] = jnp.where(part == j, chosen, 0.0).astype(BF16)
        from_south = (south[j] == edge_tile + 56.0).astype(F32)
        from_north = (north[j] == edge_tile).astype(F32)
        from_west = body & (west[j] == first_tile + 7.0)
        from_west = from_west | ((row == 7) & (south_west[j] == 64.0)) | ((row == 72) & (north_west[j] == 8.0))
        from_east = body & (east[j] == first_tile)
        from_east = from_east | ((row == 7) & (south_east[j] == 57.0)) | ((row == 72) & (north_east[j] == 1.0))
        lanes = slice(j * 128, (j + 1) * 128)
        home_plan[:, lanes] = (here[j] == tile).astype(F32).astype(BF16)
        strips = [from_south, from_north, from_west.astype(F32), from_east.astype(F32)]
        strip_plan[:, lanes] = jnp.concatenate(strips, axis=0).astype(BF16)


def surface_kernel(planes, low, high, after, out, main, middle):
    flags = place()
    fill_main(main, planes, range(3), flags, low, high)
    first_stage(main, middle, None, range(2), 2, window_masks(flags))
    for first in BODY:
        centre, change = main_tendency(middle, None, 0, 2, first, 8)
        for c in range(2):
            value = 0.5 * (main[c, 0, first : first + 8, :] + centre[c]) + 0.1 * change[c]
            out[first - TOP : first - TOP + 8, 128 * c : 128 * c + 128] = value


def wind_kernel(inner, blocks, from_west, from_east, east, west, plan, out, rim, rim_middle):
    flags = place()
    fill_rim(rim, 1, flags, (from_west, from_east, east, west))
    first_rim_stage(rim, rim_middle, 1, flags)
    centre, change = rim_tendency(rim_middle, 1, 0, TOP, AY)
    lane = iota((AY, 128), 1)
    later = []
    for c in range(2):
        sides = 0.5 * (rim[c, 0, TOP : TOP + AY, :] + centre[c]) + 0.1 * change[c]
        field = jnp.where(lane < 2, roll(sides, -12, 1), inner[:, 128 * c : 128 * c + 128])
        later.append(jnp.where(lane >= 126, roll(sides, 124, 1), field))
    pieces = parts(jnp.concatenate([blocks[...]] + [swap_blocks(x) for x in later], axis=1))
    pieces = jnp.concatenate(pieces + (jnp.zeros((64, 512), BF16),), axis=0)
    picked = dot(plan[...], pieces)
    for j in range(2):
        for q in range(4):
            out[pl.ds(j * 4 + q, 128, stride=8), :] = picked[j * 128 : (j + 1) * 128, q * 128 : (q + 1) * 128]


def slopes(p):
    cell = iota((8, FC), 1)
    col = cell - 80 * ((cell * 52429) >> 22)
    east = jnp.where(col == 79, p, roll(p, -1, 1))
    west = jnp.where(col == 0, p, roll(p, 1, 1))
    north = jnp.where(cell >= FC - 80, p, roll(p, -80, 1))
    south = jnp.where(cell < 80, p, roll(p, 80, 1))
    gx, gy = 0.5 * (east - west), 0.5 * (north - south)
    square = 1.0 + gx * gx + gy * gy
    inverse = lax.rsqrt(square)
    return gx * inverse, gy * inverse, square * inverse


def fuel_fields(rates, heats, kinds, burns, depths, rate, heat, level, slope_x, slope_y, reach):
    for g in range(3):
        here = slice(8 * g, 8 * g + 8)
        kind = kinds[here, :]
        rate_cell = jnp.zeros(kind.shape, F32)
        heat_cell = jnp.zeros(kind.shape, F32)
        for k in range(13):
            match = kind == k
            rate_cell = jnp.where(match, rates[0:1, k : k + 1], rate_cell)
            heat_cell = jnp.where(match, heats[0:1, k : k + 1], heat_cell)
        p = jnp.where(burns[here, :] == 1, -depths[here, :], depths[here, :])
        along_x, along_y, stretch = slopes(p)
        rate[here, :] = rate_cell
        heat[here, :] = heat_cell
        level[here, :] = p
        slope_x[here, :] = along_x
        slope_y[here, :] = along_y
        reach[here, :] = rate_cell * stretch


def step_kernel(
    atmos, from_west, from_east, east, west, low, high, rates, heats, category, burn, depth,
    out, rim, rate, heat, level, slope_x, slope_y, reach,
    main, middle, rim_middle, edge, planes, kinds, burns, depths, sems,
):
    flags = place()
    groups = [pl.ds(4 * g, 4) for g in range(4)]
    loads = [pltpu.make_async_copy(atmos.at[:, x], planes.at[:, x], sems.at[g]) for g, x in enumerate(groups)]
    stores = [pltpu.make_async_copy(main.at[:, x], out.at[:, x], sems.at[4 + g]) for g, x in enumerate(groups)]
    fuel = [
        pltpu.make_async_copy(source, target, sems.at[8 + i])
        for i, (source, target) in enumerate(((category, kinds), (burn, burns), (depth, depths)))
    ]
    for load in loads + fuel:
        load.start()
    fill_rim(rim, 2, flags, (from_west, from_east, east, west))
    edge_lanes(rim, edge, 2)
    masks = window_masks(flags)
    for g in range(4):
        loads[g].wait()
        fill_main(main, planes, range(4 * g, 4 * g + 4), flags, low, high)
        first_stage(main, middle, edge, range(max(4 * g - 1, 0), 4 * g + 3 if g < 3 else LEV), LEV - 1, masks)
    first_rim_stage(rim, rim_middle, 2, flags)
    edge_lanes(rim_middle, edge, 2)

    def write(c, level, first, value):
        if first in masks:
            value = jnp.where(masks[first], value, 0.0)
        main[c, level, first : first + 8, :] = value

    for g in range(4):
        second_stage(middle, main, edge, range(4 * g, 4 * g + 4), LEV - 1, ALL_ROWS, write)
        stores[g].start()
    second_rim_stage(rim_middle, rim, 2, flags)
    for load in fuel:
        load.wait()
    fuel_fields(rates, heats, kinds, burns, depths, rate, heat, level, slope_x, slope_y, reach)
    for store in stores:
        store.wait()


def fire_kernel(
    received, plan, sends, live, rate, heat, level, slope_x, slope_y, reach, table_in, rim,
    out, out_level, wind, released, spread, gather, sent, new_level, sems,
):
    gather_copy = pltpu.make_async_copy(table_in, gather, sems.at[2])
    gather_copy.start()
    cell = iota((1, FC), 1)
    fire_row = (cell * 52429) >> 22
    fire_col = cell - 80 * fire_row
    coarse = ((fire_row * 13108) >> 16) * 16 + ((fire_col * 13108) >> 16)
    spread[...] = (iota((128, FC), 0) == coarse).astype(F32).astype(BF16)
    rows = [[received[pl.ds(j * 4 + q, 128, stride=8), :] for q in range(4)] for j in range(2)]
    table = jnp.concatenate([jnp.concatenate(r, axis=1) for r in rows], axis=0)
    winds = pick(plan[...], table)
    winds = [winds[0:SLOTS, q * 128 : (q + 1) * 128] for q in range(4)]
    wind[...] = pick_right(jnp.concatenate(winds, axis=0), spread[...], dot)

    for g in range(3):
        here = slice(8 * g, 8 * g + 8)
        alive = live[here, 0:1] > 0.0
        p = level[here, :]
        tanh_p = jnp.tanh(p)
        along_x, along_y, far = slope_x[here, :], slope_y[here, :], reach[here, :]
        for t in range(2):
            if t:
                along_x, along_y, stretch = slopes(p)
                far = rate[here, :] * stretch
            u = wind[t * 48 + 8 * g : t * 48 + 8 * g + 8, :]
            v = wind[t * 48 + 24 + 8 * g : t * 48 + 32 + 8 * g, :]
            along = u * along_x + v * along_y
            softplus = jnp.maximum(along, 0.0) + jnp.log(1.0 + jnp.exp(-jnp.abs(along)))
            p = jnp.where(alive, p - far * (1.0 + softplus), p)
            tanh_new = jnp.tanh(p)
            released[t * 24 + 8 * g : t * 24 + 8 * g + 8, :] = heat[here, :] * (tanh_p - tanh_new)
            tanh_p = tanh_new
        new_level[here, :] = p
    level_copy = pltpu.make_async_copy(new_level, out_level, sems.at[0])
    level_copy.start()
    gather_copy.wait()
    sums = 0.02 * pick_right(released[...], gather[...], dot)

    heats = jnp.concatenate([sums[0:SLOTS], sums[SLOTS:]], axis=1)
    gap = jnp.zeros((8, 256), F32)
    heats = jnp.concatenate([heats, gap, heats, gap, jnp.zeros((64, 256), F32)], axis=0)
    blocks = pick(sends[...], heats)
    lane = iota((128, 128), 1)
    group, spot = lane // 16, lane % 16
    for j in range(2):
        first = blocks[j * 128 : (j + 1) * 128, 0:128]
        sent[pl.ds(j, 128, stride=6), :] = first
        sent[pl.ds(2 + j, 128, stride=6), :] = blocks[j * 128 : (j + 1) * 128, 128:256]
        north, south = roll(first, -1, 0), roll(first, 1, 0)
        west, east = roll(first, NTY, 0), roll(first, -NTY, 0)
        corners = jnp.where((lane == 40) | (lane == 56), roll(west, 41, 1), roll(east, 57, 1))
        strip = jnp.where(group < 2, north, jnp.where(group >= 6, south, 0.0))
        middle_rows = (group >= 2) & (group < 6)
        strip = jnp.where(middle_rows & (spot >= 14), west, strip)
        strip = jnp.where(middle_rows & ((spot == 12) | (spot == 13)), roll(west, 62, 1), strip)
        strip = jnp.where(middle_rows & (spot < 2), east, strip)
        strip = jnp.where(middle_rows & ((spot == 2) | (spot == 3)), roll(east, 66, 1), strip)
        strip = jnp.where((lane == 40) | (lane == 41), roll(corners, 1, 0), strip)
        strip = jnp.where((lane == 56) | (lane == 57), roll(corners, -1, 0), strip)
        sent[pl.ds(4 + j, 128, stride=6), :] = strip
    copy = pltpu.make_async_copy(sent, out, sems.at[1])
    copy.start()
    copy.wait()
    level_copy.wait()


def heat_fields(received, home_plan, strip_plan):
    rows = [received[pl.ds(q, 128, stride=6), :] for q in range(6)]
    table = jnp.concatenate(
        [jnp.concatenate([rows[0], rows[2]], axis=1), jnp.concatenate([rows[1], rows[3]], axis=1)], axis=0
    )
    home = pick(home_plan[...], table)
    strips = pick(strip_plan[...], jnp.concatenate(rows[4:6], axis=0))
    lane8 = iota((8, 128), 1)
    blocks = jnp.concatenate(
        [
            jnp.where(lane8 >= 96, strips[0:8], 0.0),
            home[:, 0:128],
            jnp.where(lane8 < 32, strips[8:16], 0.0),
        ],
        axis=0,
    )
    first, second = swap_blocks(blocks), swap_blocks(home[:, 128:256])

    lane, row = iota((80, 128), 1), iota((80, 128), 0)
    group, spot, y = lane // 16, lane % 16, row % 8
    straight = (y >= 2) & (y < 6)
    corner = (row == 7) | (row == 72)
    wanted_group = jnp.where(y < 2, y + 4, jnp.where(y > 5, y - 4, y))
    wanted_group = jnp.where(row == 7, 2, jnp.where(row == 72, 3, wanted_group))
    fits = group == wanted_group
    west_spot = spot - jnp.where(corner, 8, jnp.where(straight, 14, 12))
    east_spot = spot - jnp.where(corner, 9, jnp.where(straight, 0, 2))
    width = jnp.where(corner, 1, 2)
    west_fits = fits & (west_spot >= 0) & (west_spot < width)
    east_fits = fits & (east_spot >= 0) & (east_spot < width)
    value = jnp.where(west_fits, strips[16:96], 0.0) + jnp.where(east_fits, strips[96:176], 0.0)
    for shift in (64, 32, 16):
        value = value + roll(value, shift, 1)
    to_west = jnp.where(corner, roll(value, 3, 1), jnp.where(straight, roll(value, -4, 1), roll(value, -2, 1)))
    to_east = jnp.where(corner, roll(value, -5, 1), jnp.where(straight, roll(value, 4, 1), roll(value, 2, 1)))
    rim = jnp.where((lane == 11) | ((lane == 10) & ~corner), to_west, 0.0)
    rim = jnp.where((lane == 4) | ((lane == 5) & ~corner), to_east, rim)
    rim = jnp.where((lane == 12) | (lane == 13), roll(first, 12, 1), rim)
    rim = jnp.where((lane == 2) | (lane == 3), roll(first, 4, 1), rim)
    return first, second, rim


def upper_kernel(main_in, rim, fire_level, out, kept, bottom, main, middle, rim_middle, edge, result, sems):
    flags = place()
    groups = [(0, 5), (5, 4), (9, 4), (13, 3)]
    loads = [
        pltpu.make_async_copy(main_in.at[:, pl.ds(*x)], main.at[:, pl.ds(*x)], sems.at[g])
        for g, x in enumerate(groups)
    ]
    for load in loads:
        load.start()
    edge_lanes(rim, edge, 2)
    masks = window_masks(flags)
    for g, (first, count) in enumerate(groups):
        loads[g].wait()
        end = first + count - 1 if g < 3 else LEV
        first_stage(main, middle, edge, range(max(first - 1, 2), end), LEV - 1, masks)
    first_rim_stage(rim, rim_middle, 2, flags)
    edge_lanes(rim_middle, edge, 2)
    bottom[...] = main[:, 0:3]
    kept[...] = middle[:, 2:4]

    def write(c, level, first, value):
        result[c, level - 3, first - TOP : first - TOP + 8, :] = value

    stores = []
    for g, (first, count) in enumerate(((3, 4), (7, 4), (11, 5))):
        second_stage(middle, main, edge, range(first, first + count), LEV - 1, BODY, write)
        part = result.at[:, pl.ds(first - 3, count)]
        stores.append(pltpu.make_async_copy(part, out.at[:, pl.ds(first, count)], sems.at[4 + g]))
        stores[g].start()
    for store in stores:
        store.wait()


def lower_kernel(
    received, home_plan, strip_plan, main_in, rim_in, kept, upper, out, main, middle, rim, rim_middle, edge,
    result, sems,
):
    flags = place()
    main[...] = main_in[...]
    rim[:, 0] = rim_in[:, 0]
    middle[:, 2:4] = kept[...]
    first, second, rim_heat = heat_fields(received, home_plan, strip_plan)
    main[2, 0, 4:84, :] = main[2, 0, 4:84, :] + first
    rim[2, 0, 4:84, :] = rim[2, 0, 4:84, :] + rim_heat
    edge_lanes(rim, edge, 1)
    first_stage(main, middle, edge, range(2), 2, window_masks(flags))
    first_rim_stage(rim, rim_middle, 1, flags)
    edge_lanes(rim_middle, edge, 1)

    def write(c, level, row, value):
        if c == 2 and level == 0:
            value = value + second[row - TOP : row - TOP + 8]
        result[c, level, row - TOP : row - TOP + 8, :] = value

    stores = []
    for level in (2, 1, 0):
        second_stage(middle, main, edge, (level,), 3, BODY, write)
        stores.append(pltpu.make_async_copy(result.at[:, level], out.at[:, level], sems.at[level]))
        stores[-1].start()
    for store in stores:
        store.wait()


SMEM = pl.BlockSpec(memory_space=pltpu.SMEM)
VMEM = pl.BlockSpec(memory_space=pltpu.VMEM)
HBM = pl.BlockSpec(memory_space=pltpu.HBM)
ANY = pl.BlockSpec(memory_space=pl.ANY)


def shape(*dims, dtype=F32):
    return jax.ShapeDtypeStruct(dims, dtype)


def hbm(*dims):
    return pltpu.HBM(dims, F32)


def in_hbm(x):
    return pltpu.with_memory_space_constraint(x, pltpu.HBM)


def call(kernel, name, out_shape, in_specs, scratch=(), out_specs=None, flops=0, moved=0, mib=16, aliases=None):
    return pl.pallas_call(
        kernel,
        out_shape=out_shape,
        in_specs=in_specs,
        out_specs=jax.tree.map(lambda _: VMEM, out_shape) if out_specs is None else out_specs,
        scratch_shapes=list(scratch),
        input_output_aliases=aliases or {},
        compiler_params=pltpu.CompilerParams(vmem_limit_bytes=mib << 20),
        cost_estimate=pl.CostEstimate(flops=flops, bytes_accessed=moved, transcendentals=0),
        name=name,
    )


def gather_table():
    cell = np.arange(FC)
    coarse = cell // 80 // 5 * 16 + cell % 80 // 5
    return jnp.asarray((coarse[:, None] == np.arange(128)[None, :]).astype(np.float32), BF16)


def both_ways(to_next, to_previous, axis):
    size = lax.axis_size(axis)
    ahead = [(i, (i + 1) % size) for i in range(size)]
    return (
        lax.ppermute(to_next, axis, ahead),
        lax.ppermute(to_previous, axis, [(j, i) for i, j in ahead]),
    )


def exchange(x):
    return lax.all_to_all(x.reshape(-1), AXES, 0, 0, tiled=True).reshape(x.shape)


def main_buffer(levels):
    return pltpu.VMEM((3, levels, ROWS, 128), F32)


def rim_buffer(halves):
    return pltpu.VMEM((3, halves, ROWS, 128), F32)


def copy_sems(n):
    return pltpu.SemaphoreType.DMA((n,))


def on_device(atmos, slot_tile, fuel_cat, front_burn, front_depth, fuel_rate, fuel_heat):
    tiles = slot_tile.reshape(NTY, NTX, SLOTS).transpose(2, 1, 0).reshape(SLOTS, DEVICES)
    tiles = jnp.pad(tiles, ((0, 8), (0, 0)), constant_values=-1)
    atmos = in_hbm(atmos)

    rows = shape(24, 8, 128)
    eight = pltpu.VMEM((3, LEV, 8, 128), F32)
    up, down = call(pack_rows, "pack_rows", (rows, rows), [HBM], [eight, eight, copy_sems(2)], mib=8)(atmos)
    low, high = both_ways(up, down, "ty")
    body = shape(2, AY, 128)
    east_rows, west_rows, surface, blocks = call(
        pack_columns, "pack_columns", (body, body, shape(3, 3, AY, 128), shape(64, 256)), [HBM], [pltpu.VMEM((3, LEV, AY, 128), F32), copy_sems(4)],
        flops=4_000_000, moved=1_800_000, mib=8,
    )(atmos)
    columns = shape(2, AY + 8, 128)
    east, west = call(join_columns, "join_columns", (columns, columns), [VMEM] * 4, mib=8)(
        east_rows, west_rows, low, high
    )
    from_west, from_east = both_ways(east, west, "tx")
    halo = (from_west, from_east, east, west, low, high)

    cells = shape(SLOTS, FC)
    wind_plan, fire_plan, fire_sends, alive, home_plan, strip_plan = call(
        plan_kernel,
        "plan",
        (
            shape(256, 256, dtype=BF16),
            shape(32, 256, dtype=BF16),
            shape(256, 128, dtype=BF16),
            shape(32, 128),
            shape(64, 256, dtype=BF16),
            shape(176, 256, dtype=BF16),
        ),
        [VMEM],
        flops=4_000_000,
        moved=400_000,
        mib=8,
    )(tiles)
    inner = call(
        surface_kernel,
        "surface",
        shape(AY, 256),
        [VMEM] * 3 + [ANY],
        [main_buffer(3), main_buffer(3)],
        flops=10_000_000,
        moved=2_000_000,
        mib=8,
    )(surface, low, high, west)
    winds = call(
        wind_kernel,
        "wind",
        shape(DEVICES * 8, 128),
        [VMEM] * 7,
        [rim_buffer(1), rim_buffer(1)],
        flops=10_000_000,
        moved=2_000_000,
        mib=8,
    )(inner, blocks, from_west, from_east, east, west, wind_plan)
    got_winds = exchange(winds)

    main, rim, *fuel = call(
        step_kernel,
        "step",
        (hbm(3, LEV, ROWS, 128), shape(3, 2, ROWS, 128)) + (cells,) * 6,
        [HBM] + [VMEM] * 8 + [HBM] * 3,
        [main_buffer(LEV), main_buffer(LEV), rim_buffer(2), rim_buffer(2)]
        + [pltpu.VMEM((3, LEV, AY, 128), F32)]
        + [pltpu.VMEM((SLOTS, FC), jnp.int32)] * 2
        + [pltpu.VMEM((SLOTS, FC), F32), copy_sems(11)],
        (HBM,) + (VMEM,) * 7,
        flops=40_000_000,
        moved=8_000_000,
        mib=12,
    )(
        atmos,
        *halo,
        fuel_rate.reshape(1, -1),
        fuel_heat.reshape(1, -1),
        in_hbm(fuel_cat),
        in_hbm(front_burn),
        in_hbm(front_depth),
    )

    heats, fire_level = call(
        fire_kernel,
        "fire",
        (hbm(DEVICES * 6, 128), hbm(SLOTS, FC)),
        [VMEM] * 10 + [HBM, ANY],
        [
            pltpu.VMEM((4 * SLOTS, FC), F32),
            pltpu.VMEM((2 * SLOTS, FC), F32),
            pltpu.VMEM((128, FC), BF16),
            pltpu.VMEM((FC, 128), BF16),
            pltpu.VMEM((DEVICES * 6, 128), F32),
            pltpu.VMEM((SLOTS, FC), F32),
            copy_sems(3),
        ],
        (HBM, HBM),
        flops=40_000_000,
        moved=4_000_000,
    )(got_winds, fire_plan, fire_sends, alive, *fuel, in_hbm(gather_table()), rim)
    got_heats = exchange(heats)

    upper, kept, bottom = call(
        upper_kernel,
        "upper",
        (hbm(3, LEV, AY, 128), shape(3, 2, ROWS, 128), shape(3, 3, ROWS, 128)),
        [HBM, VMEM, HBM],
        [main_buffer(LEV), main_buffer(LEV), rim_buffer(2), rim_buffer(2)]
        + [pltpu.VMEM((3, LEV - 3, AY, 128), F32), copy_sems(7)],
        (HBM, VMEM, VMEM),
        flops=40_000_000,
        moved=8_000_000,
        mib=12,
    )(in_hbm(main), rim, in_hbm(fire_level))
    atmos_out = call(
        lower_kernel,
        "lower",
        hbm(3, LEV, AY, 128),
        [VMEM] * 6 + [HBM],
        [
            main_buffer(3),
            main_buffer(4),
            rim_buffer(1),
            rim_buffer(1),
            rim_buffer(1),
            pltpu.VMEM((3, 3, AY, 128), F32),
            copy_sems(3),
        ],
        HBM,
        flops=10_000_000,
        moved=2_000_000,
        mib=12,
        aliases={6: 0},
    )(got_heats, home_plan, strip_plan, bottom, rim, kept, in_hbm(upper))
    return atmos_out, fire_level


def solution(mesh):
    in_specs = (
        P(None, None, "ty", "tx"),
        P(),
        P(("ty", "tx"), None),
        P(("ty", "tx"), None),
        P(("ty", "tx"), None),
        P(),
        P(),
    )
    out_specs = (P(None, None, "ty", "tx"), P(("ty", "tx"), None))
    return jax.shard_map(
        on_device, mesh=mesh, in_specs=in_specs, out_specs=out_specs, check_vma=False
    )
```

```python
import jax
import jax.numpy as jnp
import numpy as np
from jax import lax
from jax.experimental import pallas as pl
from jax.experimental.pallas import tpu as pltpu
from jax.sharding import PartitionSpec as P

AXES = ("tx", "ty")
NTY, NTX, DEVICES = 8, 16, 128
LEV, AY, AX = 16, 64, 128
SLOTS, FC = 24, 3200
ROWS = 88
TOP = 12
F32, BF16 = jnp.float32, jnp.bfloat16


def roll(x, shift, axis):
    size = x.shape[axis]
    return pltpu.roll(x, shift % size, axis) if shift % size else x


def place():
    ty, tx = lax.axis_index("ty"), lax.axis_index("tx")
    return tx * NTY + ty, ty, tx


def iota(shape, dim):
    return lax.broadcasted_iota(jnp.int32, shape, dim)


def parts(x):
    high = x.astype(BF16)
    rest = x - high.astype(F32)
    middle = rest.astype(BF16)
    low = (rest - middle.astype(F32)).astype(BF16)
    return high, middle, low


def dot(a, b):
    return jnp.dot(a, b, preferred_element_type=F32)


def pick(onehot, x):
    high, middle, _ = parts(x)
    return dot(onehot, high) + dot(onehot, middle)


def swap_blocks(x):
    x = x.reshape(x.shape[0] // 8, 8, 128)
    sub, group = iota(x.shape, 1), iota(x.shape, 2) // 16
    for step in (1, 2, 4):
        sub_bit, group_bit = (sub & step) != 0, (group & step) != 0
        below = roll(roll(x, -step, 1), 16 * step, 2)
        above = roll(roll(x, step, 1), -16 * step, 2)
        x = jnp.where(sub_bit == group_bit, x, jnp.where(group_bit, below, above))
    return x.reshape(x.shape[0] * 8, 128)


def pick_right(x, onehot, product):
    high, middle, _ = parts(x)
    both = product(jnp.concatenate([high, middle], axis=0), onehot)
    return both[0 : x.shape[0]] + both[x.shape[0] :]


def slot_facts(tile):
    row, col = tile >> 7, tile & 127
    owner = (col >> 3) * NTY + (row >> 3)
    local = (row & 7) * 8 + (col & 7)
    live = tile >= 0
    return jnp.where(live, owner, -1), local + 1, live


def earlier(member):
    lower = (iota((32, 32), 0) > iota((32, 32), 1)).astype(F32).astype(BF16)
    return dot(lower, member.astype(BF16))


def slots_of(owner, local, home):
    member = (owner == home).astype(F32)
    before = earlier(member)
    numbers = member * local.astype(F32)
    return [
        jnp.sum(jnp.where(before == float(j), numbers, 0.0), axis=0, keepdims=True)
        for j in (0, 1)
    ]


def pack_rows(atmos, up, down, low_rows, high_rows, sems):
    copies = [
        pltpu.make_async_copy(atmos.at[:, :, pl.ds(0, 8), :], low_rows, sems.at[0]),
        pltpu.make_async_copy(atmos.at[:, :, pl.ds(AY - 8, 8), :], high_rows, sems.at[1]),
    ]
    for copy in copies:
        copy.start()
    for copy in copies:
        copy.wait()
    for c in range(3):
        for level in range(LEV):
            plane = c * LEV + level
            where = pl.ds(4 * (plane % 2), 4)
            up[plane // 2, where, :] = high_rows[c, level, 4:8, :]
            down[plane // 2, where, :] = low_rows[c, level, 0:4, :]


def packed_columns(plane, half, rows, quarters=None):
    lane = iota((rows, 128), 1)
    group, spot = lane // 16, lane % 16
    both = [jnp.zeros((rows, 128), F32)] * 3
    for k in range(8):
        if quarters is not None and k % 4 == 0:
            quarters[2 * half + k // 4].wait()
        for c in range(3):
            both[c] = jnp.where(group == k, roll(plane(c, half * 8 + k), 16 * k + 4, 1), both[c])
    to_east = jnp.zeros((rows, 128), F32)
    to_west = jnp.zeros((rows, 128), F32)
    for c in range(3):
        inside = (spot >= 4 * c) & (spot < 4 * c + 4)
        to_east = jnp.where(inside, roll(both[c], 4 * c, 1), to_east)
        to_west = jnp.where(inside, roll(both[c], 4 * c - 4, 1), to_west)
    return to_east, to_west


def pack_columns(atmos, after, east, west, surface, blocks, planes, sems):
    quarters = [
        pltpu.make_async_copy(atmos.at[:, pl.ds(4 * i, 4)], planes.at[:, pl.ds(4 * i, 4)], sems.at[i])
        for i in range(4)
    ]
    for copy in quarters:
        copy.start()
    for half in range(2):
        east[half], west[half] = packed_columns(lambda c, level: planes[c, level], half, AY, quarters)
        if half == 0:
            surface[...] = planes[:, 0:3]
            blocks[...] = jnp.concatenate([swap_blocks(planes[c, 0]) for c in range(2)], axis=1)


def join_columns(east_rows, west_rows, low, high, east, west):
    def plane(c, level):
        piece = c * LEV + level
        where = slice(4 * (piece % 2), 4 * (piece % 2) + 4)
        return jnp.concatenate([low[piece // 2, where, :], high[piece // 2, where, :]], axis=0)

    for half in range(2):
        east[half, 0:AY, :] = east_rows[half]
        west[half, 0:AY, :] = west_rows[half]
        east[half, AY : AY + 8, :], west[half, AY : AY + 8, :] = packed_columns(plane, half, 8)


def rim_of(c, from_west, from_east, east, west):
    spot = iota(east.shape, 1) % 16
    out = jnp.where(spot < 4, roll(east, -4 * c, 1), roll(from_east, 4 - 4 * c, 1))
    out = jnp.where(spot < 8, out, roll(from_west, 8 - 4 * c, 1))
    return jnp.where(spot < 12, out, roll(west, 12 - 4 * c, 1))


def inside_window(first, rows, flags):
    y = iota((rows, 128), 0) + (first - TOP)
    return ((y >= 0) | (flags[1] > 0)) & ((y < AY) | (flags[1] < NTY - 1))


def rim_inside(first, rows, flags):
    spot = iota((rows, 128), 1) % 16
    east_out = (spot >= 4) & (spot < 8) & (flags[2] == NTX - 1)
    west_out = (spot >= 8) & (spot < 12) & (flags[2] == 0)
    return inside_window(first, rows, flags) & ~(east_out | west_out)


def fill_rim(rim, halves, flags, messages):
    for c in range(3):
        for half in range(halves):
            for source, first, rows in ((0, TOP, AY), (AY, 8, 4), (AY + 4, 76, 4)):
                value = rim_of(c, *(m[half, source : source + rows, :] for m in messages))
                rim[c, half, first : first + rows, :] = jnp.where(rim_inside(first, rows, flags), value, 0.0)


def fill_main(main, atmos, levels, flags, low, high):
    for c in range(3):
        for level in levels:
            piece = c * LEV + level
            where = slice(4 * (piece % 2), 4 * (piece % 2) + 4)
            main[c, level, TOP : TOP + AY, :] = atmos[c, level]
            main[c, level, 8:12, :] = jnp.where(flags[1] > 0, low[piece // 2, where, :], 0.0)
            main[c, level, 76:80, :] = jnp.where(flags[1] < NTY - 1, high[piece // 2, where, :], 0.0)


def tendency(centre, east, west, north, south, vertical):
    u, v, _ = centre
    up, vp = jnp.maximum(u, 0.0), jnp.maximum(v, 0.0)
    k_west, k_east = up + 0.25, up - u + 0.25
    k_south, k_north = vp + 0.25, vp - v + 0.25
    k_centre = k_west + k_east + k_south + k_north + 1.0
    out = []
    for c in range(3):
        out.append(
            k_west * west[c]
            + k_east * east[c]
            + k_south * south[c]
            + k_north * north[c]
            + 0.5 * vertical[c]
            - k_centre * centre[c]
        )
    out[0] = out[0] + 0.3 * v - 0.25 * (east[2] - west[2])
    out[1] = out[1] - 0.3 * u - 0.25 * (north[2] - south[2])
    return out


def edge_lanes(rim, edge, halves):
    spot = iota((72, 128), 1) % 16
    for c in range(3):
        for half in range(halves):
            x = rim[c, half, 8:80, :]
            edge[c, half, 8:80, :] = jnp.where(spot == 5, roll(x, -6, 1), x)


def main_tendency(source, edge, level, last, first, rows):
    lane = iota((rows, 128), 1)
    above, below = min(level + 1, last), max(level - 1, 0)
    here = pl.ds(first, rows)
    centre, east, west, north, south, vertical = [], [], [], [], [], []
    for c in range(3):
        x = source[c, level, here, :]
        centre.append(x)
        east.append(roll(x, -1, 1))
        west.append(roll(x, 1, 1))
        if edge is not None:
            side = roll(edge[c, level // 8, here, :], 123 - 16 * (level % 8), 1)
            east[c] = jnp.where(lane == 127, side, east[c])
            west[c] = jnp.where(lane == 0, side, west[c])
        north.append(source[c, level, pl.ds(first + 1, rows), :])
        south.append(source[c, level, pl.ds(first - 1, rows), :])
        vertical.append(source[c, above, here, :] + source[c, below, here, :])
    return centre, tendency(centre, east, west, north, south, vertical)


def rim_tendency(source, halves, half, first, rows):
    lane = iota((rows, 128), 1)
    here = pl.ds(first, rows)
    centre, east, west, north, south, vertical = [], [], [], [], [], []
    for c in range(3):
        x = source[c, half, here, :]
        next_up = source[c, 1, here, :] if half == 0 and halves == 2 else x
        next_down = source[c, 0, here, :] if half == 1 else x
        above = jnp.where(lane < 112, roll(x, -16, 1), x if next_up is x else roll(next_up, -16, 1))
        below = jnp.where(lane >= 16, roll(x, 16, 1), x if next_down is x else roll(next_down, 16, 1))
        centre.append(x)
        east.append(roll(x, -1, 1))
        west.append(roll(x, 1, 1))
        north.append(source[c, half, pl.ds(first + 1, rows), :])
        south.append(source[c, half, pl.ds(first - 1, rows), :])
        vertical.append(above + below)
    return centre, tendency(centre, east, west, north, south, vertical)


CHUNKS = ((8, 24), (32, 24), (56, 24))
ALL_ROWS = tuple(range(8, 80, 8))
BODY = tuple(range(TOP, TOP + AY, 8))


def window_masks(flags):
    return {first: inside_window(first, 8, flags) for first in (8, 72)}


def first_stage(source, target, edge, levels, last, masks):
    for level in levels:
        for first in ALL_ROWS:
            centre, change = main_tendency(source, edge, level, last, first, 8)
            for c in range(3):
                value = centre[c] + 0.2 * change[c]
                if first in masks:
                    value = jnp.where(masks[first], value, 0.0)
                target[c, level, first : first + 8, :] = value


def second_stage(source, state, edge, levels, last, rows, write):
    for level in levels:
        for first in rows:
            centre, change = main_tendency(source, edge, level, last, first, 8)
            for c in range(3):
                old = state[c, level, first : first + 8, :]
                write(c, level, first, 0.5 * (old + centre[c]) + 0.1 * change[c])


def first_rim_stage(source, target, halves, flags):
    for half in range(halves):
        for first, rows in CHUNKS:
            centre, change = rim_tendency(source, halves, half, first, rows)
            for c in range(3):
                value = centre[c] + 0.2 * change[c]
                target[c, half, pl.ds(first, rows), :] = jnp.where(rim_inside(first, rows, flags), value, 0.0)


def second_rim_stage(source, state, halves, flags):
    for half in range(halves):
        for first, rows in CHUNKS:
            centre, change = rim_tendency(source, halves, half, first, rows)
            for c in range(3):
                here = pl.ds(first, rows)
                value = 0.5 * (state[c, half, here, :] + centre[c]) + 0.1 * change[c]
                state[c, half, here, :] = jnp.where(rim_inside(first, rows, flags), value, 0.0)


def plan_kernel(tiles, wind_plan, fire_plan, fire_sends, alive, home_plan, strip_plan):
    flags = place()
    me, ty, tx = flags[0], flags[1], flags[2]
    listed = tiles[...]
    owner, local, _ = slot_facts(listed)

    def numbers(dy, dx):
        ok = (ty + dy >= 0) & (ty + dy < NTY) & (tx + dx >= 0) & (tx + dx < NTX)
        return slots_of(owner, local, jnp.where(ok, me + dx * NTY + dy, -7))

    here = numbers(0, 0)
    north, south, west, east = numbers(1, 0), numbers(-1, 0), numbers(0, -1), numbers(0, 1)
    south_west, south_east = numbers(-1, -1), numbers(-1, 1)
    north_west, north_east = numbers(1, -1), numbers(1, 1)
    tile = iota((64, 128), 0).astype(F32) + 1.0
    edge_tile = iota((8, 128), 0).astype(F32) + 1.0
    row = iota((80, 128), 0)
    first_tile = ((row // 8 - 1) * 8 + 1).astype(F32)
    body = (row >= 8) & (row < 72)

    for j in range(2):
        chosen = (here[j] == tile).astype(F32)
        chosen = jnp.concatenate([chosen, chosen], axis=0).T.astype(BF16)
        wind_plan[j * 128 : (j + 1) * 128, 0:128] = chosen
        wind_plan[j * 128 : (j + 1) * 128, 128:256] = chosen
    mine = jnp.sum(
        jnp.where(iota((32, 128), 1) == me, listed.astype(F32), 0.0), axis=1, keepdims=True
    ).astype(jnp.int32)
    holder, _, live = slot_facts(mine)
    member = (holder == iota((32, 128), 1)).astype(F32)
    before = earlier(member)
    places = [jnp.where(before == float(j), member, 0.0) for j in (0, 1)]
    fire_plan[...] = jnp.concatenate(places, axis=1).astype(BF16)
    alive[...] = jnp.where(live, jnp.ones((32, 128), F32), 0.0)

    chosen = jnp.concatenate(places + [jnp.zeros((64, 128), F32)], axis=0).T
    part = iota((128, 128), 1) // 32
    for j in range(2):
        fire_sends[j * 128 : (j + 1) * 128, :] = jnp.where(part == j, chosen, 0.0).astype(BF16)
        from_south = (south[j] == edge_tile + 56.0).astype(F32)
        from_north = (north[j] == edge_tile).astype(F32)
        from_west = body & (west[j] == first_tile + 7.0)
        from_west = from_west | ((row == 7) & (south_west[j] == 64.0)) | ((row == 72) & (north_west[j] == 8.0))
        from_east = body & (east[j] == first_tile)
        from_east = from_east | ((row == 7) & (south_east[j] == 57.0)) | ((row == 72) & (north_east[j] == 1.0))
        lanes = slice(j * 128, (j + 1) * 128)
        home_plan[:, lanes] = (here[j] == tile).astype(F32).astype(BF16)
        strips = [from_south, from_north, from_west.astype(F32), from_east.astype(F32)]
        strip_plan[:, lanes] = jnp.concatenate(strips, axis=0).astype(BF16)


def surface_kernel(planes, low, high, after, out, main, middle):
    flags = place()
    fill_main(main, planes, range(3), flags, low, high)
    first_stage(main, middle, None, range(2), 2, window_masks(flags))
    for first in BODY:
        centre, change = main_tendency(middle, None, 0, 2, first, 8)
        for c in range(2):
            value = 0.5 * (main[c, 0, first : first + 8, :] + centre[c]) + 0.1 * change[c]
            out[first - TOP : first - TOP + 8, 128 * c : 128 * c + 128] = value


def wind_kernel(inner, blocks, from_west, from_east, east, west, plan, out, rim, rim_middle):
    flags = place()
    fill_rim(rim, 1, flags, (from_west, from_east, east, west))
    first_rim_stage(rim, rim_middle, 1, flags)
    centre, change = rim_tendency(rim_middle, 1, 0, TOP, AY)
    lane = iota((AY, 128), 1)
    later = []
    for c in range(2):
        sides = 0.5 * (rim[c, 0, TOP : TOP + AY, :] + centre[c]) + 0.1 * change[c]
        field = jnp.where(lane < 2, roll(sides, -12, 1), inner[:, 128 * c : 128 * c + 128])
        later.append(jnp.where(lane >= 126, roll(sides, 124, 1), field))
    pieces = parts(jnp.concatenate([blocks[...]] + [swap_blocks(x) for x in later], axis=1))
    pieces = jnp.concatenate(pieces + (jnp.zeros((64, 512), BF16),), axis=0)
    picked = dot(plan[...], pieces)
    for j in range(2):
        for q in range(4):
            out[pl.ds(j * 4 + q, 128, stride=8), :] = picked[j * 128 : (j + 1) * 128, q * 128 : (q + 1) * 128]


def slopes(p):
    cell = iota((8, FC), 1)
    col = cell - 80 * ((cell * 52429) >> 22)
    east = jnp.where(col == 79, p, roll(p, -1, 1))
    west = jnp.where(col == 0, p, roll(p, 1, 1))
    north = jnp.where(cell >= FC - 80, p, roll(p, -80, 1))
    south = jnp.where(cell < 80, p, roll(p, 80, 1))
    gx, gy = 0.5 * (east - west), 0.5 * (north - south)
    square = 1.0 + gx * gx + gy * gy
    inverse = lax.rsqrt(square)
    return gx * inverse, gy * inverse, square * inverse


def fuel_fields(rates, heats, kinds, burns, depths, rate, heat, level, slope_x, slope_y, reach):
    for g in range(3):
        here = slice(8 * g, 8 * g + 8)
        kind = kinds[here, :]
        rate_cell = jnp.zeros(kind.shape, F32)
        heat_cell = jnp.zeros(kind.shape, F32)
        for k in range(13):
            match = kind == k
            rate_cell = jnp.where(match, rates[0:1, k : k + 1], rate_cell)
            heat_cell = jnp.where(match, heats[0:1, k : k + 1], heat_cell)
        p = jnp.where(burns[here, :] == 1, -depths[here, :], depths[here, :])
        along_x, along_y, stretch = slopes(p)
        rate[here, :] = rate_cell
        heat[here, :] = heat_cell
        level[here, :] = p
        slope_x[here, :] = along_x
        slope_y[here, :] = along_y
        reach[here, :] = rate_cell * stretch


def step_kernel(
    atmos, from_west, from_east, east, west, low, high, rates, heats, category, burn, depth,
    out, rim, rate, heat, level, slope_x, slope_y, reach,
    main, middle, rim_middle, edge, planes, kinds, burns, depths, sems,
):
    flags = place()
    groups = [pl.ds(4 * g, 4) for g in range(4)]
    loads = [pltpu.make_async_copy(atmos.at[:, x], planes.at[:, x], sems.at[g]) for g, x in enumerate(groups)]
    stores = [pltpu.make_async_copy(main.at[:, x], out.at[:, x], sems.at[4 + g]) for g, x in enumerate(groups)]
    fuel = [
        pltpu.make_async_copy(source, target, sems.at[8 + i])
        for i, (source, target) in enumerate(((category, kinds), (burn, burns), (depth, depths)))
    ]
    for load in loads + fuel:
        load.start()
    fill_rim(rim, 2, flags, (from_west, from_east, east, west))
    edge_lanes(rim, edge, 2)
    masks = window_masks(flags)
    for g in range(4):
        loads[g].wait()
        fill_main(main, planes, range(4 * g, 4 * g + 4), flags, low, high)
        first_stage(main, middle, edge, range(max(4 * g - 1, 0), 4 * g + 3 if g < 3 else LEV), LEV - 1, masks)
    first_rim_stage(rim, rim_middle, 2, flags)
    edge_lanes(rim_middle, edge, 2)

    def write(c, level, first, value):
        if first in masks:
            value = jnp.where(masks[first], value, 0.0)
        main[c, level, first : first + 8, :] = value

    for g in range(4):
        second_stage(middle, main, edge, range(4 * g, 4 * g + 4), LEV - 1, ALL_ROWS, write)
        stores[g].start()
    second_rim_stage(rim_middle, rim, 2, flags)
    for load in fuel:
        load.wait()
    fuel_fields(rates, heats, kinds, burns, depths, rate, heat, level, slope_x, slope_y, reach)
    for store in stores:
        store.wait()


def fire_kernel(
    received, plan, sends, live, rate, heat, level, slope_x, slope_y, reach, table_in, rim,
    out, out_level, wind, released, spread, gather, sent, new_level, sems,
):
    gather_copy = pltpu.make_async_copy(table_in, gather, sems.at[2])
    gather_copy.start()
    cell = iota((1, FC), 1)
    fire_row = (cell * 52429) >> 22
    fire_col = cell - 80 * fire_row
    coarse = ((fire_row * 13108) >> 16) * 16 + ((fire_col * 13108) >> 16)
    spread[...] = (iota((128, FC), 0) == coarse).astype(F32).astype(BF16)
    rows = [[received[pl.ds(j * 4 + q, 128, stride=8), :] for q in range(4)] for j in range(2)]
    table = jnp.concatenate([jnp.concatenate(r, axis=1) for r in rows], axis=0)
    winds = pick(plan[...], table)
    winds = [winds[0:SLOTS, q * 128 : (q + 1) * 128] for q in range(4)]
    wind[...] = pick_right(jnp.concatenate(winds, axis=0), spread[...], dot)

    for g in range(3):
        here = slice(8 * g, 8 * g + 8)
        alive = live[here, 0:1] > 0.0
        p = level[here, :]
        tanh_p = jnp.tanh(p)
        along_x, along_y, far = slope_x[here, :], slope_y[here, :], reach[here, :]
        for t in range(2):
            if t:
                along_x, along_y, stretch = slopes(p)
                far = rate[here, :] * stretch
            u = wind[t * 48 + 8 * g : t * 48 + 8 * g + 8, :]
            v = wind[t * 48 + 24 + 8 * g : t * 48 + 32 + 8 * g, :]
            along = u * along_x + v * along_y
            softplus = jnp.maximum(along, 0.0) + jnp.log(1.0 + jnp.exp(-jnp.abs(along)))
            p = jnp.where(alive, p - far * (1.0 + softplus), p)
            tanh_new = jnp.tanh(p)
            released[t * 24 + 8 * g : t * 24 + 8 * g + 8, :] = heat[here, :] * (tanh_p - tanh_new)
            tanh_p = tanh_new
        new_level[here, :] = p
    level_copy = pltpu.make_async_copy(new_level, out_level, sems.at[0])
    level_copy.start()
    gather_copy.wait()
    sums = 0.02 * pick_right(released[...], gather[...], dot)

    heats = jnp.concatenate([sums[0:SLOTS], sums[SLOTS:]], axis=1)
    gap = jnp.zeros((8, 256), F32)
    heats = jnp.concatenate([heats, gap, heats, gap, jnp.zeros((64, 256), F32)], axis=0)
    blocks = pick(sends[...], heats)
    lane = iota((128, 128), 1)
    group, spot = lane // 16, lane % 16
    for j in range(2):
        first = blocks[j * 128 : (j + 1) * 128, 0:128]
        sent[pl.ds(j, 128, stride=6), :] = first
        sent[pl.ds(2 + j, 128, stride=6), :] = blocks[j * 128 : (j + 1) * 128, 128:256]
        north, south = roll(first, -1, 0), roll(first, 1, 0)
        west, east = roll(first, NTY, 0), roll(first, -NTY, 0)
        corners = jnp.where((lane == 40) | (lane == 56), roll(west, 41, 1), roll(east, 57, 1))
        strip = jnp.where(group < 2, north, jnp.where(group >= 6, south, 0.0))
        middle_rows = (group >= 2) & (group < 6)
        strip = jnp.where(middle_rows & (spot >= 14), west, strip)
        strip = jnp.where(middle_rows & ((spot == 12) | (spot == 13)), roll(west, 62, 1), strip)
        strip = jnp.where(middle_rows & (spot < 2), east, strip)
        strip = jnp.where(middle_rows & ((spot == 2) | (spot == 3)), roll(east, 66, 1), strip)
        strip = jnp.where((lane == 40) | (lane == 41), roll(corners, 1, 0), strip)
        strip = jnp.where((lane == 56) | (lane == 57), roll(corners, -1, 0), strip)
        sent[pl.ds(4 + j, 128, stride=6), :] = strip
    copy = pltpu.make_async_copy(sent, out, sems.at[1])
    copy.start()
    copy.wait()
    level_copy.wait()


def heat_fields(received, home_plan, strip_plan):
    rows = [received[pl.ds(q, 128, stride=6), :] for q in range(6)]
    table = jnp.concatenate(
        [jnp.concatenate([rows[0], rows[2]], axis=1), jnp.concatenate([rows[1], rows[3]], axis=1)], axis=0
    )
    home = pick(home_plan[...], table)
    strips = pick(strip_plan[...], jnp.concatenate(rows[4:6], axis=0))
    lane8 = iota((8, 128), 1)
    blocks = jnp.concatenate(
        [
            jnp.where(lane8 >= 96, strips[0:8], 0.0),
            home[:, 0:128],
            jnp.where(lane8 < 32, strips[8:16], 0.0),
        ],
        axis=0,
    )
    first, second = swap_blocks(blocks), swap_blocks(home[:, 128:256])

    lane, row = iota((80, 128), 1), iota((80, 128), 0)
    group, spot, y = lane // 16, lane % 16, row % 8
    straight = (y >= 2) & (y < 6)
    corner = (row == 7) | (row == 72)
    wanted_group = jnp.where(y < 2, y + 4, jnp.where(y > 5, y - 4, y))
    wanted_group = jnp.where(row == 7, 2, jnp.where(row == 72, 3, wanted_group))
    fits = group == wanted_group
    west_spot = spot - jnp.where(corner, 8, jnp.where(straight, 14, 12))
    east_spot = spot - jnp.where(corner, 9, jnp.where(straight, 0, 2))
    width = jnp.where(corner, 1, 2)
    west_fits = fits & (west_spot >= 0) & (west_spot < width)
    east_fits = fits & (east_spot >= 0) & (east_spot < width)
    value = jnp.where(west_fits, strips[16:96], 0.0) + jnp.where(east_fits, strips[96:176], 0.0)
    for shift in (64, 32, 16):
        value = value + roll(value, shift, 1)
    to_west = jnp.where(corner, roll(value, 3, 1), jnp.where(straight, roll(value, -4, 1), roll(value, -2, 1)))
    to_east = jnp.where(corner, roll(value, -5, 1), jnp.where(straight, roll(value, 4, 1), roll(value, 2, 1)))
    rim = jnp.where((lane == 11) | ((lane == 10) & ~corner), to_west, 0.0)
    rim = jnp.where((lane == 4) | ((lane == 5) & ~corner), to_east, rim)
    rim = jnp.where((lane == 12) | (lane == 13), roll(first, 12, 1), rim)
    rim = jnp.where((lane == 2) | (lane == 3), roll(first, 4, 1), rim)
    return first, second, rim


def upper_kernel(main_in, rim, fire_level, out, kept, bottom, main, middle, rim_middle, edge, result, sems):
    flags = place()
    groups = [(0, 5), (5, 4), (9, 4), (13, 3)]
    loads = [
        pltpu.make_async_copy(main_in.at[:, pl.ds(*x)], main.at[:, pl.ds(*x)], sems.at[g])
        for g, x in enumerate(groups)
    ]
    for load in loads:
        load.start()
    edge_lanes(rim, edge, 2)
    masks = window_masks(flags)
    for g, (first, count) in enumerate(groups):
        loads[g].wait()
        end = first + count - 1 if g < 3 else LEV
        first_stage(main, middle, edge, range(max(first - 1, 2), end), LEV - 1, masks)
    first_rim_stage(rim, rim_middle, 2, flags)
    edge_lanes(rim_middle, edge, 2)
    bottom[...] = main[:, 0:3]
    kept[...] = middle[:, 2:4]

    def write(c, level, first, value):
        result[c, level - 3, first - TOP : first - TOP + 8, :] = value

    stores = []
    for g, (first, count) in enumerate(((3, 4), (7, 4), (11, 5))):
        second_stage(middle, main, edge, range(first, first + count), LEV - 1, BODY, write)
        part = result.at[:, pl.ds(first - 3, count)]
        stores.append(pltpu.make_async_copy(part, out.at[:, pl.ds(first, count)], sems.at[4 + g]))
        stores[g].start()
    for store in stores:
        store.wait()


def lower_kernel(
    received, home_plan, strip_plan, main_in, rim_in, kept, upper, out, main, middle, rim, rim_middle, edge,
    result, sems,
):
    flags = place()
    main[...] = main_in[...]
    rim[:, 0] = rim_in[:, 0]
    middle[:, 2:4] = kept[...]
    first, second, rim_heat = heat_fields(received, home_plan, strip_plan)
    main[2, 0, 4:84, :] = main[2, 0, 4:84, :] + first
    rim[2, 0, 4:84, :] = rim[2, 0, 4:84, :] + rim_heat
    edge_lanes(rim, edge, 1)
    first_stage(main, middle, edge, range(2), 2, window_masks(flags))
    first_rim_stage(rim, rim_middle, 1, flags)
    edge_lanes(rim_middle, edge, 1)

    def write(c, level, row, value):
        if c == 2 and level == 0:
            value = value + second[row - TOP : row - TOP + 8]
        result[c, level, row - TOP : row - TOP + 8, :] = value

    stores = []
    for level in (2, 1, 0):
        second_stage(middle, main, edge, (level,), 3, BODY, write)
        stores.append(pltpu.make_async_copy(result.at[:, level], out.at[:, level], sems.at[level]))
        stores[-1].start()
    for store in stores:
        store.wait()


SMEM = pl.BlockSpec(memory_space=pltpu.SMEM)
VMEM = pl.BlockSpec(memory_space=pltpu.VMEM)
HBM = pl.BlockSpec(memory_space=pltpu.HBM)
ANY = pl.BlockSpec(memory_space=pl.ANY)


def shape(*dims, dtype=F32):
    return jax.ShapeDtypeStruct(dims, dtype)


def hbm(*dims):
    return pltpu.HBM(dims, F32)


def in_hbm(x):
    return pltpu.with_memory_space_constraint(x, pltpu.HBM)


def call(kernel, name, out_shape, in_specs, scratch=(), out_specs=None, flops=0, moved=0, mib=16, aliases=None):
    return pl.pallas_call(
        kernel,
        out_shape=out_shape,
        in_specs=in_specs,
        out_specs=jax.tree.map(lambda _: VMEM, out_shape) if out_specs is None else out_specs,
        scratch_shapes=list(scratch),
        input_output_aliases=aliases or {},
        compiler_params=pltpu.CompilerParams(vmem_limit_bytes=mib << 20),
        cost_estimate=pl.CostEstimate(flops=flops, bytes_accessed=moved, transcendentals=0),
        name=name,
    )


def gather_table():
    cell = np.arange(FC)
    coarse = cell // 80 // 5 * 16 + cell % 80 // 5
    return jnp.asarray((coarse[:, None] == np.arange(128)[None, :]).astype(np.float32), BF16)


def both_ways(to_next, to_previous, axis):
    size = lax.axis_size(axis)
    ahead = [(i, (i + 1) % size) for i in range(size)]
    return (
        lax.ppermute(to_next, axis, ahead),
        lax.ppermute(to_previous, axis, [(j, i) for i, j in ahead]),
    )


def exchange(x):
    return lax.all_to_all(x.reshape(-1), AXES, 0, 0, tiled=True).reshape(x.shape)


def main_buffer(levels):
    return pltpu.VMEM((3, levels, ROWS, 128), F32)


def rim_buffer(halves):
    return pltpu.VMEM((3, halves, ROWS, 128), F32)


def copy_sems(n):
    return pltpu.SemaphoreType.DMA((n,))


def on_device(atmos, slot_tile, fuel_cat, front_burn, front_depth, fuel_rate, fuel_heat):
    tiles = slot_tile.reshape(NTY, NTX, SLOTS).transpose(2, 1, 0).reshape(SLOTS, DEVICES)
    tiles = jnp.pad(tiles, ((0, 8), (0, 0)), constant_values=-1)
    atmos = in_hbm(atmos)

    rows = shape(24, 8, 128)
    eight = pltpu.VMEM((3, LEV, 8, 128), F32)
    up, down = call(pack_rows, "pack_rows", (rows, rows), [HBM], [eight, eight, copy_sems(2)], mib=8)(atmos)
    low, high = both_ways(up, down, "ty")
    body = shape(2, AY, 128)
    east_rows, west_rows, surface, blocks = call(
        pack_columns, "pack_columns", (body, body, shape(3, 3, AY, 128), shape(64, 256)), [HBM, ANY], [pltpu.VMEM((3, LEV, AY, 128), F32), copy_sems(4)],
        flops=4_000_000, moved=1_800_000, mib=8,
    )(atmos, down)
    columns = shape(2, AY + 8, 128)
    east, west = call(join_columns, "join_columns", (columns, columns), [VMEM] * 4, mib=8)(
        east_rows, west_rows, low, high
    )
    from_west, from_east = both_ways(east, west, "tx")
    halo = (from_west, from_east, east, west, low, high)

    cells = shape(SLOTS, FC)
    wind_plan, fire_plan, fire_sends, alive, home_plan, strip_plan = call(
        plan_kernel,
        "plan",
        (
            shape(256, 256, dtype=BF16),
            shape(32, 256, dtype=BF16),
            shape(256, 128, dtype=BF16),
            shape(32, 128),
            shape(64, 256, dtype=BF16),
            shape(176, 256, dtype=BF16),
        ),
        [VMEM],
        flops=4_000_000,
        moved=400_000,
        mib=8,
    )(tiles)
    inner = call(
        surface_kernel,
        "surface",
        shape(AY, 256),
        [VMEM] * 3 + [ANY],
        [main_buffer(3), main_buffer(3)],
        flops=10_000_000,
        moved=2_000_000,
        mib=8,
    )(surface, low, high, west)
    winds = call(
        wind_kernel,
        "wind",
        shape(DEVICES * 8, 128),
        [VMEM] * 7,
        [rim_buffer(1), rim_buffer(1)],
        flops=10_000_000,
        moved=2_000_000,
        mib=8,
    )(inner, blocks, from_west, from_east, east, west, wind_plan)
    got_winds = exchange(winds)

    main, rim, *fuel = call(
        step_kernel,
        "step",
        (hbm(3, LEV, ROWS, 128), shape(3, 2, ROWS, 128)) + (cells,) * 6,
        [HBM] + [VMEM] * 8 + [HBM] * 3,
        [main_buffer(LEV), main_buffer(LEV), rim_buffer(2), rim_buffer(2)]
        + [pltpu.VMEM((3, LEV, AY, 128), F32)]
        + [pltpu.VMEM((SLOTS, FC), jnp.int32)] * 2
        + [pltpu.VMEM((SLOTS, FC), F32), copy_sems(11)],
        (HBM,) + (VMEM,) * 7,
        flops=40_000_000,
        moved=8_000_000,
        mib=12,
    )(
        atmos,
        *halo,
        fuel_rate.reshape(1, -1),
        fuel_heat.reshape(1, -1),
        in_hbm(fuel_cat),
        in_hbm(front_burn),
        in_hbm(front_depth),
    )

    heats, fire_level = call(
        fire_kernel,
        "fire",
        (hbm(DEVICES * 6, 128), hbm(SLOTS, FC)),
        [VMEM] * 10 + [HBM, ANY],
        [
            pltpu.VMEM((4 * SLOTS, FC), F32),
            pltpu.VMEM((2 * SLOTS, FC), F32),
            pltpu.VMEM((128, FC), BF16),
            pltpu.VMEM((FC, 128), BF16),
            pltpu.VMEM((DEVICES * 6, 128), F32),
            pltpu.VMEM((SLOTS, FC), F32),
            copy_sems(3),
        ],
        (HBM, HBM),
        flops=40_000_000,
        moved=4_000_000,
    )(got_winds, fire_plan, fire_sends, alive, *fuel, in_hbm(gather_table()), rim)
    got_heats = exchange(heats)

    upper, kept, bottom = call(
        upper_kernel,
        "upper",
        (hbm(3, LEV, AY, 128), shape(3, 2, ROWS, 128), shape(3, 3, ROWS, 128)),
        [HBM, VMEM, HBM],
        [main_buffer(LEV), main_buffer(LEV), rim_buffer(2), rim_buffer(2)]
        + [pltpu.VMEM((3, LEV - 3, AY, 128), F32), copy_sems(7)],
        (HBM, VMEM, VMEM),
        flops=40_000_000,
        moved=8_000_000,
        mib=12,
    )(in_hbm(main), rim, in_hbm(fire_level))
    atmos_out = call(
        lower_kernel,
        "lower",
        hbm(3, LEV, AY, 128),
        [VMEM] * 6 + [HBM],
        [
            main_buffer(3),
            main_buffer(4),
            rim_buffer(1),
            rim_buffer(1),
            rim_buffer(1),
            pltpu.VMEM((3, 3, AY, 128), F32),
            copy_sems(3),
        ],
        HBM,
        flops=10_000_000,
        moved=2_000_000,
        mib=12,
        aliases={6: 0},
    )(got_heats, home_plan, strip_plan, bottom, rim, kept, in_hbm(upper))
    return atmos_out, fire_level


def solution(mesh):
    in_specs = (
        P(None, None, "ty", "tx"),
        P(),
        P(("ty", "tx"), None),
        P(("ty", "tx"), None),
        P(("ty", "tx"), None),
        P(),
        P(),
    )
    out_specs = (P(None, None, "ty", "tx"), P(("ty", "tx"), None))
    return jax.shard_map(
        on_device, mesh=mesh, in_specs=in_specs, out_specs=out_specs, check_vma=False
    )
```
